32 devices in a mesh: seq: 2 (over y), chain: 16 (over z, x, core).
Axes of the slice: x: 2, y: 2, z: 4, core: 2. Of those that a mesh axis runs over, the one named last changes fastest.
Arguments:
- tokens: bfloat16 [16, 2, 512, 768], P('chain', None, 'seq'), may hold values from -6 to 6
- cotangent: bfloat16 [16, 2, 512, 768], P('chain', None, 'seq'), may hold values from -6 to 6
- chain_start: int32 [16, 2], P('chain'), may hold values from 0 to 1, as said below
- seg_len: int32 [16, 2], P('chain'), may hold values from 1 to 512, as said below
- query_weight: bfloat16 [768, 768], P(('seq', 'chain')), may hold values from -0.21875 to 0.21875
- key_weight: bfloat16 [768, 768], P(('seq', 'chain')), may hold values from -0.21875 to 0.21875
- value_weight: bfloat16 [768, 768], P(('seq', 'chain')), may hold values from -0.21875 to 0.21875
- output_weight: bfloat16 [768, 768], P(('seq', 'chain')), may hold values from -0.625 to 0.625
- query_bias: bfloat16 [768], P(('seq', 'chain')), may hold values from -1.796875 to 1.796875
- value_bias: bfloat16 [768], P(('seq', 'chain')), may hold values from -1.796875 to 1.796875
- output_bias: bfloat16 [768], P(('seq', 'chain')), may hold values from -1.796875 to 1.796875
- first_gain: bfloat16 [768], P(('seq', 'chain')), may hold values from 0.5 to 1.5
- first_shift: bfloat16 [768], P(('seq', 'chain')), may hold values from -1.796875 to 1.796875
- inner_weight: bfloat16 [768, 3072], P(('seq', 'chain')), may hold values from -0.21875 to 0.21875
- inner_bias: bfloat16 [3072], P(('seq', 'chain')), may hold values from -1.796875 to 1.796875
- outer_weight: bfloat16 [3072, 768], P(('seq', 'chain')), may hold values from -0.109375 to 0.109375
- outer_bias: bfloat16 [768], P(('seq', 'chain')), may hold values from -1.796875 to 1.796875
- second_gain: bfloat16 [768], P(('seq', 'chain')), may hold values from 0.5 to 1.5
- second_shift: bfloat16 [768], P(('seq', 'chain')), may hold values from -1.796875 to 1.796875
- read_init: bfloat16 [10, 768], P(None, ('seq', 'chain')), may hold values from -6 to 6
- write_init: bfloat16 [10, 768], P(None, ('seq', 'chain')), may hold values from -6 to 6
Outputs:
- layer_out: bfloat16 [16, 2, 512, 768], P('chain', None, 'seq')
- input_grad: bfloat16 [16, 2, 512, 768], P('chain', None, 'seq')
- query_weight_grad: float32 [768, 768], P(('seq', 'chain'))
- key_weight_grad: float32 [768, 768], P(('seq', 'chain'))
- value_weight_grad: float32 [768, 768], P(('seq', 'chain'))
- output_weight_grad: float32 [768, 768], P(('seq', 'chain'))
- query_bias_grad: float32 [768], P(('seq', 'chain'))
- value_bias_grad: float32 [768], P(('seq', 'chain'))
- output_bias_grad: float32 [768], P(('seq', 'chain'))
- first_gain_grad: float32 [768], P(('seq', 'chain'))
- first_shift_grad: float32 [768], P(('seq', 'chain'))
- inner_weight_grad: float32 [768, 3072], P(('seq', 'chain'))
- inner_bias_grad: float32 [3072], P(('seq', 'chain'))
- outer_weight_grad: float32 [3072, 768], P(('seq', 'chain'))
- outer_bias_grad: float32 [768], P(('seq', 'chain'))
- second_gain_grad: float32 [768], P(('seq', 'chain'))
- second_shift_grad: float32 [768], P(('seq', 'chain'))
- read_init_grad: float32 [10, 768], P(None, ('seq', 'chain'))
- write_init_grad: float32 [10, 768], P(None, ('seq', 'chain'))
The draws below stay inside these ranges and needn't reach their ends.
Inputs may be any that keep to these rules, and one draw needn't show every extreme that they name: `chain_start`: every group's first slot begins a chain; a chain holds one to 2 consecutive slots of one group. `seg_len`: A segment that its document continues past (the next slot has chain_start 0) is full; only a chain's last segment may be partial.
All inputs are finite; a program needn't handle non-finite values.
Results may differ from the reference program's by a relative error of at most 0.018.
Values may be sent and summed in bfloat16 or wider, within the bound.
A program may use at most 192 MiB of HBM per device.

```python
import math
import jax
import jax.numpy as jnp
from jax import lax

D = 768
HEADS = 12
HEAD_DIM = 64
FF = 3072
SEG = 512
MEM = 10
SLOTS = 2
GROUPS = 16


def chain_layout(key):
    base = jax.random.fold_in(key, 7)
    start_key = jax.random.fold_in(base, 1)
    length_key = jax.random.fold_in(base, 2)
    starts = jax.random.randint(start_key, (GROUPS, SLOTS), 0, 2)
    column = jnp.arange(SLOTS)[None, :]
    row_index = jnp.arange(GROUPS)[:, None]
    starts = jnp.where(column == 0, 1, starts)
    starts = jnp.where((row_index == 0) & (column == 1), 0, starts)
    following = jnp.concatenate([starts[:, 1:], jnp.ones((GROUPS, 1), starts.dtype)], axis=1)
    tails = jax.random.randint(length_key, (GROUPS, SLOTS), 1, SEG + 1)
    lengths = jnp.where(following == 1, tails, SEG)
    return (starts.astype(jnp.int32), lengths.astype(jnp.int32))


def draw_chain_start(key, part):
    return chain_layout(key)[0]


def draw_seg_len(key, part):
    return chain_layout(key)[1]


def level_of(rng, dims, shards, low, top_value):
    gain, own = 1.0, jax.random.fold_in(rng, 6)
    for axis_at, parts in shards:
        steps = jnp.exp(jax.random.uniform(jax.random.fold_in(own, axis_at), (parts,), jnp.float32, low / len(shards), top_value / len(shards)))
        gain = gain * jnp.repeat(steps, dims[axis_at] // parts).reshape([-1 if axis == axis_at else 1 for axis in range(len(dims))])
    return gain


def scatter_about(stream_key, dims, deviation, bound, split=(), held_as=jnp.bfloat16):
    gain = level_of(stream_key, dims, split, -0.22, 0.18) if split else 1.0
    entries = jax.random.normal(stream_key, dims, jnp.float32) * deviation * gain
    return jnp.minimum(jnp.maximum(entries, -bound), bound).astype(held_as)


def setup_inputs(seed: int = 0) -> dict:
    key_of = jax.random.split(jax.random.key(seed), 22)
    return {
        "tokens": scatter_about(key_of[0], (GROUPS, SLOTS, SEG, D), 1.0, 6.0, ((0, 16), (2, 2))),
        "cotangent": scatter_about(key_of[1], (GROUPS, SLOTS, SEG, D), 1.0, 6.0, ((0, 16), (2, 2))),
        "chain_start": draw_chain_start(jax.random.fold_in(key_of[21], 71), 0),
        "seg_len": draw_seg_len(jax.random.fold_in(key_of[21], 71), 0),
        "query_weight": scatter_about(key_of[4], (D, D), D ** -0.5, 0.21875, ((0, 32),)),
        "key_weight": scatter_about(key_of[5], (D, D), D ** -0.5, 0.21875, ((0, 32),)),
        "value_weight": scatter_about(key_of[6], (D, D), D ** -0.5, 0.21875, ((0, 32),)),
        "output_weight": scatter_about(key_of[7], (D, D), (D // 8) ** -0.5, 0.625, ((0, 32),)),
        "query_bias": scatter_about(key_of[8], (D,), 0.3, 1.796875, ((0, 32),)),
        "value_bias": scatter_about(key_of[9], (D,), 0.3, 1.796875, ((0, 32),)),
        "output_bias": scatter_about(key_of[10], (D,), 0.3, 1.796875, ((0, 32),)),
        "first_gain": jnp.clip(1.0 + 0.1 * jax.random.normal(key_of[11], (D,), jnp.float32), 0.5, 1.5).astype(jnp.bfloat16),
        "first_shift": scatter_about(key_of[12], (D,), 0.3, 1.796875, ((0, 32),)),
        "inner_weight": scatter_about(key_of[13], (D, FF), D ** -0.5, 0.21875, ((0, 32),)),
        "inner_bias": scatter_about(key_of[14], (FF,), 0.3, 1.796875, ((0, 32),)),
        "outer_weight": scatter_about(key_of[15], (FF, D), FF ** -0.5, 0.109375, ((0, 32),)),
        "outer_bias": scatter_about(key_of[16], (D,), 0.3, 1.796875, ((0, 32),)),
        "second_gain": jnp.clip(1.0 + 0.1 * jax.random.normal(key_of[17], (D,), jnp.float32), 0.5, 1.5).astype(jnp.bfloat16),
        "second_shift": scatter_about(key_of[18], (D,), 0.3, 1.796875, ((0, 32),)),
        "read_init": scatter_about(key_of[19], (MEM, D), 1.0, 6.0, ((1, 32),)),
        "write_init": scatter_about(key_of[20], (MEM, D), 1.0, 6.0, ((1, 32),)),
    }


@jax.custom_vjp
def low(v):
    return lax.optimization_barrier(v.astype(jnp.bfloat16)).astype(jnp.float32)

@jax.custom_vjp
def low_back(v):
    return v

def low_keep(v):
    return (low(v), None)

def low_pass(kept, grad):
    return (grad,)

def back_keep(v):
    return (v, None)

def back_low(kept, grad):
    return (low(grad),)
low.defvjp(low_keep, low_pass)
low_back.defvjp(back_keep, back_low)

def matmul(former, latter):
    return jnp.dot(former, latter, precision=lax.Precision.HIGHEST, preferred_element_type=jnp.float32)

def layer_norm(summed, gain_vec, shift_vec):
    row_mean = lax.optimization_barrier(jnp.mean(summed, axis=-1, keepdims=True))
    centred = summed - row_mean
    variance = lax.optimization_barrier(jnp.mean(centred * centred, axis=-1, keepdims=True))
    return centred * lax.rsqrt(variance + 1e-12) * gain_vec + shift_vec

def block_layer(params, hidden, key_valid):
    query_weight, key_weight, value_weight, output_weight, query_bias, value_bias, output_bias, first_gain, first_shift, inner_weight, inner_bias, outer_weight, outer_bias, second_gain, second_shift, read_init, write_init = params
    row_count = hidden.shape[0]
    score_scale = 1.0 / math.sqrt(HEAD_DIM)
    hidden_b = low(hidden)
    query_val = low(low_back(matmul(hidden_b, query_weight) + query_bias))
    key_val = low(low_back(matmul(hidden_b, key_weight)))
    value_val = low(low_back(matmul(hidden_b, value_weight) + value_bias))
    query_heads = query_val.reshape(row_count, HEADS, HEAD_DIM)
    key_heads = key_val.reshape(row_count, HEADS, HEAD_DIM)
    value_heads = value_val.reshape(row_count, HEADS, HEAD_DIM)
    scores = low_back(jnp.einsum('qhd,khd->hqk', query_heads, key_heads, precision=lax.Precision.HIGHEST) * score_scale)
    scores = jnp.where(key_valid[None, None, :], scores, -1000000000.0)
    probs = jax.nn.softmax(scores, axis=-1)
    mixed_out = jnp.einsum('hqk,khd->qhd', low(probs), value_heads, precision=lax.Precision.HIGHEST)
    mixed_out = low(low_back(mixed_out.reshape(row_count, HEADS * HEAD_DIM)))
    branch = low_back(matmul(mixed_out, output_weight) + output_bias)
    first = layer_norm(hidden + branch, first_gain, first_shift)
    inner_pre = low_back(matmul(low(first), inner_weight) + inner_bias)
    active = low(jax.nn.gelu(inner_pre, approximate=False))
    outer = low_back(matmul(active, outer_weight) + outer_bias)
    return layer_norm(first + outer, second_gain, second_shift)

def group_pass(params, group_tokens, starts, lengths):
    read_init = params[15]
    write_init = params[16]
    carried = jnp.zeros((MEM, D), read_init.dtype)
    memory_valid = jnp.ones((2 * MEM,), dtype=bool)
    outputs = []
    for slot_index in range(SLOTS):
        read_rows = jnp.where(starts[slot_index] == 1, read_init, low(carried))
        hidden = jnp.concatenate([read_rows, write_init, group_tokens[slot_index]], axis=0)
        token_valid = jnp.arange(SEG) < lengths[slot_index]
        key_valid = jnp.concatenate([memory_valid, token_valid], axis=0)
        second = block_layer(params, hidden, key_valid)
        outputs.append(second[2 * MEM:])
        carried = second[MEM:2 * MEM]
    return jnp.stack(outputs, axis=0)

def reference(tokens, cotangent, chain_start, seg_len, query_weight, key_weight, value_weight, output_weight, query_bias, value_bias, output_bias, first_gain, first_shift, inner_weight, inner_bias, outer_weight, outer_bias, second_gain, second_shift, read_init, write_init):
    params = tuple((w.astype(jnp.float32) for w in (query_weight, key_weight, value_weight, output_weight, query_bias, value_bias, output_bias, first_gain, first_shift, inner_weight, inner_bias, outer_weight, outer_bias, second_gain, second_shift, read_init, write_init)))

    def one_group(grad_list, packed):
        group_tokens, group_cotangent, starts, lengths = packed

        def forward(prm, rows_in):
            return group_pass(prm, rows_in, starts, lengths)
        outputs, pullback = jax.vjp(forward, params, group_tokens.astype(jnp.float32))
        param_grads, token_grads = pullback(group_cotangent.astype(jnp.float32))
        grad_list = tuple((acc + new for acc, new in zip(grad_list, param_grads)))
        return (grad_list, (outputs.astype(jnp.bfloat16), token_grads.astype(jnp.bfloat16)))
    zero_grads = tuple((jnp.zeros_like(w) for w in params))
    grads, (layer_out, input_grad) = lax.scan(one_group, zero_grads, (tokens, cotangent, chain_start, seg_len))
    return (layer_out, input_grad, grads[0], grads[1], grads[2], grads[3], grads[4], grads[5], grads[6], grads[7], grads[8], grads[9], grads[10], grads[11], grads[12], grads[13], grads[14], grads[15], grads[16])
```

```python
import functools
import math

import jax
import jax.numpy as jnp
from jax import lax
from jax.experimental import pallas as pl
from jax.experimental.pallas import tpu as pltpu
from jax.sharding import PartitionSpec as P

HEADS = 12
MEM = 10
EPS = 1e-12
INV_ROOT_TWO = 1.0 / math.sqrt(2.0)
INV_ROOT_TWO_PI = 1.0 / math.sqrt(2.0 * math.pi)
NEG_FILL = -1000000000.0

MESH = pl.DeviceIdType.MESH


def place():
    seq = lax.axis_index("seq")
    chain = lax.axis_index("chain")
    return seq, chain // 4, lax.rem(chain // 2, 2), lax.rem(chain, 2)


def block_of(levels, seq, level, side, core):
    return seq * (4 * levels) + level * 4 + side * 2 + core


def device_of(seq, level, side, core):
    return (seq, level * 4 + side * 2 + core)


def greet(levels):
    seq, level, side, core = place()
    barrier = pltpu.get_barrier_semaphore()

    def tell(*target):
        pl.semaphore_signal(barrier, inc=1, device_id=device_of(*target), device_id_type=MESH)

    tell(seq, level, side, 1 - core)
    tell(seq, level, 1 - side, core)
    tell(1 - seq, level, side, core)

    @pl.when(level > 0)
    def _():
        tell(seq, level - 1, side, core)

    @pl.when(level < levels - 1)
    def _():
        tell(seq, level + 1, side, core)

    pl.semaphore_wait(
        barrier,
        3 + (level > 0).astype(jnp.int32) + (level < levels - 1).astype(jnp.int32),
    )


def gather_kernel(levels, parts, late, *refs):
    count = len(parts)
    arrays = 1 + max(p[0] for p in parts)
    shard_refs, whole_refs = refs[:arrays], refs[arrays : 2 * arrays]
    recv_sems, send_sems, own_sems = refs[2 * arrays :]
    seq, level, side, core = place()
    greet(levels)
    targets = {
        0: (seq, level, side, 1 - core),
        1: (seq, level, 1 - side, core),
        2: (1 - seq, level, side, core),
        3: (seq, level + 1, side, core),
        4: (seq, level - 1, side, core),
    }

    def block(step_seq, at, step_side, of_core):
        return block_of(
            levels, seq if step_seq == 0 else 1 - seq, at, side if step_side == 0 else 1 - side, of_core
        )

    def shard_view(part):
        array, row, rows, column, columns = parts[part]
        return shard_refs[array].at[pl.ds(row, rows), pl.ds(column, columns)]

    def whole_view(part, index):
        array, row, rows, column, columns = parts[part]
        return whole_refs[array].at[index, pl.ds(row, rows), pl.ds(column, columns)]

    def copy(part, index, kind, own=False):
        source = shard_view(part) if own else whole_view(part, index)
        return pltpu.make_async_remote_copy(
            src_ref=source,
            dst_ref=whole_view(part, index),
            send_sem=send_sems.at[part, index, kind],
            recv_sem=recv_sems.at[part, index],
            device_id=device_of(*targets[kind]),
            device_id_type=MESH,
        )

    def arrived(part, index):
        copy(part, index, 0).wait_recv()

    def over_column(part, index, own=False, plane=True):
        if plane:
            copy(part, index, 1, own).start()
            copy(part, index, 2, own).start()
        copy(part, index, 0, own).start()

    mine = block(0, level, 0, core)

    def up(part, index, own=False):
        @pl.when(level < levels - 1)
        def _():
            copy(part, index, 3, own).start()

    def down(part, index, own=False):
        @pl.when(level > 0)
        def _():
            copy(part, index, 4, own).start()

    def route(part):
        return part % 2

    for part in range(count):
        up(part, mine, True)
        down(part, mine, True)
        over_column(part, mine, True)
        pltpu.make_async_copy(shard_view(part), whole_view(part, mine), own_sems.at[part]).start()

    def from_plane(part, at):
        beside = block(0, at, 1, core)
        arrived(part, beside)
        if route(part) == 0:
            copy(part, beside, 2).start()
        copy(part, beside, 0).start()
        across = block(1, at, 0, core)
        arrived(part, across)
        if route(part) == 1:
            copy(part, across, 1).start()
        copy(part, across, 0).start()

    def from_corner(part, at):
        corner = block(1, at, 1, core)
        arrived(part, corner)
        copy(part, corner, 0).start()

    def guarded(at, body):
        pl.when(jnp.logical_and(at >= 0, at < levels))(body)

    for step in range(levels + 2):
        for part in range(count):
            if part in late:
                continue
            if 1 <= step < levels:
                for sign in (-1, 1):
                    at = level + sign * step

                    def column(part=part, at=at, sign=sign):
                        index = block(0, at, 0, core)
                        arrived(part, index)
                        (up if sign < 0 else down)(part, index)
                        over_column(part, index)

                    guarded(at, column)
            if 1 <= step < levels + 1:
                near = step - 1
                for sign in (-1, 1) if near else (1,):
                    at = level + sign * near
                    guarded(at, functools.partial(from_plane, part, at))
            if step >= 2:
                near = step - 2
                for sign in (-1, 1) if near else (1,):
                    at = level + sign * near
                    guarded(at, functools.partial(from_corner, part, at))
        if step == 1:
            for part in late:
                from_plane(part, level)
                for index in (block(0, level, 1, core), block(1, level, 0, core)):
                    up(part, index)
                    down(part, index)
        if step == 2:
            for part in late:
                from_corner(part, level)
                up(part, block(1, level, 1, core))
                down(part, block(1, level, 1, core))
        if step >= 2 and step - 1 < levels:
            far = step - 1
            for part in late:
                for sign in (-1, 1):
                    at = level + sign * far

                    def four(part=part, at=at, sign=sign):
                        for place_at in ((0, 0), (0, 1), (1, 0), (1, 1)):
                            index = block(place_at[0], at, place_at[1], core)
                            arrived(part, index)
                            (up if sign < 0 else down)(part, index)
                            copy(part, index, 0).start()

                    guarded(at, four)

    for part in range(count):
        def other(at, carry, part=part):
            for place_at in ((0, 0), (0, 1), (1, 0), (1, 1)):
                arrived(part, block(place_at[0], at, place_at[1], 1 - core))
            return carry

        lax.fori_loop(0, levels, other, 0)

    for part in range(count):
        pltpu.make_async_copy(shard_view(part), whole_view(part, mine), own_sems.at[part]).wait()

        def left(at, carry, part=part):
            for place_at in ((0, 0), (0, 1), (1, 0), (1, 1)):
                index = block(place_at[0], at, place_at[1], core)
                copy(part, index, 0).wait_send()
                in_plane = part in late
                if part in late:
                    here = at == level
                else:
                    here = True
                if place_at == (0, 0):
                    def sides():
                        copy(part, index, 1).wait_send()
                        copy(part, index, 2).wait_send()
                    if here is True: sides()
                    else: pl.when(here)(sides)
                if place_at == (0, 1) and route(part) == 0:
                    fn = lambda: copy(part, index, 2).wait_send()
                    if here is True: fn()
                    else: pl.when(here)(fn)
                if place_at == (1, 0) and route(part) == 1:
                    fn = lambda: copy(part, index, 1).wait_send()
                    if here is True: fn()
                    else: pl.when(here)(fn)
                if place_at == (0, 0) or part in late:
                    @pl.when(jnp.logical_and(at <= level, level < levels - 1))
                    def _():
                        copy(part, index, 3).wait_send()

                    @pl.when(jnp.logical_and(at >= level, level > 0))
                    def _():
                        copy(part, index, 4).wait_send()
            return carry

        lax.fori_loop(0, levels, left, 0)


def gather_all(levels, shards, parts, late):
    count, arrays = len(parts), len(shards)
    total = 8 * levels
    anywhere = pl.BlockSpec(memory_space=pl.ANY)
    return pl.pallas_call(
        functools.partial(gather_kernel, levels, parts, late),
        out_shape=[jax.ShapeDtypeStruct((total,) + s.shape, s.dtype) for s in shards],
        in_specs=[anywhere] * arrays,
        out_specs=[anywhere] * arrays,
        scratch_shapes=[
            pltpu.SemaphoreType.DMA((count, total)),
            pltpu.SemaphoreType.DMA((count, total, 5)),
            pltpu.SemaphoreType.DMA((count,)),
        ],
        compiler_params=pltpu.CompilerParams(collective_id=0, has_side_effects=True),
        name="gather_weights",
    )(*shards)


def scatter_kernel(levels, parts, *refs):
    count = len(parts)
    arrays = 1 + max(p[0] for p in parts)
    part_refs, out_refs = refs[:arrays], refs[arrays : 2 * arrays]
    at_ref = 2 * arrays
    core_refs, side_refs, seq_refs, below_refs, above_refs = (
        refs[at_ref + i * count : at_ref + (i + 1) * count] for i in range(5)
    )
    core_send, core_recv, side_send, side_recv, seq_send, seq_recv, up_send, up_recv, down_send, down_recv = refs[
        at_ref + 5 * count :
    ]
    seq, level, side, core = place()
    greet(levels)

    def block(rel, at, of_core):
        return block_of(
            levels, seq if rel < 2 else 1 - seq, at, side if rel % 2 == 0 else 1 - side, of_core
        )

    def view(part, index):
        array, row, rows, column, columns = parts[part]
        return part_refs[array].at[index, pl.ds(row, rows), pl.ds(column, columns)]

    def remote(source, target, send_sem, recv_sem, device):
        return pltpu.make_async_remote_copy(
            src_ref=source, dst_ref=target, send_sem=send_sem, recv_sem=recv_sem,
            device_id=device_of(*device), device_id_type=MESH,
        )

    def over_core(part, at, rel):
        slot = at * 4 + rel
        return remote(
            view(part, block(rel, at, 1 - core)), core_refs[part].at[slot],
            core_send.at[part, slot], core_recv.at[part, slot], (seq, level, side, 1 - core),
        )

    def over_side(part, at, rel, routed):
        slot = at * 2 + routed
        return remote(
            core_refs[part].at[at * 4 + rel], side_refs[part].at[slot],
            side_send.at[part, slot], side_recv.at[part, slot], (seq, level, 1 - side, core),
        )

    def over_seq(part, at, rel, routed):
        slot = at * 2 + routed
        return remote(
            core_refs[part].at[at * 4 + rel], seq_refs[part].at[slot],
            seq_send.at[part, slot], seq_recv.at[part, slot], (1 - seq, level, side, core),
        )

    def over_up(part, at):
        return remote(
            core_refs[part].at[at * 4], below_refs[part].at[at],
            up_send.at[part, at], up_recv.at[part, at], (seq, level + 1, side, core),
        )

    def over_down(part, at):
        return remote(
            core_refs[part].at[at * 4], above_refs[part].at[at],
            down_send.at[part, at], down_recv.at[part, at], (seq, level - 1, side, core),
        )

    def route(part):
        return part % 2

    def loop(body):
        def step(at, carry):
            body(at)
            return carry
        lax.fori_loop(0, levels, step, 0)

    def total(part, at, rel, *more):
        value = view(part, block(rel, at, core))[...].astype(jnp.float32)
        value = value + core_refs[part][at * 4 + rel].astype(jnp.float32)
        for ref in more:
            value = value + ref[...].astype(jnp.float32)
        return value

    def keep(part, at, rel, value):
        core_refs[part][at * 4 + rel] = value.astype(jnp.bfloat16)

    def start_core(part):
        for rel in (3, 1, 2, 0):
            loop(lambda at: over_core(part, at, rel).start())

    def stage_corner(part):
        def body(at):
            over_core(part, at, 3).wait_recv()
            keep(part, at, 3, total(part, at, 3))
            (over_side if route(part) == 0 else over_seq)(part, at, 3, 1).start()
        loop(body)

    def stage_plane(part):
        def body(at):
            over_core(part, at, 1).wait_recv()
            over_core(part, at, 2).wait_recv()
            if route(part) == 1:
                keep_first, first, keep_second = 2, 2, 1
                keep(part, at, 2, total(part, at, 2))
                over_seq(part, at, 2, 0).start()
                over_seq(part, at, 3, 1).wait_recv()
                keep(part, at, 1, total(part, at, 1, seq_refs[part].at[at * 2 + 1]))
                over_side(part, at, 1, 0).start()
            else:
                keep(part, at, 1, total(part, at, 1))
                over_side(part, at, 1, 0).start()
                over_side(part, at, 3, 1).wait_recv()
                keep(part, at, 2, total(part, at, 2, side_refs[part].at[at * 2 + 1]))
                over_seq(part, at, 2, 0).start()
        loop(body)

    def ready(part, at):
        over_core(part, at, 0).wait_recv()
        over_side(part, at, 1, 0).wait_recv()
        over_seq(part, at, 2, 0).wait_recv()

    def column_total(part, at, *more):
        return total(part, at, 0, side_refs[part].at[at * 2], seq_refs[part].at[at * 2], *more)

    def stage_line(part):
        def body(turn, carry):
            high = levels - 1 - turn

            @pl.when(level < high)
            def _():
                ready(part, high)

                @pl.when(level == 0)
                def _():
                    keep(part, high, 0, column_total(part, high))

                @pl.when(level > 0)
                def _():
                    over_up(part, high).wait_recv()
                    keep(part, high, 0, column_total(part, high, below_refs[part].at[high]))

                over_up(part, high).start()

            @pl.when(level > turn)
            def _():
                ready(part, turn)

                @pl.when(level == levels - 1)
                def _():
                    keep(part, turn, 0, column_total(part, turn))

                @pl.when(level < levels - 1)
                def _():
                    over_down(part, turn).wait_recv()
                    keep(part, turn, 0, column_total(part, turn, above_refs[part].at[turn]))

                over_down(part, turn).start()

            return carry

        lax.fori_loop(0, levels - 1, body, 0)

    def stage_last(part):
        array, row, rows, column, columns = parts[part]
        out = out_refs[array].at[pl.ds(row, rows), pl.ds(column, columns)]
        ready(part, level)
        out[...] = column_total(part, level)

        @pl.when(level > 0)
        def _():
            over_up(part, level).wait_recv()
            out[...] += below_refs[part][level].astype(jnp.float32)

        @pl.when(level < levels - 1)
        def _():
            over_down(part, level).wait_recv()
            out[...] += above_refs[part][level].astype(jnp.float32)

    stages = (start_core, stage_corner, stage_plane, stage_line, stage_last)
    for turn in range(count + len(stages) - 1):
        for depth in range(len(stages)):
            if 0 <= turn - depth < count:
                stages[depth](turn - depth)

    for part in range(count):
        def left(at, part=part):
            for rel in range(4):
                over_core(part, at, rel).wait_send()
            over_side(part, at, 1, 0).wait_send()
            over_seq(part, at, 2, 0).wait_send()
            (over_side if route(part) == 0 else over_seq)(part, at, 3, 1).wait_send()

            @pl.when(at > level)
            def _():
                over_up(part, at).wait_send()

            @pl.when(at < level)
            def _():
                over_down(part, at).wait_send()
        loop(left)


def scatter_all(levels, grads, parts):
    count, arrays = len(parts), len(grads)
    sizes = [(p[2], p[4]) for p in parts]
    inside = pl.BlockSpec(memory_space=pltpu.VMEM)
    scratch = []
    for blocks in (4 * levels, 2 * levels, 2 * levels, levels, levels):
        scratch += [pltpu.VMEM((blocks,) + size, jnp.bfloat16) for size in sizes]
    for blocks in (4 * levels, 2 * levels, 2 * levels, levels, levels):
        scratch += [pltpu.SemaphoreType.DMA((count, blocks))] * 2
    return pl.pallas_call(
        functools.partial(scatter_kernel, levels, parts),
        out_shape=[jax.ShapeDtypeStruct(g.shape[1:], jnp.float32) for g in grads],
        in_specs=[inside] * arrays,
        out_specs=[inside] * arrays,
        scratch_shapes=scratch,
        compiler_params=pltpu.CompilerParams(
            collective_id=1, has_side_effects=True, vmem_limit_bytes=60 * 2**20
        ),
        name="scatter_grads",
    )(*grads)


def fori(count, body):
    def step(index, carry):
        body(index)
        return carry

    lax.fori_loop(0, count, step, 0)


def span(index, size):
    return pl.ds(pl.multiple_of(index * size, size), size)


def dot_nn(former, latter):
    return jnp.dot(former, latter, preferred_element_type=jnp.float32)


def dot_nt(former, latter):
    return lax.dot_general(former, latter, (((1,), (1,)), ((), ())), preferred_element_type=jnp.float32)


def dot_tn(former, latter):
    return lax.dot_general(former, latter, (((0,), (0,)), ((), ())), preferred_element_type=jnp.float32)


def fold(rows):
    return jnp.sum(rows.reshape(rows.shape[0] // 8, 8, rows.shape[1]), axis=0)


TILE = 256
CHUNK = 48
MEMORY = 32
LANES = 128


def middle_kernel(
    start_ref,
    mask_ref,
    token_ref,
    other_ref,
    cot_ref,
    vec_ref,
    inner_bias_ref,
    query_hbm,
    key_hbm,
    value_hbm,
    output_hbm,
    inner_hbm,
    outer_hbm,
    layer_ref,
    own_ref,
    pair_ref,
    small_ref,
    inner_bias_grad_ref,
    query_grad_hbm,
    key_grad_hbm,
    value_grad_hbm,
    output_grad_hbm,
    inner_grad_hbm,
    outer_grad_hbm,
    wq,
    wk,
    wv,
    wo,
    wi,
    w2,
    hid,
    query,
    key,
    value,
    probs,
    mixed,
    normed_one,
    normed_two,
    inverse_one,
    inverse_two,
    first_b,
    slope,
    active,
    grad_two_b,
    grad_one_b,
    grad_mixed,
    grad_query,
    grad_key,
    grad_value,
    work,
    memory,
    send_rows,
    recv_rows,
    stage,
    load_sems,
    stage_sems,
    pair_sems,
):
    slots, half, width = token_ref.shape
    rows = half + MEMORY
    keys = rows + half
    hidden_width = wi.shape[1]
    pairs = width // LANES
    scale = 1.0 / math.sqrt(width // HEADS)
    seq = lax.axis_index("seq")
    chain = lax.axis_index("chain")
    is_owner = seq == 0
    barrier = pltpu.get_barrier_semaphore()
    pl.semaphore_signal(barrier, inc=1, device_id=(1 - seq, chain), device_id_type=MESH)
    loads = [
        pltpu.make_async_copy(source, target, load_sems.at[i])
        for i, (source, target) in enumerate(
            (
                (query_hbm, wq),
                (key_hbm, wk),
                (value_hbm, wv),
                (output_hbm, wo),
                (inner_hbm, wi),
                (outer_hbm, w2),
            )
        )
    ]
    for load in loads:
        load.start()
    line = 2 * MEM

    def vec(at):
        return vec_ref[line + at : line + at + 1, :]

    def vec_tile(at, index):
        return vec_ref[line + at : line + at + 1, span(index, TILE)]

    lane = lax.broadcasted_iota(jnp.int32, (1, LANES), 1)
    low_half = lane < LANES // 2
    mem_row = lax.broadcasted_iota(jnp.int32, (MEMORY, 1), 0)
    tiles = width // TILE

    def half_of(values, which, factor):
        keep = low_half if which == 0 else jnp.logical_not(low_half)
        return values * jnp.where(keep, factor, 0.0).astype(values.dtype)

    def forward(slot):
        query_rows = pl.ds(half, rows)
        hid[slot, 0:half] = other_ref[slot]
        hid[slot, half : 2 * half] = token_ref[slot]
        initial = jnp.where(mem_row < line, vec_ref[0:MEMORY, :], 0.0)
        if slot > 0:
            second = work[half:rows].astype(jnp.bfloat16).astype(jnp.float32)
            carried = pltpu.roll(second, MEMORY - MEM, 0)
        else:
            carried = jnp.zeros_like(initial)
        restart = start_ref[slot] == 1
        initial = jnp.where(jnp.logical_or(mem_row >= MEM, restart), initial, carried)
        hid[slot, 2 * half : keys] = initial.astype(jnp.bfloat16)
        if slot == 0:
            loads[0].wait()

        def query_tile(j):
            query[slot, :, span(j, TILE)] = (
                dot_nn(hid[slot, query_rows], wq[:, span(j, TILE)]) + vec_tile(0, j)
            ).astype(jnp.bfloat16)

        fori(tiles, query_tile)
        if slot == 0:
            loads[1].wait()

        def key_tile(j):
            key[slot, :, span(j, TILE)] = dot_nn(hid[slot], wk[:, span(j, TILE)]).astype(jnp.bfloat16)

        fori(tiles, key_tile)
        if slot == 0:
            loads[2].wait()

        def value_tile(j):
            value[slot, :, span(j, TILE)] = (dot_nn(hid[slot], wv[:, span(j, TILE)]) + vec_tile(1, j)).astype(
                jnp.bfloat16
            )

        fori(tiles, value_tile)
        valid = mask_ref[slot]

        def attend(p):
            here = span(p, LANES)
            query_pair = query[slot, :, here]
            key_pair = key[slot, :, here]
            value_pair = value[slot, :, here]
            sides = []
            for which in range(2):
                scores = dot_nt(half_of(query_pair, which, scale), key_pair) + valid
                top = jnp.max(scores, axis=1, keepdims=True)
                raised = jnp.exp(scores - top)
                total = jnp.sum(raised, axis=1, keepdims=True)
                share = (raised * (1.0 / total)).astype(jnp.bfloat16)
                probs[slot, 2 * p + which] = share
                sides.append(dot_nn(share, value_pair))
            mixed[slot, :, here] = jnp.where(low_half, sides[0], sides[1]).astype(jnp.bfloat16)

        fori(pairs, attend)
        if slot == 0:
            loads[3].wait()

        def branch_tile(j):
            here = span(j, TILE)
            work[:, here] = (
                dot_nn(mixed[slot], wo[:, here]) + vec_tile(2, j) + hid[slot, query_rows, here].astype(jnp.float32)
            )

        fori(tiles, branch_tile)

        def norm_chunk(normed, inverse, gain_at, shift_at):
            def body(r):
                here = span(r, CHUNK)
                z = work[here, :]
                centred = z - jnp.mean(z, axis=1, keepdims=True)
                inv = lax.rsqrt(jnp.mean(centred * centred, axis=1, keepdims=True) + EPS)
                unit = centred * inv
                normed[slot, here] = unit.astype(jnp.bfloat16)
                inverse[slot, here] = inv
                out = unit * vec(gain_at) + vec(shift_at)
                work[here, :] = out
                if normed is normed_one:
                    first_b[slot, here] = out.astype(jnp.bfloat16)

            return body

        fori(rows // CHUNK, norm_chunk(normed_one, inverse_one, 3, 4))
        if slot == 0:
            loads[4].wait()

        def inner_tile(j):
            here = span(j, TILE)
            u = dot_nn(first_b[slot], wi[:, here]) + inner_bias_ref[:, here]
            cumulative = 0.5 * (1.0 + lax.erf(u * INV_ROOT_TWO))
            density = jnp.exp(-0.5 * u * u) * INV_ROOT_TWO_PI
            active[slot, :, here] = (u * cumulative).astype(jnp.bfloat16)
            slope[slot, :, here] = (cumulative + u * density).astype(jnp.bfloat16)

        fori(hidden_width // TILE, inner_tile)
        if slot == 0:
            loads[5].wait()

        def outer_tile(j):
            here = span(j, TILE)
            work[:, here] += dot_nn(active[slot], w2[:, here]) + vec_tile(5, j)

        fori(tiles, outer_tile)
        fori(rows // CHUNK, norm_chunk(normed_two, inverse_two, 6, 7))
        layer_ref[slot] = work[0:half].astype(jnp.bfloat16)

    def add_small(at, folded):
        small_ref[line + at : line + at + 1, :] += jnp.sum(folded, axis=0, keepdims=True)

    def backward(slot):
        work[0:half] = cot_ref[slot].astype(jnp.float32)
        work[half:rows] = memory[...]

        def norm_back_pass(normed, inverse, gain_at, shift_at, bias_at, rounded):
            zero = jnp.zeros((8, width), jnp.float32)

            def body(r, sums):
                here = span(r, CHUNK)
                grad = work[here, :]
                unit = normed[slot, here].astype(jnp.float32)
                gain_sum = sums[0] + fold(grad * unit)
                shift_sum = sums[1] + fold(grad)
                scaled = grad * vec(gain_at)
                dz = inverse[slot, here] * (
                    scaled
                    - jnp.mean(scaled, axis=1, keepdims=True)
                    - unit * jnp.mean(scaled * unit, axis=1, keepdims=True)
                )
                work[here, :] = dz
                dz_b = dz.astype(jnp.bfloat16)
                rounded[slot, here] = dz_b
                return (gain_sum, shift_sum, sums[2] + fold(dz_b.astype(jnp.float32)))

            sums = lax.fori_loop(0, rows // CHUNK, body, (zero, zero, zero))
            add_small(gain_at, sums[0])
            add_small(shift_at, sums[1])
            add_small(bias_at, sums[2])

        norm_back_pass(normed_two, inverse_two, 6, 7, 5, grad_two_b)

        def inner_tile(j):
            here = span(j, TILE)
            grad = (dot_nt(grad_two_b[slot], w2[here, :]) * slope[slot, :, here].astype(jnp.float32)).astype(
                jnp.bfloat16
            )
            slope[slot, :, here] = grad
            inner_bias_grad_ref[:, here] += jnp.sum(grad.astype(jnp.float32), axis=0, keepdims=True)

        fori(hidden_width // TILE, inner_tile)

        def first_tile(j):
            here = span(j, TILE)
            work[:, here] += dot_nt(slope[slot], wi[here, :])

        fori(tiles, first_tile)
        norm_back_pass(normed_one, inverse_one, 3, 4, 2, grad_one_b)

        def mixed_tile(j):
            here = span(j, TILE)
            grad_mixed[:, here] = dot_nt(grad_one_b[slot], wo[here, :]).astype(jnp.bfloat16)

        fori(tiles, mixed_tile)

        def attend(p):
            here = span(p, LANES)
            query_pair = query[slot, :, here]
            key_pair = key[slot, :, here]
            value_pair = value[slot, :, here]
            mixed_pair = grad_mixed[:, here]
            dq, dk, dv = [], [], []
            for which in range(2):
                share = probs[slot, 2 * p + which]
                grad = dot_nt(half_of(mixed_pair, which, 1.0), value_pair)
                soft = share.astype(jnp.float32)
                delta = jnp.sum(grad * soft, axis=1, keepdims=True)
                grad_b = (soft * (grad - delta)).astype(jnp.bfloat16)
                dq.append(dot_nn(grad_b, key_pair))
                dk.append(dot_tn(grad_b, query_pair))
                dv.append(dot_tn(share, mixed_pair))
            dq_b = (jnp.where(low_half, dq[0], dq[1]) * scale).astype(jnp.bfloat16)
            dv_b = jnp.where(low_half, dv[0], dv[1]).astype(jnp.bfloat16)
            grad_query[slot, :, here] = dq_b
            grad_key[slot, :, here] = (jnp.where(low_half, dk[0], dk[1]) * scale).astype(jnp.bfloat16)
            grad_value[slot, :, here] = dv_b
            small_ref[line : line + 1, here] += jnp.sum(dq_b.astype(jnp.float32), axis=0, keepdims=True)
            small_ref[line + 1 : line + 2, here] += jnp.sum(dv_b.astype(jnp.float32), axis=0, keepdims=True)

        fori(pairs, attend)

        def input_tile(j):
            here = span(j, TILE)
            both = dot_nt(grad_key[slot], wk[here, :]) + dot_nt(grad_value[slot], wv[here, :])
            pair_ref[slot, :, here] = both[0:half].astype(jnp.bfloat16)
            mine = both[half:keys] + dot_nt(grad_query[slot], wq[here, :]) + work[:, here]
            own_ref[slot, :, here] = mine[0:half]
            memory[:, here] = mine[half:rows]

        fori(tiles, input_tile)
        restart = start_ref[slot] == 1
        grads = memory[...]
        counted = jnp.logical_or(
            jnp.logical_and(mem_row < MEM, restart), jnp.logical_and(mem_row >= MEM, mem_row < line)
        )
        small_ref[0:MEMORY, :] += jnp.where(counted, grads, 0.0)
        if slot > 0:
            passed = jnp.where(jnp.logical_and(mem_row < MEM, jnp.logical_not(restart)), grads, 0.0)
            send_rows[...] = passed
            pl.semaphore_wait(barrier, 1)
            swap = pltpu.make_async_remote_copy(
                src_ref=send_rows,
                dst_ref=recv_rows,
                send_sem=pair_sems.at[0],
                recv_sem=pair_sems.at[1],
                device_id=(1 - seq, chain),
                device_id_type=MESH,
            )
            swap.start()
            swap.wait()
            summed = pltpu.roll(passed + recv_rows[...], MEM, 0)
            memory[...] = jnp.where(is_owner, summed, 0.0)

    small_ref[...] = jnp.zeros_like(small_ref)
    inner_bias_grad_ref[...] = jnp.zeros_like(inner_bias_grad_ref)
    for slot in range(slots):
        forward(slot)
    memory[...] = jnp.zeros_like(memory)
    for slot in reversed(range(slots)):
        backward(slot)

    def emit(count, compute, target):
        def copy(j):
            buffer = lax.rem(j, 2)
            return pltpu.make_async_copy(stage.at[buffer], target(j), stage_sems.at[buffer])

        def body(j):
            @pl.when(j >= 2)
            def _():
                copy(j - 2).wait()

            stage[lax.rem(j, 2)] = compute(j).astype(jnp.bfloat16)
            copy(j).start()

        fori(count, body)
        copy(count - 2).wait()
        copy(count - 1).wait()

    def product(former, latter):
        total = None
        for slot in range(slots):
            term = dot_tn(former(slot), latter(slot))
            total = term if total is None else total + term
        return total

    emit(
        tiles,
        lambda j: product(lambda s: hid[s, half:keys, span(j, TILE)], lambda s: grad_query[s]),
        lambda j: query_grad_hbm.at[span(j, TILE)],
    )
    emit(
        tiles,
        lambda j: product(lambda s: hid[s, :, span(j, TILE)], lambda s: grad_key[s]),
        lambda j: key_grad_hbm.at[span(j, TILE)],
    )
    emit(
        tiles,
        lambda j: product(lambda s: hid[s, :, span(j, TILE)], lambda s: grad_value[s]),
        lambda j: value_grad_hbm.at[span(j, TILE)],
    )
    emit(
        tiles,
        lambda j: product(lambda s: mixed[s, :, span(j, TILE)], lambda s: grad_one_b[s]),
        lambda j: output_grad_hbm.at[span(j, TILE)],
    )
    emit(
        hidden_width // TILE,
        lambda j: product(
            lambda s: first_b[s, :, span(lax.rem(j, tiles), TILE)], lambda s: slope[s, :, span(j // tiles, width)]
        ),
        lambda j: inner_grad_hbm.at[span(lax.rem(j, tiles), TILE), span(j // tiles, width)],
    )
    emit(
        hidden_width // TILE,
        lambda j: product(lambda s: active[s, :, span(j, TILE)], lambda s: grad_two_b[s]),
        lambda j: outer_grad_hbm.at[span(j, TILE)],
    )


def middle(start, mask, tokens, others, cotangent, vectors, inner_bias, weights):
    slots, half, width = tokens.shape
    rows, keys = half + MEMORY, 2 * half + MEMORY
    hidden_width = inner_bias.shape[1]
    bf16, f32 = jnp.bfloat16, jnp.float32
    inside = pl.BlockSpec(memory_space=pltpu.VMEM)
    anywhere = pl.BlockSpec(memory_space=pl.ANY)
    shape = jax.ShapeDtypeStruct
    dma = pltpu.SemaphoreType.DMA
    return pl.pallas_call(
        middle_kernel,
        out_shape=[
            shape((slots, half, width), bf16),
            shape((slots, half, width), f32),
            shape((slots, half, width), bf16),
            shape((MEMORY, width), f32),
            shape((1, hidden_width), f32),
        ]
        + [shape(w.shape, bf16) for w in weights],
        in_specs=[pl.BlockSpec(memory_space=pltpu.SMEM)] + [inside] * 6 + [anywhere] * 6,
        out_specs=[inside] * 5 + [anywhere] * 6,
        scratch_shapes=[pltpu.VMEM(w.shape, bf16) for w in weights]
        + [
            pltpu.VMEM((slots, keys, width), bf16),
            pltpu.VMEM((slots, rows, width), bf16),
            pltpu.VMEM((slots, keys, width), bf16),
            pltpu.VMEM((slots, keys, width), bf16),
            pltpu.VMEM((slots, HEADS, rows, keys), bf16),
            pltpu.VMEM((slots, rows, width), bf16),
            pltpu.VMEM((slots, rows, width), bf16),
            pltpu.VMEM((slots, rows, width), bf16),
            pltpu.VMEM((slots, rows, 1), f32),
            pltpu.VMEM((slots, rows, 1), f32),
            pltpu.VMEM((slots, rows, width), bf16),
            pltpu.VMEM((slots, rows, hidden_width), bf16),
            pltpu.VMEM((slots, rows, hidden_width), bf16),
            pltpu.VMEM((slots, rows, width), bf16),
            pltpu.VMEM((slots, rows, width), bf16),
            pltpu.VMEM((rows, width), bf16),
            pltpu.VMEM((slots, rows, width), bf16),
            pltpu.VMEM((slots, keys, width), bf16),
            pltpu.VMEM((slots, keys, width), bf16),
            pltpu.VMEM((rows, width), f32),
            pltpu.VMEM((MEMORY, width), f32),
            pltpu.VMEM((MEMORY, width), f32),
            pltpu.VMEM((MEMORY, width), f32),
            pltpu.VMEM((2, TILE, width), bf16),
            dma((6,)),
            dma((2,)),
            dma((2,)),
        ],
        compiler_params=pltpu.CompilerParams(
            collective_id=2, has_side_effects=True, vmem_limit_bytes=62 * 2**20
        ),
        cost_estimate=pl.CostEstimate(flops=31 * 10**9, bytes_accessed=40 * 10**6, transcendentals=10**7),
        name="layer",
    )(start, mask, tokens, others, cotangent, vectors, inner_bias, *weights)


def small_block(vectors, inner_bias, read_init, write_init):
    width = vectors[0].shape[0]
    inner_width = inner_bias.shape[0]
    rows = jnp.concatenate([read_init, write_init] + [v[None] for v in vectors], axis=0)
    rows = jnp.pad(rows, ((0, 4), (0, 128 - width)))
    return rows + jnp.pad(inner_bias[None], ((28, 3), (0, 128 - inner_width)))


def shards(
    tokens,
    cotangent,
    chain_start,
    seg_len,
    query_weight,
    key_weight,
    value_weight,
    output_weight,
    query_bias,
    value_bias,
    output_bias,
    first_gain,
    first_shift,
    inner_weight,
    inner_bias,
    outer_weight,
    outer_bias,
    second_gain,
    second_shift,
    read_init,
    write_init,
):
    slot_count = tokens.shape[1]
    half_rows = tokens.shape[2]
    model_width = tokens.shape[3]
    blocks = lax.axis_size("seq") * lax.axis_size("chain")
    levels = lax.axis_size("chain") // 4
    width = model_width // blocks
    inner_columns = inner_weight.shape[1]
    inner_width = inner_bias.shape[0]
    kernels = width % 8 == 0
    small = small_block(
        (query_bias, value_bias, output_bias, first_gain, first_shift, outer_bias, second_gain, second_shift),
        inner_bias,
        read_init,
        write_init,
    )
    shard_list = [query_weight, key_weight, value_weight, output_weight, inner_weight, outer_weight, small]
    parts = [(i, 0, width, 0, model_width) for i in range(4)]
    parts += [(4, 0, width, 0, inner_columns // 2), (4, 0, width, inner_columns // 2, inner_columns // 2)]
    parts += [(5, 0, inner_width // 2, 0, model_width), (5, inner_width // 2, inner_width // 2, 0, model_width)]
    parts += [(6, 0, 32, 0, 128)]
    pair = [(0, 1), (1, 0)]
    others = lax.ppermute(tokens[0], "seq", pair)
    if kernels:
        whole = gather_all(levels, shard_list, parts, (7,))
    else:
        whole = [lax.all_gather(w, ("seq", "chain"), axis=0) for w in shard_list]
    whole_query, whole_key, whole_value, whole_output, whole_inner, whole_outer = (
        w.reshape(-1, w.shape[-1]) for w in whole[:6]
    )
    small_all = whole[6]
    vectors = small_all[:, :, :width].transpose(1, 0, 2).reshape(32, model_width).astype(jnp.float32)
    bias_inner = small_all[:, 28, :inner_width].reshape(1, -1).astype(jnp.float32)
    my_index = lax.axis_index("seq")
    place_in = jnp.arange(half_rows)
    position = jnp.concatenate(
        [
            (1 - my_index) * half_rows + place_in,
            my_index * half_rows + place_in,
            jnp.where(jnp.arange(MEMORY) < 2 * MEM, -1, 1 << 30),
        ]
    )
    mask = jnp.where(position[None, :] < seg_len[0][:, None], 0.0, NEG_FILL)[:, None, :]
    results = middle(
        chain_start[0],
        mask,
        tokens[0],
        others,
        cotangent[0],
        vectors,
        bias_inner,
        (whole_query, whole_key, whole_value, whole_output, whole_inner, whole_outer),
    )
    layer_out = results[0][None]
    received = lax.ppermute(results[2], "seq", pair)
    input_grad = (results[1] + received.astype(jnp.float32)).astype(jnp.bfloat16)[None]
    small_grads = jnp.pad(
        results[3].reshape(32, blocks, width).transpose(1, 0, 2), ((0, 0), (0, 0), (0, 128 - width))
    )
    inner_rows = jnp.pad(results[4].reshape(blocks, 1, inner_width), ((0, 0), (28, 3), (0, 128 - inner_width)))
    small_grads = jnp.where(jnp.arange(32)[None, :, None] == 28, inner_rows, small_grads).astype(jnp.bfloat16)
    weight_grads = [g.reshape((blocks,) + s.shape) for g, s in zip(results[5:], shard_list)]
    partial_grads = weight_grads + [small_grads]
    if kernels:
        sums = scatter_all(levels, partial_grads, parts)
    else:
        sums = [
            lax.psum_scatter(
                lax.psum_scatter(
                    g.reshape((-1,) + g.shape[2:]), "seq", scatter_dimension=0, tiled=True
                ).astype(jnp.float32),
                "chain", scatter_dimension=0, tiled=True,
            )
            for g in partial_grads
        ]
    small_sum = sums[6].reshape(32, 128)
    vector = [small_sum[20 + i, :width] for i in range(8)]
    return (
        layer_out,
        input_grad,
        sums[0],
        sums[1],
        sums[2],
        sums[3],
        vector[0],
        vector[1],
        vector[2],
        vector[3],
        vector[4],
        sums[4],
        small_sum[28, :inner_width],
        sums[5],
        vector[5],
        vector[6],
        vector[7],
        small_sum[:MEM, :width],
        small_sum[MEM : 2 * MEM, :width],
    )


def solution(mesh):
    placed = (
        P("chain", None, "seq", None),
        P("chain", None, "seq", None),
        P("chain", None),
        P("chain", None),
        P(("seq", "chain"), None),
        P(("seq", "chain"), None),
        P(("seq", "chain"), None),
        P(("seq", "chain"), None),
        P(("seq", "chain")),
        P(("seq", "chain")),
        P(("seq", "chain")),
        P(("seq", "chain")),
        P(("seq", "chain")),
        P(("seq", "chain"), None),
        P(("seq", "chain")),
        P(("seq", "chain"), None),
        P(("seq", "chain")),
        P(("seq", "chain")),
        P(("seq", "chain")),
        P(None, ("seq", "chain")),
        P(None, ("seq", "chain")),
    )
    return jax.shard_map(
        shards,
        mesh=mesh,
        in_specs=placed,
        out_specs=(
            P("chain", None, "seq", None),
            P("chain", None, "seq", None),
            P(("seq", "chain"), None),
            P(("seq", "chain"), None),
            P(("seq", "chain"), None),
            P(("seq", "chain"), None),
            P(("seq", "chain")),
            P(("seq", "chain")),
            P(("seq", "chain")),
            P(("seq", "chain")),
            P(("seq", "chain")),
            P(("seq", "chain"), None),
            P(("seq", "chain")),
            P(("seq", "chain"), None),
            P(("seq", "chain")),
            P(("seq", "chain")),
            P(("seq", "chain")),
            P(None, ("seq", "chain")),
            P(None, ("seq", "chain")),
        ),
        check_vma=False,
    )
```

```python
import functools
import math

import jax
import jax.numpy as jnp
from jax import lax
from jax.experimental import pallas as pl
from jax.experimental.pallas import tpu as pltpu
from jax.sharding import PartitionSpec as P

HEADS = 12
MEM = 10
EPS = 1e-12
INV_ROOT_TWO = 1.0 / math.sqrt(2.0)
INV_ROOT_TWO_PI = 1.0 / math.sqrt(2.0 * math.pi)
NEG_FILL = -1000000000.0

MESH = pl.DeviceIdType.MESH


def place():
    seq = lax.axis_index("seq")
    chain = lax.axis_index("chain")
    return seq, chain // 4, lax.rem(chain // 2, 2), lax.rem(chain, 2)


def block_of(levels, seq, level, side, core):
    return seq * (4 * levels) + level * 4 + side * 2 + core


def device_of(seq, level, side, core):
    return (seq, level * 4 + side * 2 + core)


def greet(levels):
    seq, level, side, core = place()
    barrier = pltpu.get_barrier_semaphore()

    def tell(*target):
        pl.semaphore_signal(barrier, inc=1, device_id=device_of(*target), device_id_type=MESH)

    tell(seq, level, side, 1 - core)
    tell(seq, level, 1 - side, core)
    tell(1 - seq, level, side, core)

    @pl.when(level > 0)
    def _():
        tell(seq, level - 1, side, core)

    @pl.when(level < levels - 1)
    def _():
        tell(seq, level + 1, side, core)

    pl.semaphore_wait(
        barrier,
        3 + (level > 0).astype(jnp.int32) + (level < levels - 1).astype(jnp.int32),
    )


def gather_kernel(levels, parts, late, *refs):
    count = len(parts)
    arrays = 1 + max(p[0] for p in parts)
    shard_refs, whole_refs = refs[:arrays], refs[arrays : 2 * arrays]
    recv_sems, send_sems, own_sems = refs[2 * arrays :]
    seq, level, side, core = place()
    greet(levels)
    targets = {
        0: (seq, level, side, 1 - core),
        1: (seq, level, 1 - side, core),
        2: (1 - seq, level, side, core),
        3: (seq, level + 1, side, core),
        4: (seq, level - 1, side, core),
    }

    def block(step_seq, at, step_side, of_core):
        return block_of(
            levels, seq if step_seq == 0 else 1 - seq, at, side if step_side == 0 else 1 - side, of_core
        )

    def shard_view(part):
        array, row, rows, column, columns = parts[part]
        return shard_refs[array].at[pl.ds(row, rows), pl.ds(column, columns)]

    def whole_view(part, index):
        array, row, rows, column, columns = parts[part]
        return whole_refs[array].at[index, pl.ds(row, rows), pl.ds(column, columns)]

    def copy(part, index, kind, own=False):
        source = shard_view(part) if own else whole_view(part, index)
        return pltpu.make_async_remote_copy(
            src_ref=source,
            dst_ref=whole_view(part, index),
            send_sem=send_sems.at[part, index, kind],
            recv_sem=recv_sems.at[part, index],
            device_id=device_of(*targets[kind]),
            device_id_type=MESH,
        )

    def arrived(part, index):
        copy(part, index, 0).wait_recv()

    def over_column(part, index, own=False, plane=True):
        if plane:
            copy(part, index, 1, own).start()
            copy(part, index, 2, own).start()
        copy(part, index, 0, own).start()

    mine = block(0, level, 0, core)

    def up(part, index, own=False):
        @pl.when(level < levels - 1)
        def _():
            copy(part, index, 3, own).start()

    def down(part, index, own=False):
        @pl.when(level > 0)
        def _():
            copy(part, index, 4, own).start()

    def route(part):
        return part % 2

    for part in range(count):
        up(part, mine, True)
        down(part, mine, True)
        over_column(part, mine, True)
        pltpu.make_async_copy(shard_view(part), whole_view(part, mine), own_sems.at[part]).start()

    def from_plane(part, at):
        beside = block(0, at, 1, core)
        arrived(part, beside)
        if route(part) == 0:
            copy(part, beside, 2).start()
        copy(part, beside, 0).start()
        across = block(1, at, 0, core)
        arrived(part, across)
        if route(part) == 1:
            copy(part, across, 1).start()
        copy(part, across, 0).start()

    def from_corner(part, at):
        corner = block(1, at, 1, core)
        arrived(part, corner)
        copy(part, corner, 0).start()

    def guarded(at, body):
        pl.when(jnp.logical_and(at >= 0, at < levels))(body)

    for step in range(levels + 2):
        for part in range(count):
            if part in late:
                continue
            if 1 <= step < levels:
                for sign in (-1, 1):
                    at = level + sign * step

                    def column(part=part, at=at, sign=sign):
                        index = block(0, at, 0, core)
                        arrived(part, index)
                        (up if sign < 0 else down)(part, index)
                        over_column(part, index)

                    guarded(at, column)
            if 1 <= step < levels + 1:
                near = step - 1
                for sign in (-1, 1) if near else (1,):
                    at = level + sign * near
                    guarded(at, functools.partial(from_plane, part, at))
            if step >= 2:
                near = step - 2
                for sign in (-1, 1) if near else (1,):
                    at = level + sign * near
                    guarded(at, functools.partial(from_corner, part, at))
        if step == 1:
            for part in late:
                from_plane(part, level)
                for index in (block(0, level, 1, core), block(1, level, 0, core)):
                    up(part, index)
                    down(part, index)
        if step == 2:
            for part in late:
                from_corner(part, level)
                up(part, block(1, level, 1, core))
                down(part, block(1, level, 1, core))
        if step >= 2 and step - 1 < levels:
            far = step - 1
            for part in late:
                for sign in (-1, 1):
                    at = level + sign * far

                    def four(part=part, at=at, sign=sign):
                        for place_at in ((0, 0), (0, 1), (1, 0), (1, 1)):
                            index = block(place_at[0], at, place_at[1], core)
                            arrived(part, index)
                            (up if sign < 0 else down)(part, index)
                            copy(part, index, 0).start()

                    guarded(at, four)

    for part in range(count):
        def other(at, carry, part=part):
            for place_at in ((0, 0), (0, 1), (1, 0), (1, 1)):
                arrived(part, block(place_at[0], at, place_at[1], 1 - core))
            return carry

        lax.fori_loop(0, levels, other, 0)

    for part in range(count):
        pltpu.make_async_copy(shard_view(part), whole_view(part, mine), own_sems.at[part]).wait()

        def left(at, carry, part=part):
            for place_at in ((0, 0), (0, 1), (1, 0), (1, 1)):
                index = block(place_at[0], at, place_at[1], core)
                copy(part, index, 0).wait_send()
                in_plane = part in late
                if part in late:
                    here = at == level
                else:
                    here = True
                if place_at == (0, 0):
                    def sides():
                        copy(part, index, 1).wait_send()
                        copy(part, index, 2).wait_send()
                    if here is True: sides()
                    else: pl.when(here)(sides)
                if place_at == (0, 1) and route(part) == 0:
                    fn = lambda: copy(part, index, 2).wait_send()
                    if here is True: fn()
                    else: pl.when(here)(fn)
                if place_at == (1, 0) and route(part) == 1:
                    fn = lambda: copy(part, index, 1).wait_send()
                    if here is True: fn()
                    else: pl.when(here)(fn)
                if place_at == (0, 0) or part in late:
                    @pl.when(jnp.logical_and(at <= level, level < levels - 1))
                    def _():
                        copy(part, index, 3).wait_send()

                    @pl.when(jnp.logical_and(at >= level, level > 0))
                    def _():
                        copy(part, index, 4).wait_send()
            return carry

        lax.fori_loop(0, levels, left, 0)


def gather_all(levels, shards, parts, late):
    count, arrays = len(parts), len(shards)
    total = 8 * levels
    anywhere = pl.BlockSpec(memory_space=pl.ANY)
    return pl.pallas_call(
        functools.partial(gather_kernel, levels, parts, late),
        out_shape=[jax.ShapeDtypeStruct((total,) + s.shape, s.dtype) for s in shards],
        in_specs=[anywhere] * arrays,
        out_specs=[anywhere] * arrays,
        scratch_shapes=[
            pltpu.SemaphoreType.DMA((count, total)),
            pltpu.SemaphoreType.DMA((count, total, 5)),
            pltpu.SemaphoreType.DMA((count,)),
        ],
        compiler_params=pltpu.CompilerParams(collective_id=0, has_side_effects=True),
        name="gather_weights",
    )(*shards)


def scatter_kernel(levels, parts, *refs):
    count = len(parts)
    arrays = 1 + max(p[0] for p in parts)
    part_refs, out_refs = refs[:arrays], refs[arrays : 2 * arrays]
    at_ref = 2 * arrays
    core_refs, side_refs, seq_refs, below_refs, above_refs = (
        refs[at_ref + i * count : at_ref + (i + 1) * count] for i in range(5)
    )
    core_send, core_recv, side_send, side_recv, seq_send, seq_recv, up_send, up_recv, down_send, down_recv = refs[
        at_ref + 5 * count :
    ]
    seq, level, side, core = place()
    greet(levels)

    def block(rel, at, of_core):
        return block_of(
            levels, seq if rel < 2 else 1 - seq, at, side if rel % 2 == 0 else 1 - side, of_core
        )

    def view(part, index):
        array, row, rows, column, columns = parts[part]
        return part_refs[array].at[index, pl.ds(row, rows), pl.ds(column, columns)]

    def remote(source, target, send_sem, recv_sem, device):
        return pltpu.make_async_remote_copy(
            src_ref=source, dst_ref=target, send_sem=send_sem, recv_sem=recv_sem,
            device_id=device_of(*device), device_id_type=MESH,
        )

    def over_core(part, at, rel):
        slot = at * 4 + rel
        return remote(
            view(part, block(rel, at, 1 - core)), core_refs[part].at[slot],
            core_send.at[part, slot], core_recv.at[part, slot], (seq, level, side, 1 - core),
        )

    def over_side(part, at, rel, routed):
        slot = at * 2 + routed
        return remote(
            core_refs[part].at[at * 4 + rel], side_refs[part].at[slot],
            side_send.at[part, slot], side_recv.at[part, slot], (seq, level, 1 - side, core),
        )

    def over_seq(part, at, rel, routed):
        slot = at * 2 + routed
        return remote(
            core_refs[part].at[at * 4 + rel], seq_refs[part].at[slot],
            seq_send.at[part, slot], seq_recv.at[part, slot], (1 - seq, level, side, core),
        )

    def over_up(part, at):
        return remote(
            core_refs[part].at[at * 4], below_refs[part].at[at],
            up_send.at[part, at], up_recv.at[part, at], (seq, level + 1, side, core),
        )

    def over_down(part, at):
        return remote(
            core_refs[part].at[at * 4], above_refs[part].at[at],
            down_send.at[part, at], down_recv.at[part, at], (seq, level - 1, side, core),
        )

    def route(part):
        return part % 2

    def loop(body):
        def step(at, carry):
            body(at)
            return carry
        lax.fori_loop(0, levels, step, 0)

    def total(part, at, rel, *more):
        value = view(part, block(rel, at, core))[...].astype(jnp.float32)
        value = value + core_refs[part][at * 4 + rel].astype(jnp.float32)
        for ref in more:
            value = value + ref[...].astype(jnp.float32)
        return value

    def keep(part, at, rel, value):
        core_refs[part][at * 4 + rel] = value.astype(jnp.bfloat16)

    def start_core(part):
        for rel in (3, 1, 2, 0):
            loop(lambda at: over_core(part, at, rel).start())

    def stage_corner(part):
        def body(at):
            over_core(part, at, 3).wait_recv()
            keep(part, at, 3, total(part, at, 3))
            (over_side if route(part) == 0 else over_seq)(part, at, 3, 1).start()
        loop(body)

    def stage_plane(part):
        def body(at):
            over_core(part, at, 1).wait_recv()
            over_core(part, at, 2).wait_recv()
            if route(part) == 1:
                keep_first, first, keep_second = 2, 2, 1
                keep(part, at, 2, total(part, at, 2))
                over_seq(part, at, 2, 0).start()
                over_seq(part, at, 3, 1).wait_recv()
                keep(part, at, 1, total(part, at, 1, seq_refs[part].at[at * 2 + 1]))
                over_side(part, at, 1, 0).start()
            else:
                keep(part, at, 1, total(part, at, 1))
                over_side(part, at, 1, 0).start()
                over_side(part, at, 3, 1).wait_recv()
                keep(part, at, 2, total(part, at, 2, side_refs[part].at[at * 2 + 1]))
                over_seq(part, at, 2, 0).start()
        loop(body)

    def ready(part, at):
        over_core(part, at, 0).wait_recv()
        over_side(part, at, 1, 0).wait_recv()
        over_seq(part, at, 2, 0).wait_recv()

    def column_total(part, at, *more):
        return total(part, at, 0, side_refs[part].at[at * 2], seq_refs[part].at[at * 2], *more)

    def stage_line(part):
        def body(turn, carry):
            high = levels - 1 - turn

            @pl.when(level < high)
            def _():
                ready(part, high)

                @pl.when(level == 0)
                def _():
                    keep(part, high, 0, column_total(part, high))

                @pl.when(level > 0)
                def _():
                    over_up(part, high).wait_recv()
                    keep(part, high, 0, column_total(part, high, below_refs[part].at[high]))

                over_up(part, high).start()

            @pl.when(level > turn)
            def _():
                ready(part, turn)

                @pl.when(level == levels - 1)
                def _():
                    keep(part, turn, 0, column_total(part, turn))

                @pl.when(level < levels - 1)
                def _():
                    over_down(part, turn).wait_recv()
                    keep(part, turn, 0, column_total(part, turn, above_refs[part].at[turn]))

                over_down(part, turn).start()

            return carry

        lax.fori_loop(0, levels - 1, body, 0)

    def stage_last(part):
        array, row, rows, column, columns = parts[part]
        out = out_refs[array].at[pl.ds(row, rows), pl.ds(column, columns)]
        ready(part, level)
        out[...] = column_total(part, level)

        @pl.when(level > 0)
        def _():
            over_up(part, level).wait_recv()
            out[...] += below_refs[part][level].astype(jnp.float32)

        @pl.when(level < levels - 1)
        def _():
            over_down(part, level).wait_recv()
            out[...] += above_refs[part][level].astype(jnp.float32)

    stages = (start_core, stage_corner, stage_plane, stage_line, stage_last)
    for turn in range(count + len(stages) - 1):
        for depth in range(len(stages)):
            if 0 <= turn - depth < count:
                stages[depth](turn - depth)

    for part in range(count):
        def left(at, part=part):
            for rel in range(4):
                over_core(part, at, rel).wait_send()
            over_side(part, at, 1, 0).wait_send()
            over_seq(part, at, 2, 0).wait_send()
            (over_side if route(part) == 0 else over_seq)(part, at, 3, 1).wait_send()

            @pl.when(at > level)
            def _():
                over_up(part, at).wait_send()

            @pl.when(at < level)
            def _():
                over_down(part, at).wait_send()
        loop(left)


def scatter_all(levels, grads, parts):
    count, arrays = len(parts), len(grads)
    sizes = [(p[2], p[4]) for p in parts]
    inside = pl.BlockSpec(memory_space=pltpu.VMEM)
    scratch = []
    for blocks in (4 * levels, 2 * levels, 2 * levels, levels, levels):
        scratch += [pltpu.VMEM((blocks,) + size, jnp.bfloat16) for size in sizes]
    for blocks in (4 * levels, 2 * levels, 2 * levels, levels, levels):
        scratch += [pltpu.SemaphoreType.DMA((count, blocks))] * 2
    return pl.pallas_call(
        functools.partial(scatter_kernel, levels, parts),
        out_shape=[jax.ShapeDtypeStruct(g.shape[1:], jnp.float32) for g in grads],
        in_specs=[inside] * arrays,
        out_specs=[inside] * arrays,
        scratch_shapes=scratch,
        compiler_params=pltpu.CompilerParams(
            collective_id=1, has_side_effects=True, vmem_limit_bytes=60 * 2**20
        ),
        name="scatter_grads",
    )(*grads)


def fori(count, body):
    def step(index, carry):
        body(index)
        return carry

    lax.fori_loop(0, count, step, 0)


def span(index, size):
    return pl.ds(pl.multiple_of(index * size, size), size)


def dot_nn(former, latter):
    return jnp.dot(former, latter, preferred_element_type=jnp.float32)


def dot_nt(former, latter):
    return lax.dot_general(former, latter, (((1,), (1,)), ((), ())), preferred_element_type=jnp.float32)


def dot_tn(former, latter):
    return lax.dot_general(former, latter, (((0,), (0,)), ((), ())), preferred_element_type=jnp.float32)


def fold(rows):
    return jnp.sum(rows.reshape(rows.shape[0] // 8, 8, rows.shape[1]), axis=0)


CHUNK = 48
MEMORY = 32
LANES = 128
LINE = 2 * MEM


class Layer:
    def __init__(self, seq, refs):
        self.seq = seq
        self.__dict__.update(refs)
        self.slots, self.half, self.width = self.cot.shape
        self.rows = self.half + MEMORY
        self.keys = self.rows + self.half
        self.hidden = self.w_inner.shape[1]
        self.pairs = self.width // LANES
        self.scale = 1.0 / math.sqrt(self.width // HEADS)
        lane = lax.broadcasted_iota(jnp.int32, (1, LANES), 1)
        self.low = lane < LANES // 2
        self.low_f = jnp.where(self.low, 1.0, 0.0)
        self.low_b = self.low_f.astype(jnp.bfloat16)
        self.high_f = 1.0 - self.low_f
        self.high_b = self.high_f.astype(jnp.bfloat16)
        self.mem_row = lax.broadcasted_iota(jnp.int32, (MEMORY, 1), 0)

    def vec(self, at):
        return self.vectors[LINE + at : LINE + at + 1, :]

    def slot_rows(self, slot):
        return pl.ds(slot * self.rows, self.rows)

    def slot_keys(self, slot):
        return pl.ds(slot * self.keys, self.keys)

    def slot_queries(self, slot):
        return pl.ds(slot * self.keys + self.half, self.rows)

    def weight(self, at):
        return self.w_attention.at[:, pl.ds(at * self.width, self.width)]

    def set_memory(self, slot):
        initial = jnp.where(self.mem_row < LINE, self.vectors[0:MEMORY, :], 0.0)
        if slot > 0:
            second = self.work[self.half : self.rows].astype(jnp.bfloat16).astype(jnp.float32)
            carried = pltpu.roll(second, MEMORY - MEM, 0)
        else:
            carried = jnp.zeros_like(initial)
        restart = self.start[slot] == 1
        initial = jnp.where(jnp.logical_or(self.mem_row >= MEM, restart), initial, carried)
        base = slot * self.keys + 2 * self.half
        self.hid[base : base + MEMORY] = initial.astype(jnp.bfloat16)

    def project_query(self, slot):
        out = dot_nn(self.hid[self.slot_queries(slot)], self.weight(0)[...]) + self.vec(0)
        self.query[self.slot_rows(slot)] = out.astype(jnp.bfloat16)

    def project_key(self, slot):
        self.key[self.slot_keys(slot)] = dot_nn(self.hid[self.slot_keys(slot)], self.weight(1)[...]).astype(
            jnp.bfloat16
        )

    def project_value(self, slot):
        out = dot_nn(self.hid[self.slot_keys(slot)], self.weight(2)[...]) + self.vec(1)
        self.value[self.slot_keys(slot)] = out.astype(jnp.bfloat16)

    def attend(self, slot):
        valid = self.mask[slot]
        low_scaled = (self.low_f * self.scale).astype(jnp.bfloat16)
        high_scaled = (self.high_f * self.scale).astype(jnp.bfloat16)
        rows = self.rows
        for p in range(self.pairs):
            here = pl.ds(p * LANES, LANES)
            query_pair = self.query[self.slot_rows(slot), here]
            key_pair = self.key[self.slot_keys(slot), here]
            value_pair = self.value[self.slot_keys(slot), here]
            stacked = jnp.concatenate([query_pair * low_scaled, query_pair * high_scaled], axis=0)
            scores = dot_nt(stacked, key_pair) + valid
            raised = jnp.exp(scores - jnp.max(scores, axis=1, keepdims=True)).astype(jnp.bfloat16)
            self.shares[slot * self.pairs + p] = raised
            ones = jnp.ones((self.keys, LANES), jnp.bfloat16)
            summed = dot_nn(raised, jnp.concatenate([value_pair, ones], axis=1))
            inverse = 1.0 / summed[:, LANES:]
            out = summed[:, :LANES] * inverse
            self.inverse_total[self.slot_rows(slot), here] = jnp.where(self.low, inverse[:rows], inverse[rows:])
            self.mixed[self.slot_rows(slot), here] = jnp.where(self.low, out[:rows], out[rows:]).astype(jnp.bfloat16)

    def norm(self, slot, normed, inverse, gain_at, shift_at, rounded=None):
        for r in range(self.rows // CHUNK):
            here = pl.ds(r * CHUNK, CHUNK)
            there = pl.ds(slot * self.rows + r * CHUNK, CHUNK)
            z = self.work[here, :]
            centred = z - jnp.mean(z, axis=1, keepdims=True)
            inv = lax.rsqrt(jnp.mean(centred * centred, axis=1, keepdims=True) + EPS)
            unit = centred * inv
            normed[there] = unit.astype(jnp.bfloat16)
            inverse[there] = inv
            out = unit * self.vec(gain_at) + self.vec(shift_at)
            self.work[here, :] = out
            if rounded is not None:
                rounded[there] = out.astype(jnp.bfloat16)

    def branch(self, slot):
        out = dot_nn(self.mixed[self.slot_rows(slot)], self.weight(3)[...]) + self.vec(2)
        self.work[...] = out + self.hid[self.slot_queries(slot)].astype(jnp.float32)
        self.norm(slot, self.normed_one, self.inverse_one, 3, 4, self.first_b)

    def inner(self, slot, j):
        here = span(j, self.width)
        u = dot_nn(self.first_b[self.slot_rows(slot)], self.w_inner[:, here]) + self.inner_bias[:, here]
        cumulative = 0.5 * (1.0 + lax.erf(u * INV_ROOT_TWO))
        density = jnp.exp(-0.5 * u * u) * INV_ROOT_TWO_PI
        self.active[self.slot_rows(slot), here] = (u * cumulative).astype(jnp.bfloat16)
        self.slope[self.slot_rows(slot), here] = (cumulative + u * density).astype(jnp.bfloat16)

    def outer(self, slot):
        self.work[...] += dot_nn(self.active[self.slot_rows(slot)], self.w_outer[...]) + self.vec(5)
        self.norm(slot, self.normed_two, self.inverse_two, 6, 7)
        self.layer_out[slot] = self.work[0 : self.half].astype(jnp.bfloat16)

    def add_small(self, at, folded):
        self.small[LINE + at : LINE + at + 1, :] += jnp.sum(folded, axis=0, keepdims=True)

    def norm_back(self, slot, normed, inverse, gain_at, shift_at, bias_at, rounded):
        zero = jnp.zeros((8, self.width), jnp.float32)
        gain_sum, shift_sum, bias_sum = zero, zero, zero
        for r in range(self.rows // CHUNK):
            here = pl.ds(r * CHUNK, CHUNK)
            there = pl.ds(slot * self.rows + r * CHUNK, CHUNK)
            grad = self.work[here, :]
            unit = normed[there].astype(jnp.float32)
            gain_sum = gain_sum + fold(grad * unit)
            shift_sum = shift_sum + fold(grad)
            scaled = grad * self.vec(gain_at)
            dz = inverse[there] * (
                scaled
                - jnp.mean(scaled, axis=1, keepdims=True)
                - unit * jnp.mean(scaled * unit, axis=1, keepdims=True)
            )
            self.work[here, :] = dz
            dz_b = dz.astype(jnp.bfloat16)
            rounded[there] = dz_b
            bias_sum = bias_sum + fold(dz_b.astype(jnp.float32))
        self.add_small(gain_at, gain_sum)
        self.add_small(shift_at, shift_sum)
        self.add_small(bias_at, bias_sum)

    def outer_back(self, slot):
        self.work[0 : self.half] = self.cot[slot].astype(jnp.float32)
        self.work[self.half : self.rows] = self.memory[...]
        self.norm_back(slot, self.normed_two, self.inverse_two, 6, 7, 5, self.grad_two_b)

        def tile(j):
            here = span(j, self.width)
            rows = self.slot_rows(slot)
            grad = dot_nt(self.grad_two_b[rows], self.w_outer[here, :]) * self.slope[rows, here].astype(jnp.float32)
            grad_b = grad.astype(jnp.bfloat16)
            self.slope[rows, here] = grad_b
            self.inner_bias_grad[:, here] += jnp.sum(fold(grad_b.astype(jnp.float32)), axis=0, keepdims=True)

        fori(self.hidden // self.width, tile)

    def inner_back(self, slot):
        self.work[...] += dot_nt(self.slope[self.slot_rows(slot)], self.w_inner[...])
        self.norm_back(slot, self.normed_one, self.inverse_one, 3, 4, 2, self.grad_one_b)

    def attend_back(self, slot):
        rows = self.rows
        own = self.slot_rows(slot)
        every = self.slot_keys(slot)
        self.grad_mixed[...] = dot_nt(self.grad_one_b[own], self.weight(3)[...])

        def pair(p):
            here = pl.ds(p * LANES, LANES)
            query_pair = self.query[own, here]
            key_pair = self.key[every, here]
            value_pair = self.value[every, here]
            grad = self.grad_mixed[:, here].astype(jnp.bfloat16).astype(jnp.float32) * self.inverse_total[own, here]
            product = grad * self.mixed[own, here].astype(jnp.float32)
            delta = jnp.concatenate(
                [
                    jnp.sum(product * self.low_f, axis=1, keepdims=True),
                    jnp.sum(product * self.high_f, axis=1, keepdims=True),
                ],
                axis=0,
            )
            grad_b = grad.astype(jnp.bfloat16)
            stacked = jnp.concatenate([grad_b * self.low_b, grad_b * self.high_b], axis=0)
            raised = self.shares[slot * self.pairs + p]
            grad_scores = (raised.astype(jnp.float32) * (dot_nt(stacked, value_pair) - delta)).astype(jnp.bfloat16)
            both = dot_nn(grad_scores, key_pair)
            query_b = (jnp.where(self.low, both[:rows], both[rows:]) * self.scale).astype(jnp.bfloat16)
            queries = jnp.concatenate([query_pair * self.low_b, query_pair * self.high_b], axis=0)
            value_b = dot_tn(stacked, raised).T.astype(jnp.bfloat16)
            self.grad_query[own, here] = query_b
            self.grad_key[every, here] = (dot_tn(queries, grad_scores) * self.scale).T.astype(jnp.bfloat16)
            self.grad_value[every, here] = value_b
            self.small[LINE : LINE + 1, here] += jnp.sum(fold(query_b.astype(jnp.float32)), axis=0, keepdims=True)
            self.small[LINE + 1 : LINE + 2, here] += jnp.sum(fold(value_b.astype(jnp.float32)), axis=0, keepdims=True)

        for p in range(self.pairs):
            pair(p)

    def input_back(self, slot):
        every = self.slot_keys(slot)
        half = self.half
        grads = dot_nt(self.grad_key[every], self.weight(1)[...]) + dot_nt(self.grad_value[every], self.weight(2)[...])
        self.pair_out[slot] = grads[0:half].astype(jnp.bfloat16)
        mine = grads[half:] + dot_nt(self.grad_query[self.slot_rows(slot)], self.weight(0)[...]) + self.work[...]
        self.own_out[slot] = mine[0:half]
        memory = mine[half:]
        restart = self.start[slot] == 1
        counted = jnp.logical_or(
            jnp.logical_and(self.mem_row < MEM, restart),
            jnp.logical_and(self.mem_row >= MEM, self.mem_row < LINE),
        )
        self.small[0:MEMORY, :] += jnp.where(counted, memory, 0.0)
        return jnp.where(jnp.logical_and(self.mem_row < MEM, jnp.logical_not(restart)), memory, 0.0)

    def outer_weight_grad(self, j):
        here = span(j, self.width)
        self.w_outer[here, :] = dot_tn(self.active[:, here], self.grad_two_b[...]).astype(jnp.bfloat16)

    def inner_weight_grad(self, j):
        here = span(j, self.width)
        self.w_inner[:, here] = dot_tn(self.first_b[...], self.slope[:, here]).astype(jnp.bfloat16)

    def output_weight_grad(self):
        self.weight(3)[...] = dot_tn(self.mixed[...], self.grad_one_b[...]).astype(jnp.bfloat16)

    def query_weight_grad(self):
        total = None
        for slot in range(self.slots):
            term = dot_tn(self.hid[self.slot_queries(slot)], self.grad_query[self.slot_rows(slot)])
            total = term if total is None else total + term
        self.weight(0)[...] = total.astype(jnp.bfloat16)

    def key_weight_grad(self):
        self.weight(1)[...] = dot_tn(self.hid[...], self.grad_key[...]).astype(jnp.bfloat16)

    def value_weight_grad(self):
        self.weight(2)[...] = dot_tn(self.hid[...], self.grad_value[...]).astype(jnp.bfloat16)


def state_shapes(slots, half, width, hidden):
    rows, keys = half + MEMORY, 2 * half + MEMORY
    bf16, f32 = jnp.bfloat16, jnp.float32
    pairs = width // LANES
    return {
        "w_attention": ((width, 4 * width), bf16),
        "w_inner": ((width, hidden), bf16),
        "w_outer": ((hidden, width), bf16),
        "hid": ((slots * keys, width), bf16),
        "query": ((slots * rows, width), bf16),
        "key": ((slots * keys, width), bf16),
        "value": ((slots * keys, width), bf16),
        "shares": ((slots * pairs, 2 * rows, keys), bf16),
        "inverse_total": ((slots * rows, width), f32),
        "mixed": ((slots * rows, width), bf16),
        "normed_one": ((slots * rows, width), bf16),
        "normed_two": ((slots * rows, width), bf16),
        "inverse_one": ((slots * rows, 1), f32),
        "inverse_two": ((slots * rows, 1), f32),
        "first_b": ((slots * rows, width), bf16),
        "slope": ((slots * rows, hidden), bf16),
        "active": ((slots * rows, hidden), bf16),
        "grad_two_b": ((slots * rows, width), bf16),
        "grad_one_b": ((slots * rows, width), bf16),
        "grad_mixed": ((rows, width), f32),
        "grad_query": ((slots * rows, width), bf16),
        "grad_key": ((slots * keys, width), bf16),
        "grad_value": ((slots * keys, width), bf16),
        "work": ((rows, width), f32),
        "memory": ((MEMORY, width), f32),
        "swap_out": ((MEMORY, width), f32),
        "swap_in": ((MEMORY, width), f32),
    }


INPUTS = ("start", "mask", "tokens", "others", "cot", "vectors", "inner_bias")
OUTPUTS = ("layer_out", "own_out", "pair_out", "small", "inner_bias_grad")


def middle_kernel(names, *refs):
    refs = list(refs)
    given = {name: refs.pop(0) for name in INPUTS}
    weights = [refs.pop(0) for _ in range(6)]
    given.update({name: refs.pop(0) for name in OUTPUTS})
    grads = [refs.pop(0) for _ in range(6)]
    given.update({name: refs.pop(0) for name in names})
    load_sems, pair_sems = refs
    seq = lax.axis_index("seq")
    chain = lax.axis_index("chain")
    barrier = pltpu.get_barrier_semaphore()
    pl.semaphore_signal(barrier, inc=1, device_id=(1 - seq, chain), device_id_type=MESH)
    layer = Layer(seq, given)
    places = [layer.weight(i) for i in range(4)] + [layer.w_inner, layer.w_outer]
    loads = [pltpu.make_async_copy(weights[i], places[i], load_sems.at[i]) for i in range(6)]
    stores = [pltpu.make_async_copy(places[i], grads[i], load_sems.at[i]) for i in range(6)]
    for load in loads:
        load.start()
    layer.small[...] = jnp.zeros_like(layer.small)
    layer.inner_bias_grad[...] = jnp.zeros_like(layer.inner_bias_grad)
    for slot in range(layer.slots):
        def need(i):
            if slot == 0:
                loads[i].wait()
        base = slot * layer.keys
        layer.hid[base : base + layer.half] = layer.others[slot]
        layer.hid[base + layer.half : base + 2 * layer.half] = layer.tokens[slot]
        layer.set_memory(slot)
        need(0)
        layer.project_query(slot)
        need(1)
        layer.project_key(slot)
        need(2)
        layer.project_value(slot)
        layer.attend(slot)
        need(3)
        layer.branch(slot)
        need(4)
        fori(layer.hidden // layer.width, lambda j: layer.inner(slot, j))
        need(5)
        layer.outer(slot)
    layer.memory[...] = jnp.zeros_like(layer.memory)
    for slot in reversed(range(layer.slots)):
        layer.outer_back(slot)
        layer.inner_back(slot)
        if slot == 0:
            fori(layer.hidden // layer.width, layer.outer_weight_grad)
            stores[5].start()
            fori(layer.hidden // layer.width, layer.inner_weight_grad)
            stores[4].start()
        layer.attend_back(slot)
        passed = layer.input_back(slot)
        if slot > 0:
            layer.swap_out[...] = passed
            pl.semaphore_wait(barrier, 1)
            swap = pltpu.make_async_remote_copy(
                src_ref=layer.swap_out,
                dst_ref=layer.swap_in,
                send_sem=pair_sems.at[0],
                recv_sem=pair_sems.at[1],
                device_id=(1 - seq, chain),
                device_id_type=MESH,
            )
            swap.start()
            swap.wait()
            summed = pltpu.roll(passed + layer.swap_in[...], MEM, 0)
            layer.memory[...] = jnp.where(seq == 0, summed, 0.0)
    layer.output_weight_grad()
    stores[3].start()
    layer.query_weight_grad()
    stores[0].start()
    layer.key_weight_grad()
    stores[1].start()
    layer.value_weight_grad()
    stores[2].start()
    for store in stores:
        store.wait()


def middle(start, mask, tokens, others, cotangent, vectors, inner_bias, weights):
    slots, half, width = tokens.shape
    hidden = inner_bias.shape[1]
    bf16, f32 = jnp.bfloat16, jnp.float32
    inside = pl.BlockSpec(memory_space=pltpu.VMEM)
    anywhere = pl.BlockSpec(memory_space=pl.ANY)
    shape = jax.ShapeDtypeStruct
    state = state_shapes(slots, half, width, hidden)
    return pl.pallas_call(
        functools.partial(middle_kernel, tuple(state)),
        out_shape=[
            shape((slots, half, width), bf16),
            shape((slots, half, width), f32),
            shape((slots, half, width), bf16),
            shape((MEMORY, width), f32),
            shape((1, hidden), f32),
        ]
        + [shape(w.shape, bf16) for w in weights],
        in_specs=[pl.BlockSpec(memory_space=pltpu.SMEM)] + [inside] * 6 + [anywhere] * 6,
        out_specs=[inside] * 5 + [anywhere] * 6,
        scratch_shapes=[pltpu.VMEM(*s) for s in state.values()]
        + [pltpu.SemaphoreType.DMA((6,)), pltpu.SemaphoreType.DMA((2,))],
        compiler_params=pltpu.CompilerParams(
            collective_id=2, has_side_effects=True, vmem_limit_bytes=62 * 2**20
        ),
        cost_estimate=pl.CostEstimate(flops=31 * 10**9, bytes_accessed=40 * 10**6, transcendentals=10**7),
        name="layer",
    )(start, mask, tokens, others, cotangent, vectors, inner_bias, *weights)


def small_block(vectors, inner_bias, read_init, write_init):
    width = vectors[0].shape[0]
    inner_width = inner_bias.shape[0]
    rows = jnp.concatenate([read_init, write_init] + [v[None] for v in vectors], axis=0)
    rows = jnp.pad(rows, ((0, 4), (0, 128 - width)))
    return rows + jnp.pad(inner_bias[None], ((28, 3), (0, 128 - inner_width)))


def shards(
    tokens,
    cotangent,
    chain_start,
    seg_len,
    query_weight,
    key_weight,
    value_weight,
    output_weight,
    query_bias,
    value_bias,
    output_bias,
    first_gain,
    first_shift,
    inner_weight,
    inner_bias,
    outer_weight,
    outer_bias,
    second_gain,
    second_shift,
    read_init,
    write_init,
):
    slot_count = tokens.shape[1]
    half_rows = tokens.shape[2]
    model_width = tokens.shape[3]
    blocks = lax.axis_size("seq") * lax.axis_size("chain")
    levels = lax.axis_size("chain") // 4
    width = model_width // blocks
    inner_columns = inner_weight.shape[1]
    inner_width = inner_bias.shape[0]
    kernels = width % 8 == 0
    small = small_block(
        (query_bias, value_bias, output_bias, first_gain, first_shift, outer_bias, second_gain, second_shift),
        inner_bias,
        read_init,
        write_init,
    )
    shard_list = [query_weight, key_weight, value_weight, output_weight, inner_weight, outer_weight, small]
    parts = [(i, 0, width, 0, model_width) for i in range(4)]
    parts += [(4, 0, width, 0, inner_columns // 2), (4, 0, width, inner_columns // 2, inner_columns // 2)]
    parts += [(5, 0, inner_width // 2, 0, model_width), (5, inner_width // 2, inner_width // 2, 0, model_width)]
    parts += [(6, 0, 32, 0, 128)]
    pair = [(0, 1), (1, 0)]
    others = lax.ppermute(tokens[0], "seq", pair)
    if kernels:
        whole = gather_all(levels, shard_list, parts, (7,))
    else:
        whole = [lax.all_gather(w, ("seq", "chain"), axis=0) for w in shard_list]
    whole_query, whole_key, whole_value, whole_output, whole_inner, whole_outer = (
        w.reshape(-1, w.shape[-1]) for w in whole[:6]
    )
    small_all = whole[6]
    vectors = small_all[:, :, :width].transpose(1, 0, 2).reshape(32, model_width).astype(jnp.float32)
    bias_inner = small_all[:, 28, :inner_width].reshape(1, -1).astype(jnp.float32)
    my_index = lax.axis_index("seq")
    place_in = jnp.arange(half_rows)
    position = jnp.concatenate(
        [
            (1 - my_index) * half_rows + place_in,
            my_index * half_rows + place_in,
            jnp.where(jnp.arange(MEMORY) < 2 * MEM, -1, 1 << 30),
        ]
    )
    mask = jnp.where(position[None, :] < seg_len[0][:, None], 0.0, NEG_FILL)[:, None, :]
    results = middle(
        chain_start[0],
        mask,
        tokens[0],
        others,
        cotangent[0],
        vectors,
        bias_inner,
        (whole_query, whole_key, whole_value, whole_output, whole_inner, whole_outer),
    )
    layer_out = results[0][None]
    received = lax.ppermute(results[2], "seq", pair)
    input_grad = (results[1] + received.astype(jnp.float32)).astype(jnp.bfloat16)[None]
    small_grads = jnp.pad(
        results[3].reshape(32, blocks, width).transpose(1, 0, 2), ((0, 0), (0, 0), (0, 128 - width))
    )
    inner_rows = jnp.pad(results[4].reshape(blocks, 1, inner_width), ((0, 0), (28, 3), (0, 128 - inner_width)))
    small_grads = jnp.where(jnp.arange(32)[None, :, None] == 28, inner_rows, small_grads).astype(jnp.bfloat16)
    weight_grads = [g.reshape((blocks,) + s.shape) for g, s in zip(results[5:], shard_list)]
    partial_grads = weight_grads + [small_grads]
    if kernels:
        sums = scatter_all(levels, partial_grads, parts)
    else:
        sums = [
            lax.psum_scatter(
                lax.psum_scatter(
                    g.reshape((-1,) + g.shape[2:]), "seq", scatter_dimension=0, tiled=True
                ).astype(jnp.float32),
                "chain", scatter_dimension=0, tiled=True,
            )
            for g in partial_grads
        ]
    small_sum = sums[6].reshape(32, 128)
    vector = [small_sum[20 + i, :width] for i in range(8)]
    return (
        layer_out,
        input_grad,
        sums[0],
        sums[1],
        sums[2],
        sums[3],
        vector[0],
        vector[1],
        vector[2],
        vector[3],
        vector[4],
        sums[4],
        small_sum[28, :inner_width],
        sums[5],
        vector[5],
        vector[6],
        vector[7],
        small_sum[:MEM, :width],
        small_sum[MEM : 2 * MEM, :width],
    )


def solution(mesh):
    placed = (
        P("chain", None, "seq", None),
        P("chain", None, "seq", None),
        P("chain", None),
        P("chain", None),
        P(("seq", "chain"), None),
        P(("seq", "chain"), None),
        P(("seq", "chain"), None),
        P(("seq", "chain"), None),
        P(("seq", "chain")),
        P(("seq", "chain")),
        P(("seq", "chain")),
        P(("seq", "chain")),
        P(("seq", "chain")),
        P(("seq", "chain"), None),
        P(("seq", "chain")),
        P(("seq", "chain"), None),
        P(("seq", "chain")),
        P(("seq", "chain")),
        P(("seq", "chain")),
        P(None, ("seq", "chain")),
        P(None, ("seq", "chain")),
    )
    return jax.shard_map(
        shards,
        mesh=mesh,
        in_specs=placed,
        out_specs=(
            P("chain", None, "seq", None),
            P("chain", None, "seq", None),
            P(("seq", "chain"), None),
            P(("seq", "chain"), None),
            P(("seq", "chain"), None),
            P(("seq", "chain"), None),
            P(("seq", "chain")),
            P(("seq", "chain")),
            P(("seq", "chain")),
            P(("seq", "chain")),
            P(("seq", "chain")),
            P(("seq", "chain"), None),
            P(("seq", "chain")),
            P(("seq", "chain"), None),
            P(("seq", "chain")),
            P(("seq", "chain")),
            P(("seq", "chain")),
            P(None, ("seq", "chain")),
            P(None, ("seq", "chain")),
        ),
        check_vma=False,
    )
```

```python
import functools
import math
from typing import Any, NamedTuple

import jax
import jax.numpy as jnp
from jax import lax
from jax.experimental import pallas as pl
from jax.experimental.pallas import tpu as pltpu
from jax.sharding import PartitionSpec as P

HEADS = 12
MEM = 10
EPS = 1e-12
INV_ROOT_TWO = 1.0 / math.sqrt(2.0)
INV_ROOT_TWO_PI = 1.0 / math.sqrt(2.0 * math.pi)
NEG_FILL = -1000000000.0

AXES = ("seq", "chain")


MESH = pl.DeviceIdType.MESH


def place():
    seq = lax.axis_index(AXES[0])
    chain = lax.axis_index(AXES[1])
    return seq, chain // 4, lax.rem(chain // 2, 2), lax.rem(chain, 2)


def block_of(levels, seq, level, side, core):
    return seq * (4 * levels) + level * 4 + side * 2 + core


def device_of(seq, level, side, core):
    return (seq, level * 4 + side * 2 + core)


def fori(count, body):
    def step(index, carry):
        body(index)
        return carry

    lax.fori_loop(0, count, step, 0)


def span(index, size):
    return pl.ds(pl.multiple_of(index * size, size), size)


def dot_nn(former, latter):
    return jnp.dot(former, latter, preferred_element_type=jnp.float32)


def dot_nt(former, latter):
    return lax.dot_general(former, latter, (((1,), (1,)), ((), ())), preferred_element_type=jnp.float32)


def dot_tn(former, latter):
    return lax.dot_general(former, latter, (((0,), (0,)), ((), ())), preferred_element_type=jnp.float32)


def fold(rows):
    return jnp.sum(rows.reshape(rows.shape[0] // 8, 8, rows.shape[1]), axis=0)


CHUNK = 48
MEMORY = 32
LANES = 128
LINE = 2 * MEM


class Layer:
    def __init__(self, seq, refs):
        self.seq = seq
        self.__dict__.update(refs)
        self.slots = self.layer_out.shape[0]
        self.half, self.width = self.layer_out.shape[1:]
        self.rows = self.half + MEMORY
        self.keys = self.rows + self.half
        self.hidden = self.w_inner.shape[1]
        self.pairs = self.width // LANES
        self.scale = 1.0 / math.sqrt(self.width // HEADS)
        lane = lax.broadcasted_iota(jnp.int32, (1, LANES), 1)
        self.low = lane < LANES // 2
        self.low_f = jnp.where(self.low, 1.0, 0.0)
        self.low_b = self.low_f.astype(jnp.bfloat16)
        self.high_f = 1.0 - self.low_f
        self.high_b = self.high_f.astype(jnp.bfloat16)
        self.mem_row = lax.broadcasted_iota(jnp.int32, (MEMORY, 1), 0)

    def vec(self, at):
        return self.vectors[LINE + at : LINE + at + 1, :]

    def slot_rows(self, slot):
        return pl.ds(slot * self.rows, self.rows)

    def slot_keys(self, slot):
        return pl.ds(slot * self.keys, self.keys)

    def slot_queries(self, slot):
        return pl.ds(slot * self.keys + self.half, self.rows)

    def weight(self, at):
        return self.w_attention.at[:, pl.ds(at * self.width, self.width)]

    def set_memory(self, slot):
        initial = jnp.where(self.mem_row < LINE, self.vectors[0:MEMORY, :], 0.0)
        if slot > 0:
            second = self.work[self.half : self.rows].astype(jnp.bfloat16).astype(jnp.float32)
            carried = pltpu.roll(second, MEMORY - MEM, 0)
        else:
            carried = jnp.zeros_like(initial)
        restart = self.start[slot] == 1
        initial = jnp.where(jnp.logical_or(self.mem_row >= MEM, restart), initial, carried)
        base = slot * self.keys + 2 * self.half
        self.hid[base : base + MEMORY] = initial.astype(jnp.bfloat16)

    def project_query(self, slot):
        out = dot_nn(self.hid[self.slot_queries(slot)], self.weight(0)[...]) + self.vec(0)
        self.query[self.slot_rows(slot)] = out.astype(jnp.bfloat16)

    def project_key(self, slot):
        self.key[self.slot_keys(slot)] = dot_nn(self.hid[self.slot_keys(slot)], self.weight(1)[...]).astype(
            jnp.bfloat16
        )

    def project_value(self, slot):
        out = dot_nn(self.hid[self.slot_keys(slot)], self.weight(2)[...]) + self.vec(1)
        self.value[self.slot_keys(slot)] = out.astype(jnp.bfloat16)

    def share_at(self, slot, p):
        return p if self.shares.shape[0] == self.pairs else slot * self.pairs + p

    def attend(self, slot, pairs=None):
        valid = self.mask[slot]
        low_scaled = (self.low_f * self.scale).astype(jnp.bfloat16)
        high_scaled = (self.high_f * self.scale).astype(jnp.bfloat16)
        rows = self.rows
        for p in pairs or range(self.pairs):
            here = pl.ds(p * LANES, LANES)
            query_pair = self.query[self.slot_rows(slot), here]
            key_pair = self.key[self.slot_keys(slot), here]
            value_pair = self.value[self.slot_keys(slot), here]
            stacked = jnp.concatenate([query_pair * low_scaled, query_pair * high_scaled], axis=0)
            scores = dot_nt(stacked, key_pair) + valid
            raised = jnp.exp(scores - jnp.max(scores, axis=1, keepdims=True)).astype(jnp.bfloat16)
            self.shares[self.share_at(slot, p)] = raised
            ones = jnp.ones((self.keys, LANES), jnp.bfloat16)
            summed = dot_nn(raised, jnp.concatenate([value_pair, ones], axis=1))
            inverse = 1.0 / summed[:, LANES:]
            out = summed[:, :LANES] * inverse
            self.inverse_total[self.slot_rows(slot), here] = jnp.where(self.low, inverse[:rows], inverse[rows:])
            self.mixed[self.slot_rows(slot), here] = jnp.where(self.low, out[:rows], out[rows:]).astype(jnp.bfloat16)

    def norm(self, slot, normed, inverse, gain_at, shift_at, rounded=None):
        for r in range(self.rows // CHUNK):
            here = pl.ds(r * CHUNK, CHUNK)
            there = pl.ds(slot * self.rows + r * CHUNK, CHUNK)
            z = self.work[here, :]
            centred = z - jnp.mean(z, axis=1, keepdims=True)
            inv = lax.rsqrt(jnp.mean(centred * centred, axis=1, keepdims=True) + EPS)
            unit = centred * inv
            normed[there] = unit.astype(jnp.bfloat16)
            self.inverse[there, inverse : inverse + 1] = inv
            out = unit * self.vec(gain_at) + self.vec(shift_at)
            self.work[here, :] = out
            if rounded is not None:
                rounded[there] = out.astype(jnp.bfloat16)

    def branch(self, slot):
        out = dot_nn(self.mixed[self.slot_rows(slot)], self.weight(3)[...]) + self.vec(2)
        self.work[...] = out + self.hid[self.slot_queries(slot)].astype(jnp.float32)
        self.norm(slot, self.normed_one, 0, 3, 4, self.first_b)

    def inner(self, slot, j):
        here = span(j, self.width)
        u = dot_nn(self.first_b[self.slot_rows(slot)], self.w_inner[:, here]) + self.inner_bias[:, here]
        cumulative = 0.5 * (1.0 + lax.erf(u * INV_ROOT_TWO))
        density = jnp.exp(-0.5 * u * u) * INV_ROOT_TWO_PI
        self.active[self.slot_rows(slot), here] = (u * cumulative).astype(jnp.bfloat16)
        self.slope[self.slot_rows(slot), here] = (cumulative + u * density).astype(jnp.bfloat16)

    def outer(self, slot):
        self.work[...] += dot_nn(self.active[self.slot_rows(slot)], self.w_outer[...]) + self.vec(5)
        self.norm(slot, self.normed_two, 1, 6, 7)
        self.layer_out[slot] = self.work[0 : self.half].astype(jnp.bfloat16)

    def add_small(self, at, folded):
        self.small[LINE + at : LINE + at + 1, :] += jnp.sum(folded, axis=0, keepdims=True)

    def norm_back(self, slot, normed, inverse, gain_at, shift_at, bias_at, rounded):
        zero = jnp.zeros((8, self.width), jnp.float32)
        gain_sum, shift_sum, bias_sum = zero, zero, zero
        for r in range(self.rows // CHUNK):
            here = pl.ds(r * CHUNK, CHUNK)
            there = pl.ds(slot * self.rows + r * CHUNK, CHUNK)
            grad = self.work[here, :]
            unit = normed[there].astype(jnp.float32)
            gain_sum = gain_sum + fold(grad * unit)
            shift_sum = shift_sum + fold(grad)
            scaled = grad * self.vec(gain_at)
            dz = self.inverse[there, inverse : inverse + 1] * (
                scaled
                - jnp.mean(scaled, axis=1, keepdims=True)
                - unit * jnp.mean(scaled * unit, axis=1, keepdims=True)
            )
            self.work[here, :] = dz
            dz_b = dz.astype(jnp.bfloat16)
            rounded[there] = dz_b
            bias_sum = bias_sum + fold(dz_b.astype(jnp.float32))
        self.add_small(gain_at, gain_sum)
        self.add_small(shift_at, shift_sum)
        self.add_small(bias_at, bias_sum)

    def outer_back(self, slot):
        self.work[0 : self.half] = self.cot[slot if self.cot.shape[0] > 1 else 0].astype(jnp.float32)
        self.work[self.half : self.rows] = self.memory[...]
        self.norm_back(slot, self.normed_two, 1, 6, 7, 5, self.grad_two_b)

        def tile(j):
            here = span(j, self.width)
            rows = self.slot_rows(slot)
            grad = dot_nt(self.grad_two_b[rows], self.w_outer[here, :]) * self.slope[rows, here].astype(jnp.float32)
            grad_b = grad.astype(jnp.bfloat16)
            self.slope[rows, here] = grad_b
            self.inner_bias_grad[:, here] += jnp.sum(fold(grad_b.astype(jnp.float32)), axis=0, keepdims=True)

        fori(self.hidden // self.width, tile)

    def inner_back(self, slot):
        self.work[...] += dot_nt(self.slope[self.slot_rows(slot)], self.w_inner[...])
        self.norm_back(slot, self.normed_one, 0, 3, 4, 2, self.grad_one_b)

    def mix_back(self, slot):
        grad = dot_nt(self.grad_one_b[self.slot_rows(slot)], self.weight(3)[...])
        self.grad_mixed[...] = grad.astype(jnp.bfloat16)

    def attend_back(self, slot, pairs=None):
        rows = self.rows
        own = self.slot_rows(slot)
        every = self.slot_keys(slot)

        def pair(p):
            here = pl.ds(p * LANES, LANES)
            query_pair = self.query[own, here]
            key_pair = self.key[every, here]
            value_pair = self.value[every, here]
            grad = self.grad_mixed[:, here].astype(jnp.float32) * self.inverse_total[own, here]
            product = grad * self.mixed[own, here].astype(jnp.float32)
            delta = jnp.concatenate(
                [
                    jnp.sum(product * self.low_f, axis=1, keepdims=True),
                    jnp.sum(product * self.high_f, axis=1, keepdims=True),
                ],
                axis=0,
            )
            grad_b = grad.astype(jnp.bfloat16)
            stacked = jnp.concatenate([grad_b * self.low_b, grad_b * self.high_b], axis=0)
            raised = self.shares[self.share_at(slot, p)]
            grad_scores = (raised.astype(jnp.float32) * (dot_nt(stacked, value_pair) - delta)).astype(jnp.bfloat16)
            both = dot_nn(grad_scores, key_pair)
            query_b = (jnp.where(self.low, both[:rows], both[rows:]) * self.scale).astype(jnp.bfloat16)
            queries = jnp.concatenate([query_pair * self.low_b, query_pair * self.high_b], axis=0)
            value_b = dot_tn(stacked, raised).T.astype(jnp.bfloat16)
            self.grad_query[own, here] = query_b
            self.grad_key[every, here] = (dot_tn(queries, grad_scores) * self.scale).T.astype(jnp.bfloat16)
            self.grad_value[every, here] = value_b
            self.small[LINE : LINE + 1, here] += jnp.sum(fold(query_b.astype(jnp.float32)), axis=0, keepdims=True)
            self.small[LINE + 1 : LINE + 2, here] += jnp.sum(fold(value_b.astype(jnp.float32)), axis=0, keepdims=True)

        for p in pairs or range(self.pairs):
            pair(p)

    def input_back(self, slot):
        every = self.slot_keys(slot)
        half = self.half
        grads = dot_nt(self.grad_key[every], self.weight(1)[...]) + dot_nt(self.grad_value[every], self.weight(2)[...])
        self.pair_out[slot] = grads[0:half].astype(jnp.bfloat16)
        mine = grads[half:] + dot_nt(self.grad_query[self.slot_rows(slot)], self.weight(0)[...]) + self.work[...]
        self.own_out[slot] = mine[0:half].astype(self.own_out.dtype)
        memory = mine[half:]
        restart = self.start[slot] == 1
        counted = jnp.logical_or(
            jnp.logical_and(self.mem_row < MEM, restart),
            jnp.logical_and(self.mem_row >= MEM, self.mem_row < LINE),
        )
        self.small[0:MEMORY, :] += jnp.where(counted, memory, 0.0)
        return jnp.where(jnp.logical_and(self.mem_row < MEM, jnp.logical_not(restart)), memory, 0.0)

    def outer_weight_grad(self, j):
        here = span(j, self.width)
        self.w_outer[here, :] = dot_tn(self.active[:, here], self.grad_two_b[...]).astype(jnp.bfloat16)

    def inner_weight_grad(self, j):
        here = span(j, self.width)
        self.w_inner[:, here] = dot_tn(self.first_b[...], self.slope[:, here]).astype(jnp.bfloat16)

    def output_weight_grad(self):
        self.weight(3)[...] = dot_tn(self.mixed[...], self.grad_one_b[...]).astype(jnp.bfloat16)

    def query_weight_grad(self):
        total = None
        for slot in range(self.slots):
            term = dot_tn(self.hid[self.slot_queries(slot)], self.grad_query[self.slot_rows(slot)])
            total = term if total is None else total + term
        self.weight(0)[...] = total.astype(jnp.bfloat16)

    def key_weight_grad(self):
        self.weight(1)[...] = dot_tn(self.hid[...], self.grad_key[...]).astype(jnp.bfloat16)

    def value_weight_grad(self):
        self.weight(2)[...] = dot_tn(self.hid[...], self.grad_value[...]).astype(jnp.bfloat16)


class State(NamedTuple):
    w_attention: Any
    w_inner: Any
    w_outer: Any
    hid: Any
    query: Any
    key: Any
    value: Any
    shares: Any
    inverse_total: Any
    mixed: Any
    normed_one: Any
    normed_two: Any
    inverse: Any
    first_b: Any
    slope: Any
    active: Any
    grad_two_b: Any
    grad_one_b: Any
    grad_mixed: Any
    grad_query: Any
    grad_key: Any
    grad_value: Any
    work: Any
    memory: Any
    swap_out: Any
    swap_in: Any


def state_shapes(slots, half, width, hidden):
    rows, keys = half + MEMORY, 2 * half + MEMORY
    bf16, f32 = jnp.bfloat16, jnp.float32
    pairs = width // LANES
    by_row, by_key = ((slots * rows, width), bf16), ((slots * keys, width), bf16)
    return State(
        w_attention=((width, 4 * width), bf16),
        w_inner=((width, hidden), bf16),
        w_outer=((hidden, width), bf16),
        hid=by_key,
        query=by_row,
        key=by_key,
        value=by_key,
        shares=((slots * pairs, 2 * rows, keys), bf16),
        inverse_total=((slots * rows, width), f32),
        mixed=by_row,
        normed_one=by_row,
        normed_two=by_row,
        inverse=((slots * rows, 2), f32),
        first_b=by_row,
        slope=((slots * rows, hidden), bf16),
        active=((slots * rows, hidden), bf16),
        grad_two_b=by_row,
        grad_one_b=by_row,
        grad_mixed=((rows, width), bf16),
        grad_query=by_row,
        grad_key=by_key,
        grad_value=by_key,
        work=((rows, width), f32),
        memory=((MEMORY, width), f32),
        swap_out=((MEMORY, width), f32),
        swap_in=((MEMORY, width), f32),
    )


class Inputs(NamedTuple):
    start: Any
    mask: Any
    tokens: Any
    others: Any
    cot: Any
    vectors: Any
    inner_bias: Any


class Outputs(NamedTuple):
    layer_out: Any
    own_out: Any
    pair_out: Any
    small: Any
    inner_bias_grad: Any


def take(refs, kind):
    return kind(*(refs.pop(0) for _ in kind._fields))._asdict()


def middle_kernel(*refs):
    refs = list(refs)
    given = take(refs, Inputs)
    weights = [refs.pop(0) for _ in range(6)]
    given.update(take(refs, Outputs))
    grads = [refs.pop(0) for _ in range(6)]
    given.update(take(refs, State))
    load_sems, pair_sems = refs
    seq = lax.axis_index(AXES[0])
    chain = lax.axis_index(AXES[1])
    barrier = pltpu.get_barrier_semaphore()
    pl.semaphore_signal(barrier, inc=1, device_id=(1 - seq, chain), device_id_type=MESH)
    layer = Layer(seq, given)
    places = [layer.weight(i) for i in range(4)] + [layer.w_inner, layer.w_outer]
    loads = [pltpu.make_async_copy(weights[i], places[i], load_sems.at[i]) for i in range(6)]
    stores = [pltpu.make_async_copy(places[i], grads[i], load_sems.at[i]) for i in range(6)]
    for load in loads:
        load.start()
    layer.small[...] = jnp.zeros_like(layer.small)
    layer.inner_bias_grad[...] = jnp.zeros_like(layer.inner_bias_grad)
    for slot in range(layer.slots):
        def need(i):
            if slot == 0:
                loads[i].wait()
        base = slot * layer.keys
        layer.hid[base : base + layer.half] = layer.others[slot]
        layer.hid[base + layer.half : base + 2 * layer.half] = layer.tokens[slot]
        layer.set_memory(slot)
        need(0)
        layer.project_query(slot)
        need(1)
        layer.project_key(slot)
        need(2)
        layer.project_value(slot)
        layer.attend(slot)
        need(3)
        layer.branch(slot)
        need(4)
        fori(layer.hidden // layer.width, lambda j: layer.inner(slot, j))
        need(5)
        layer.outer(slot)
    layer.memory[...] = jnp.zeros_like(layer.memory)
    for slot in reversed(range(layer.slots)):
        layer.outer_back(slot)
        layer.inner_back(slot)
        if slot == 0:
            fori(layer.hidden // layer.width, layer.outer_weight_grad)
            stores[5].start()
            fori(layer.hidden // layer.width, layer.inner_weight_grad)
            stores[4].start()
        layer.mix_back(slot)
        layer.attend_back(slot)
        passed = layer.input_back(slot)
        if slot > 0:
            layer.swap_out[...] = passed
            pl.semaphore_wait(barrier, 1)
            swap = pltpu.make_async_remote_copy(
                src_ref=layer.swap_out,
                dst_ref=layer.swap_in,
                send_sem=pair_sems.at[0],
                recv_sem=pair_sems.at[1],
                device_id=(1 - seq, chain),
                device_id_type=MESH,
            )
            swap.start()
            swap.wait()
            summed = pltpu.roll(passed + layer.swap_in[...], MEM, 0)
            layer.memory[...] = jnp.where(seq == 0, summed, 0.0)
    layer.output_weight_grad()
    stores[3].start()
    layer.query_weight_grad()
    stores[0].start()
    layer.key_weight_grad()
    stores[1].start()
    layer.value_weight_grad()
    stores[2].start()
    for store in stores:
        store.wait()


def middle(start, mask, tokens, others, cotangent, vectors, inner_bias, weights):
    slots, half, width = tokens.shape
    hidden = inner_bias.shape[1]
    bf16, f32 = jnp.bfloat16, jnp.float32
    inside = pl.BlockSpec(memory_space=pltpu.VMEM)
    anywhere = pl.BlockSpec(memory_space=pl.ANY)
    shape = jax.ShapeDtypeStruct
    state = state_shapes(slots, half, width, hidden)
    return pl.pallas_call(
        middle_kernel,
        out_shape=[
            shape((slots, half, width), bf16),
            shape((slots, half, width), f32),
            shape((slots, half, width), bf16),
            shape((MEMORY, width), f32),
            shape((1, hidden), f32),
        ]
        + [shape(w.shape, bf16) for w in weights],
        in_specs=[pl.BlockSpec(memory_space=pltpu.SMEM)] + [inside] * 6 + [anywhere] * 6,
        out_specs=[inside] * 5 + [anywhere] * 6,
        scratch_shapes=[pltpu.VMEM(*s) for s in state]
        + [pltpu.SemaphoreType.DMA((6,)), pltpu.SemaphoreType.DMA((2,))],
        compiler_params=pltpu.CompilerParams(
            collective_id=2, has_side_effects=True, vmem_limit_bytes=62 * 2**20
        ),
        cost_estimate=pl.CostEstimate(flops=31 * 10**9, bytes_accessed=40 * 10**6, transcendentals=10**7),
    )(start, mask, tokens, others, cotangent, vectors, inner_bias, *weights)


class Links:
    def __init__(self, levels, refs):
        self.levels = levels
        self.seq, self.level, self.side, self.core = place()
        self.__dict__.update(refs)
        self.width = self.w_attention.shape[0]
        self.thick = self.width // (4 * levels)
        self.tall = self.w_outer.shape[0] // (8 * levels)

    def device(self, kind):
        seq, level, side, core = self.seq, self.level, self.side, self.core
        return device_of(
            *(
                (seq, level, side, 1 - core),
                (seq, level, 1 - side, core),
                (1 - seq, level, side, core),
                (seq, level + 1, side, core),
                (seq, level - 1, side, core),
            )[kind]
        )

    def chip(self, rel, at):
        seq = self.seq if rel < 2 else 1 - self.seq
        side = self.side if rel % 2 == 0 else 1 - self.side
        return seq * (2 * self.levels) + at * 2 + side

    def view(self, part, chip, core, small):
        if part < 4:
            whole = self.w_attention if part < 2 else self.w_inner
            column = pl.multiple_of(core * (2 * self.width) + (part % 2) * self.width, LANES)
            return whole.at[
                pl.ds(pl.multiple_of(chip * self.thick, 16), self.thick), pl.ds(column, self.width)
            ]
        if part < 6:
            size = self.tall // 2
            row = pl.multiple_of(chip * (2 * self.tall) + core * self.tall + (part - 4) * size, 16)
            return self.w_outer.at[pl.ds(row, size), :]
        return small.at[chip * 2 + core]

    def remote(self, source, target, send_sem, recv_sem, kind):
        return pltpu.make_async_remote_copy(
            src_ref=source,
            dst_ref=target,
            send_sem=send_sem,
            recv_sem=recv_sem,
            device_id=self.device(kind),
            device_id_type=MESH,
        )

    def amount(self, part, count):
        if part < 6:
            return self.w_outer.at[pl.ds(0, count * self.thick), :]
        return self.small_all.at[pl.ds(0, count)]

    def all_sent(self, part, count, semaphore):
        whole = self.amount(part, count)
        self.remote(whole, whole, semaphore, semaphore, 0).wait_send()

    def all_arrived(self, part, count, semaphore):
        whole = self.amount(part, count)
        self.remote(whole, whole, semaphore, semaphore, 0).wait_recv()

    def has_up(self):
        return self.level < self.levels - 1

    def has_down(self):
        return self.level > 0

    def neighbours(self):
        return 3 + self.has_up().astype(jnp.int32) + self.has_down().astype(jnp.int32)

    def tell_all(self, semaphore):
        for kind in range(3):
            pl.semaphore_signal(semaphore, inc=1, device_id=self.device(kind), device_id_type=MESH)

        @pl.when(self.has_up())
        def _():
            pl.semaphore_signal(semaphore, inc=1, device_id=self.device(3), device_id_type=MESH)

        @pl.when(self.has_down())
        def _():
            pl.semaphore_signal(semaphore, inc=1, device_id=self.device(4), device_id_type=MESH)


class Gather(Links):
    def copy(self, part, rel, at, kind):
        chip = self.chip(rel, at)
        here = self.view(part, chip, self.core, self.small_all)
        arrives = self.gather_recv.at[part, chip]
        if kind == 0:
            sends, arrives = self.core_send.at[part], self.core_recv.at[part]
        elif kind < 3:
            sends = self.plane_send.at[part, kind - 1]
        elif part in LATE:
            sends = self.late_send.at[LATE.index(part), rel, at + (kind - 3)]
        else:
            sends = self.line_send.at[part, at + (kind - 3)]
        return self.remote(here, here, sends, arrives, kind)

    def arrived(self, part, rel, at):
        self.copy(part, rel, at, 1).wait_recv()

    def up(self, part, rel, at):
        pl.when(self.has_up())(lambda: self.copy(part, rel, at, 3).start())

    def down(self, part, rel, at):
        pl.when(self.has_down())(lambda: self.copy(part, rel, at, 4).start())

    def own(self, part):
        self.up(part, 0, self.level)
        self.down(part, 0, self.level)
        for kind in (1, 2, 0):
            self.copy(part, 0, self.level, kind).start()

    def from_plane(self, part, at):
        self.arrived(part, 1, at)
        if GATHER_ROUTES[part] == 0:
            self.copy(part, 1, at, 2).start()
        self.copy(part, 1, at, 0).start()
        self.arrived(part, 2, at)
        if GATHER_ROUTES[part] == 1:
            self.copy(part, 2, at, 1).start()
        self.copy(part, 2, at, 0).start()

    def from_corner(self, part, at):
        self.arrived(part, 3, at)
        self.copy(part, 3, at, 0).start()

    def guarded(self, at, body):
        pl.when(jnp.logical_and(at >= 0, at < self.levels))(body)

    def step(self, part, step):
        levels, level = self.levels, self.level
        if part in LATE:
            if step == 1:
                self.from_plane(part, level)
                for rel in (1, 2):
                    self.up(part, rel, level)
                    self.down(part, rel, level)
            if step == 2:
                self.from_corner(part, level)
                self.up(part, 3, level)
                self.down(part, 3, level)
            if 2 <= step <= levels:
                for sign in (-1, 1):
                    at = level + sign * (step - 1)

                    def four(at=at, sign=sign):
                        for rel in range(4):
                            self.arrived(part, rel, at)
                            (self.up if sign < 0 else self.down)(part, rel, at)
                            self.copy(part, rel, at, 0).start()

                    self.guarded(at, four)
            return
        if 1 <= step < levels:
            for sign in (-1, 1):
                at = level + sign * step

                def column(at=at, sign=sign):
                    self.arrived(part, 0, at)
                    (self.up if sign < 0 else self.down)(part, 0, at)
                    for kind in (1, 2, 0):
                        self.copy(part, 0, at, kind).start()

                self.guarded(at, column)
        if 1 <= step < levels + 1:
            near = step - 1
            for sign in (-1, 1) if near else (1,):
                at = level + sign * near
                self.guarded(at, functools.partial(self.from_plane, part, at))
        if 2 <= step < levels + 2:
            near = step - 2
            for sign in (-1, 1) if near else (1,):
                at = level + sign * near
                self.guarded(at, functools.partial(self.from_corner, part, at))

    def other_core(self, part):
        self.all_arrived(part, 4 * self.levels, self.core_recv.at[part])

    def sent(self, part):
        self.all_sent(part, 4 * self.levels, self.core_send.at[part])
        count = 1 if part in LATE else self.levels
        for kind in (1, 2):
            routed = GATHER_ROUTES[part] == 2 - kind
            self.all_sent(part, count * (1 + routed), self.plane_send.at[part, kind - 1])

        def body(at):
            for rel in range(4 if part in LATE else 1):
                pl.when(jnp.logical_and(at <= self.level, self.has_up()))(
                    lambda rel=rel: self.copy(part, rel, at, 3).wait_send()
                )
                pl.when(jnp.logical_and(at >= self.level, self.has_down()))(
                    lambda rel=rel: self.copy(part, rel, at, 4).wait_send()
                )

        fori(self.levels, body)


class Scatter(Links):
    def land(self, kind, part, slot):
        if part >= 2:
            return self.lands[part - 2][kind].at[slot]
        levels = self.levels
        at = slot + (0, 4 * levels, 4 * levels + self.side_slots(part), 7 * levels)[kind]
        hold = self.active if part == 0 else self.slope
        per_row = hold.shape[1] // self.width
        row = pl.multiple_of((at // per_row) * self.thick, 16)
        column = pl.multiple_of(lax.rem(at, per_row) * self.width, LANES)
        return hold.at[pl.ds(row, self.thick), pl.ds(column, self.width)]

    def route(self, part):
        return ROUTES[part]

    def side_slots(self, part):
        return (2 if self.route(part) == 0 else 1) * self.levels

    def mine(self, part, rel, at, core=None):
        return self.view(part, self.chip(rel, at), self.core if core is None else core, self.small_grad)

    def over_core(self, part, at, rel):
        return self.remote(
            self.mine(part, rel, at, 1 - self.core),
            self.land(0, part, at * 4 + rel),
            self.sum_core_send.at[part],
            self.sum_core_recv.at[part],
            0,
        )

    def over(self, kind, part, at, rel, routed):
        spot = at + (2 if routed else kind - 1) * self.levels
        return self.remote(
            self.land(0, part, at * 4 + rel),
            self.land(kind, part, at + routed * self.levels),
            self.sum_plane_send.at[part, kind - 1],
            self.sum_plane_recv.at[part, spot],
            kind,
        )

    def along(self, part, target, kind):
        slot = target + 1 if kind == 3 else target
        return self.remote(
            self.land(0, part, target * 4),
            self.land(3, part, slot),
            self.sum_line_send.at[part, target],
            self.sum_line_recv.at[part, slot],
            kind,
        )

    def total(self, part, at, rel, *more):
        value = self.mine(part, rel, at)[...].astype(jnp.float32)
        value = value + self.land(0, part, at * 4 + rel)[...].astype(jnp.float32)
        for ref in more:
            value = value + ref[...].astype(jnp.float32)
        return value

    def keep(self, part, at, rel, value):
        self.land(0, part, at * 4 + rel)[...] = value.astype(jnp.bfloat16)

    def start_core(self, part):
        for rel in (3, 1, 2, 0):
            fori(self.levels, lambda at: self.over_core(part, at, rel).start())

    def corner(self, part):
        self.all_arrived(part, 4 * self.levels, self.sum_core_recv.at[part])

        def body(at):
            self.keep(part, at, 3, self.total(part, at, 3))
            self.over(1 + self.route(part), part, at, 3, 1).start()

        fori(self.levels, body)

    def plane(self, part):
        def body(at):
            routed = 1 + self.route(part)
            first, second = (1, 2) if routed == 1 else (2, 1)
            self.keep(part, at, first, self.total(part, at, first))
            self.over(first, part, at, first, 0).start()
            self.over(routed, part, at, 3, 1).wait_recv()
            self.keep(part, at, second, self.total(part, at, second, self.land(routed, part, at + self.levels)))
            self.over(second, part, at, second, 0).start()

        fori(self.levels, body)

    def ready(self, part, at):
        self.over(1, part, at, 1, 0).wait_recv()
        self.over(2, part, at, 2, 0).wait_recv()

    def column(self, part, at, *more):
        return self.total(part, at, 0, self.land(1, part, at), self.land(2, part, at), *more)

    def line(self, part, step):
        last = self.levels - 1
        level = self.level

        def go(target, kind, first):
            self.ready(part, target)

            @pl.when(first)
            def _():
                self.keep(part, target, 0, self.column(part, target))

            @pl.when(jnp.logical_not(first))
            def _():
                self.along(part, target, kind).wait_recv()
                slot = target + 1 if kind == 3 else target
                self.keep(part, target, 0, self.column(part, target, self.land(3, part, slot)))

            self.along(part, target, kind).start()

        pl.when(jnp.logical_and(step >= level, self.has_up()))(lambda: go(last - step + level, 3, level == 0))
        pl.when(jnp.logical_and(step >= last - level, self.has_down()))(
            lambda: go(level - last + step, 4, level == last)
        )

    def last(self, part, out):
        level = self.level
        self.ready(part, level)
        out[...] = self.column(part, level)

        @pl.when(self.has_down())
        def _():
            self.along(part, level, 3).wait_recv()
            out[...] += self.land(3, part, level + 1)[...].astype(jnp.float32)

        @pl.when(self.has_up())
        def _():
            self.along(part, level, 4).wait_recv()
            out[...] += self.land(3, part, level)[...].astype(jnp.float32)

    def sent(self, part):
        self.all_sent(part, 4 * self.levels, self.sum_core_send.at[part])
        for kind in (1, 2):
            routed = self.route(part) == kind - 1
            self.all_sent(part, self.levels * (1 + routed), self.sum_plane_send.at[part, kind - 1])

        def body(at):
            pl.when(at > self.level)(lambda: self.along(part, at, 3).wait_send())
            pl.when(at < self.level)(lambda: self.along(part, at, 4).wait_send())

        fori(self.levels, body)


LATE = (5,)
ROUTES = (0, 1, 0, 1, 0, 0, 1)
PARTS = 7
GROUP_LAG = 2

GATHER_ROUTES = (1, 0, 1, 1, 0, 1, 1)


class Given(NamedTuple):
    start: Any
    length: Any
    tokens: Any
    cot_in: Any
    query_in: Any
    key_in: Any
    value_in: Any
    output_in: Any
    inner_in: Any
    outer_in: Any
    query_bias: Any
    value_bias: Any
    output_bias: Any
    first_gain: Any
    first_shift: Any
    outer_bias: Any
    second_gain: Any
    second_shift: Any
    inner_bias_in: Any
    read_in: Any
    write_in: Any


class Made(NamedTuple):
    layer_out: Any
    input_out: Any
    narrow_out: Any
    outer_out: Any
    small_out: Any
    spill: Any


class Room(NamedTuple):
    cot: Any
    mask: Any
    vectors: Any
    inner_bias: Any
    small: Any
    inner_bias_grad: Any
    pair_out: Any
    pair_in: Any
    narrow: Any
    narrow_in: Any
    small_all: Any
    small_rows: Any


class Signals(NamedTuple):
    core_send: Any
    core_recv: Any
    plane_send: Any
    line_send: Any
    late_send: Any
    gather_recv: Any
    sum_core_send: Any
    sum_core_recv: Any
    sum_plane_send: Any
    sum_plane_recv: Any
    sum_line_send: Any
    sum_line_recv: Any
    trade_sems: Any
    pair_sems: Any
    result_sems: Any
    local_sems: Any
    free_sem: Any


def spread(ref_rows, per, count):
    tiles = [None] * (per * count // LANES)
    lane = lax.broadcasted_iota(jnp.int32, (1, LANES), 1)
    for w in range(count):
        block = jnp.where(lane < per, ref_rows(w), 0.0)
        tile, shift = divmod(per * w, LANES)
        moved = pltpu.roll(block, shift, 1) if shift else block
        pieces = [(tile, jnp.where(lane >= shift, moved, 0.0) if shift else moved)]
        if shift + per > LANES:
            pieces.append((tile + 1, jnp.where(lane < shift + per - LANES, moved, 0.0)))
        for tile, piece in pieces:
            tiles[tile] = piece if tiles[tile] is None else tiles[tile] + piece
    return tiles


def picked(tile_of, per, w):
    lane = lax.broadcasted_iota(jnp.int32, (1, LANES), 1)
    tile, shift = divmod(per * w, LANES)
    block = tile_of(tile)
    if shift:
        block = pltpu.roll(block, LANES - shift, 1)
        if shift + per > LANES:
            block = jnp.where(lane < LANES - shift, block, pltpu.roll(tile_of(tile + 1), LANES - shift, 1))
    return jnp.where(lane < per, block, 0.0)


def whole_kernel(levels, *refs):
    left = list(refs)
    refs = {}
    for kind in (Given, Made, State, Room, Signals):
        refs.update(take(left, kind))
    refs.update(lands=[left[4 * i : 4 * i + 4] for i in range(PARTS - 2)])
    refs.update(own_out=refs.get(Made._fields[1]), small_grad=refs.get(Room._fields[10]))
    gather = Gather(levels, refs)
    scatter = Scatter(levels, refs)
    layer = Layer(gather.seq, refs)
    seq, level, side, core = gather.seq, gather.level, gather.side, gather.core
    width, half, keys, rows = layer.width, layer.half, layer.keys, layer.rows
    narrow = layer.narrow.shape[0]
    blocks = 8 * levels
    chip = gather.chip(0, level)
    tiles = layer.hidden // width
    barrier = pltpu.get_barrier_semaphore()
    gather.tell_all(barrier)

    for i, piece in enumerate((layer.query_in, layer.key_in, layer.value_in, layer.output_in)):
        layer.narrow[:, i * width : (i + 1) * width] = piece[...]
    layer.narrow[:, 4 * width :] = layer.inner_in[...]
    own_width = layer.query_bias.shape[1]
    layer.small_rows[...] = jnp.zeros_like(layer.small_rows)
    layer.small_rows[0:MEM, 0:own_width] = layer.read_in[...].astype(jnp.float32)
    layer.small_rows[MEM:LINE, 0:own_width] = layer.write_in[...].astype(jnp.float32)
    for i, piece in enumerate(
        (
            layer.query_bias,
            layer.value_bias,
            layer.output_bias,
            layer.first_gain,
            layer.first_shift,
            layer.outer_bias,
            layer.second_gain,
            layer.second_shift,
        )
    ):
        layer.small_rows[LINE + i : LINE + i + 1, 0:own_width] = piece[...].astype(jnp.float32)
    layer.small_rows[28:29, 0 : layer.inner_bias_in.shape[1]] = layer.inner_bias_in[...].astype(jnp.float32)
    layer.small_all[chip * 2 + core] = layer.small_rows[...].astype(jnp.bfloat16)
    own_outer = pltpu.make_async_copy(
        layer.outer_in,
        layer.w_outer.at[pl.ds(pl.multiple_of((chip * 2 + core) * gather.tall, 16), gather.tall), :],
        layer.local_sems.at[0],
    )
    own_outer.start()
    own_tokens = [
        pltpu.make_async_copy(
            layer.tokens.at[slot], layer.hid.at[pl.ds(slot * keys + half, half)], layer.local_sems.at[1 + slot]
        )
        for slot in range(layer.slots)
    ]
    cots = [
        pltpu.make_async_copy(layer.cot_in.at[slot], layer.cot.at[0], layer.local_sems.at[5 + slot])
        for slot in range(layer.slots)
    ]
    for copy in own_tokens:
        copy.start()
    cots[1].start()
    share_tokens = [
        gather.remote(
            layer.tokens.at[slot],
            layer.hid.at[pl.ds(slot * keys, half)],
            layer.pair_sems.at[0, slot],
            layer.pair_sems.at[1, slot],
            2,
        )
        for slot in range(layer.slots)
    ]
    pl.semaphore_wait(barrier, gather.neighbours())
    trade = [
        gather.remote(
            layer.narrow.at[:, pl.ds(pl.multiple_of((2 * i + 1 - core) * (2 * width), LANES), 2 * width)],
            layer.narrow_in.at[i],
            layer.trade_sems.at[0, i],
            layer.trade_sems.at[1, i],
            0,
        )
        for i in range(2)
    ]
    for copy in trade:
        copy.start()
    gather.own(6)
    own_outer.wait()
    first = core == 0
    for i, whole in enumerate((layer.w_attention, layer.w_inner)):
        trade[i].wait_recv()
        column = pl.multiple_of(core * (2 * width), LANES)
        mine = layer.narrow[:, pl.ds(pl.multiple_of((2 * i + core) * (2 * width), LANES), 2 * width)].astype(jnp.float32)
        other = layer.narrow_in[i].astype(jnp.float32)
        merged = jnp.concatenate([jnp.where(first, mine, other), jnp.where(first, other, mine)], axis=0)
        whole[pl.ds(pl.multiple_of(chip * gather.thick, 16), gather.thick), pl.ds(column, 2 * width)] = merged.astype(
            jnp.bfloat16
        )
        gather.own(2 * i)
        gather.own(2 * i + 1)
        if i == 0:
            share_tokens[0].start()
    gather.own(4)
    gather.own(5)
    for step in range(1, levels + 2):
        gather.step(6, step)

    lag = GROUP_LAG

    def turn(number):
        for group in range(3):
            for part in (2 * group, 2 * group + 1):
                if 1 <= number - lag * group <= levels + 1:
                    gather.step(part, number - lag * group)

    def have(*parts):
        for part in parts:
            gather.other_core(part)

    layer.small[...] = jnp.zeros_like(layer.small)
    layer.inner_bias_grad[...] = jnp.zeros_like(layer.inner_bias_grad)
    spot = lax.broadcasted_iota(jnp.int32, (1, keys), 1)
    position = jnp.where(
        spot < half,
        spot + (1 - seq) * half,
        jnp.where(spot < 2 * half, spot + (seq - 1) * half, jnp.where(spot < 2 * half + LINE, -1, 1 << 30)),
    )
    for slot in range(layer.slots):
        layer.mask[slot] = jnp.where(position < layer.length[slot], 0.0, NEG_FILL)

    have(6)
    vectors = spread(lambda w: layer.small_all[w].astype(jnp.float32), width // blocks, blocks)
    for i, tile in enumerate(vectors):
        layer.vectors[:, i * LANES : (i + 1) * LANES] = tile
    biases = spread(
        lambda w: layer.small_all[w].astype(jnp.float32)[28:29, :], layer.hidden // blocks, blocks
    )
    for i, tile in enumerate(biases):
        layer.inner_bias[:, i * LANES : (i + 1) * LANES] = tile
    layer.set_memory(0)

    spill = [
        pltpu.make_async_copy(layer.shares, layer.spill, layer.local_sems.at[3]),
        pltpu.make_async_copy(layer.spill, layer.shares, layer.local_sems.at[4]),
    ]

    def project():
        have(0, 1)
        own_tokens[0].wait()
        share_tokens[0].wait()
        layer.project_query(0)
        layer.project_key(0)
        layer.project_value(0)

    def attend(*pairs):
        return lambda: layer.attend(0, pairs)

    def inner(*tile_list):
        def body():
            for j in tile_list:
                layer.inner(0, j)

        return body

    work = {
        levels + 1: [project],
        levels + 2: [attend(0, 1, 2)],
        levels + 3: [attend(3, 4, 5), spill[0].start, lambda: layer.branch(0)],
    }
    for number in range(1, levels + 2 + 2 * lag):
        turn(number)
        for item in work.get(number, []):
            item()
    share_tokens[1].start()
    have(2, 3)
    fori(tiles, lambda j: layer.inner(0, j))
    have(4, 5)
    layer.outer(0)

    layer.set_memory(1)
    own_tokens[1].wait()
    share_tokens[1].wait()
    layer.project_query(1)
    layer.project_key(1)
    layer.project_value(1)
    spill[0].wait()
    layer.attend(1)
    layer.branch(1)
    fori(tiles, lambda j: layer.inner(1, j))
    layer.outer(1)
    for part in range(PARTS):
        gather.sent(part)
    for copy in trade:
        copy.wait_send()
    layer.memory[...] = jnp.zeros_like(layer.memory)

    def pair_copy(slot):
        return gather.remote(
            layer.pair_out.at[slot],
            layer.pair_in.at[slot],
            layer.pair_sems.at[2, slot],
            layer.pair_sems.at[3, slot],
            2,
        )

    cots[1].wait()
    layer.outer_back(1)
    cots[0].start()
    layer.inner_back(1)
    layer.mix_back(1)
    layer.attend_back(1)
    spill[1].start()
    passed = layer.input_back(1)
    layer.swap_out[...] = passed
    swap = gather.remote(layer.swap_out, layer.swap_in, layer.pair_sems.at[4, 0], layer.pair_sems.at[4, 1], 2)
    swap.start()
    swap.wait()
    pair_copy(1).start()
    summed = pltpu.roll(passed + layer.swap_in[...], MEM, 0)
    layer.memory[...] = jnp.where(seq == 0, summed, 0.0)
    cots[0].wait()
    layer.outer_back(0)
    layer.inner_back(0)

    def narrow_result(part):
        scatter.last(part, layer.work.at[pl.ds(part * 2 * narrow, 2 * narrow), :])
        column = pl.ds(pl.multiple_of((part // 2) * (4 * width) + core * (2 * width) + (part % 2) * width, LANES), width)
        layer.narrow_out[:, column] = layer.work[pl.ds(pl.multiple_of((2 * part + core) * narrow, 8), narrow), :]
        share_result(part).start()

    def share_result(part):
        column = pl.ds(pl.multiple_of((part // 2) * (4 * width) + core * (2 * width) + (part % 2) * width, LANES), width)
        return gather.remote(
            layer.work.at[pl.ds(pl.multiple_of((2 * part + 1 - core) * narrow, 8), narrow), :],
            layer.narrow_out.at[:, column],
            layer.result_sems.at[0, part],
            layer.result_sems.at[1, part],
            0,
        )

    def share_result_in(part):
        column = pl.ds(
            pl.multiple_of((part // 2) * (4 * width) + (1 - core) * (2 * width) + (part % 2) * width, LANES), width
        )
        return gather.remote(
            layer.work.at[pl.ds(pl.multiple_of((2 * part + 1 - core) * narrow, 8), narrow), :],
            layer.narrow_out.at[:, column],
            layer.result_sems.at[0, part],
            layer.result_sems.at[1, part],
            0,
        )

    def outer_result(part):
        size = gather.tall // 2
        scatter.last(part, layer.outer_out.at[pl.ds((part - 4) * size, size), :])

    def both(function, *parts, **more):
        for part in parts:
            function(part, **more)

    def give_input(slot):
        pair_copy(slot).wait()
        total = layer.input_out[slot].astype(jnp.float32) + layer.pair_in[slot].astype(jnp.float32)
        layer.input_out[slot] = total.astype(jnp.bfloat16)

    fori(tiles, layer.outer_weight_grad)
    both(scatter.start_core, 4, 5)
    layer.inner_weight_grad(0)
    layer.inner_weight_grad(1)
    both(scatter.corner, 4, 5)
    layer.inner_weight_grad(2)
    layer.inner_weight_grad(3)
    scatter.tell_all(layer.free_sem)
    both(scatter.start_core, 2, 3)
    both(scatter.plane, 4, 5)
    layer.mix_back(0)
    spill[1].wait()
    layer.attend_back(0, (0, 1))
    both(scatter.corner, 2, 3)
    both(scatter.line, 4, 5, step=0)
    layer.attend_back(0, (2, 3))
    both(scatter.plane, 2, 3)
    both(scatter.line, 4, 5, step=1)
    layer.attend_back(0, (4, 5))
    both(scatter.line, 4, 5, step=2)
    layer.input_back(0)
    pair_copy(0).start()
    both(scatter.line, 2, 3, step=0)
    layer.output_weight_grad()
    layer.value_weight_grad()
    both(scatter.line, 2, 3, step=1)
    layer.query_weight_grad()
    layer.key_weight_grad()
    pl.semaphore_wait(layer.free_sem, scatter.neighbours())
    both(scatter.start_core, 0, 1)
    small_tile = lambda i: layer.small[:, i * LANES : (i + 1) * LANES]
    inner_tile = lambda i: layer.inner_bias_grad[:, i * LANES : (i + 1) * LANES]
    small_row = lax.broadcasted_iota(jnp.int32, (32, 1), 0)
    for w in range(blocks):
        vectors_part = picked(small_tile, width // blocks, w)
        bias_part = picked(inner_tile, layer.hidden // blocks, w)
        layer.small_grad[w] = jnp.where(small_row == 28, bias_part, vectors_part).astype(jnp.bfloat16)
    scatter.start_core(6)
    both(outer_result, 4, 5)
    both(scatter.line, 2, 3, step=2)
    both(scatter.corner, 0, 1, 6)
    give_input(1)
    both(narrow_result, 2, 3)
    both(scatter.plane, 0, 1, 6)
    give_input(0)
    for step in range(levels - 1):
        both(scatter.line, 0, 1, 6, step=step)
    both(narrow_result, 0, 1)
    scatter.last(6, layer.small_out)
    for part in range(4):
        share_result_in(part).wait_recv()
        share_result(part).wait_send()
    for part in range(PARTS):
        scatter.sent(part)


def whole_layer(levels, start, length, tokens, cotangent, weights, vectors, inner_bias, read_init, write_init):
    slots, half, width = tokens.shape
    query_in, outer_in, inner_in = weights[0], weights[5], weights[4]
    hidden = inner_in.shape[1]
    narrow, tall = query_in.shape[0], outer_in.shape[0]
    blocks = 8 * levels
    bf16, f32 = jnp.bfloat16, jnp.float32
    inside = pl.BlockSpec(memory_space=pltpu.VMEM)
    scalars = pl.BlockSpec(memory_space=pltpu.SMEM)
    anywhere = pl.BlockSpec(memory_space=pl.ANY)
    shape = jax.ShapeDtypeStruct
    dma = pltpu.SemaphoreType.DMA
    state = state_shapes(slots, half, width, hidden)
    shares = (width // LANES,) + state.shares[0][1:]
    state = state._replace(shares=(shares, bf16))
    room = Room(
        cot=((1, half, width), bf16),
        mask=((slots, 1, 2 * half + MEMORY), f32),
        vectors=((32, width), f32),
        inner_bias=((1, hidden), f32),
        small=((32, width), f32),
        inner_bias_grad=((1, hidden), f32),
        pair_out=((slots, half, width), bf16),
        pair_in=((slots, half, width), bf16),
        narrow=((narrow, 8 * width), bf16),
        narrow_in=((2, narrow, 2 * width), bf16),
        small_all=((blocks, 32, LANES), bf16),
        small_rows=((32, LANES), f32),
    )
    signals = Signals(
        core_send=dma((PARTS,)),
        core_recv=dma((PARTS,)),
        plane_send=dma((PARTS, 2)),
        line_send=dma((PARTS, levels + 1)),
        late_send=dma((len(LATE), 4, levels + 1)),
        gather_recv=dma((PARTS, 4 * levels)),
        sum_core_send=dma((PARTS,)),
        sum_core_recv=dma((PARTS,)),
        sum_plane_send=dma((PARTS, 2)),
        sum_plane_recv=dma((PARTS, 3 * levels)),
        sum_line_send=dma((PARTS, levels)),
        sum_line_recv=dma((PARTS, levels + 1)),
        trade_sems=dma((2, 2)),
        pair_sems=dma((5, 2)),
        result_sems=dma((2, 4)),
        local_sems=dma((7,)),
        free_sem=pltpu.SemaphoreType.REGULAR,
    )
    lands = []
    for part in range(2, PARTS):
        size = (2 * narrow, width) if part < 4 else (tall // 2, width) if part < 6 else (32, LANES)
        side = 2 * levels if ROUTES[part] == 0 else levels
        lands += [pltpu.VMEM((count,) + size, bf16) for count in (4 * levels, side, 3 * levels - side, levels + 1)]
    return pl.pallas_call(
        functools.partial(whole_kernel, levels),
        out_shape=[
            shape((slots, half, width), bf16),
            shape((slots, half, width), bf16),
            shape((narrow, 8 * width), f32),
            shape((tall, width), f32),
            shape((32, LANES), f32),
            shape(shares, bf16),
        ],
        in_specs=[scalars] * 2 + [anywhere] * 2 + [inside] * 5 + [anywhere] + [inside] * 11,
        out_specs=[inside] * 5 + [anywhere],
        scratch_shapes=[pltpu.VMEM(*s) for s in state + room] + list(signals) + lands,
        compiler_params=pltpu.CompilerParams(
            collective_id=0, has_side_effects=True, vmem_limit_bytes=63 * 2**20
        ),
        cost_estimate=pl.CostEstimate(flops=31 * 10**9, bytes_accessed=10 * 10**6, transcendentals=10**7),
        name="whole_layer",
    )(start, length, tokens, cotangent, *weights, *(v[None] for v in vectors), inner_bias[None], read_init, write_init)


def hand_out_kernel(layer_ref, input_ref, narrow_ref, outer_ref, small_ref, *out_refs):
    width = outer_ref.shape[1]
    out_refs[0][...] = layer_ref[...]
    out_refs[1][...] = input_ref[...]
    for i in range(4):
        out_refs[2 + i][...] = narrow_ref[:, i * width : (i + 1) * width]
    out_refs[6][...] = narrow_ref[:, 4 * width :]
    out_refs[7][...] = outer_ref[...]
    for i in range(8):
        out_refs[8 + i][...] = small_ref[LINE + i : LINE + i + 1, 0 : out_refs[8 + i].shape[1]]
    out_refs[16][...] = small_ref[28:29, 0 : out_refs[16].shape[1]]
    out_refs[17][...] = small_ref[0:MEM, 0 : out_refs[17].shape[1]]
    out_refs[18][...] = small_ref[MEM:LINE, 0 : out_refs[18].shape[1]]


def hand_out(results, narrow, inner_width):
    layer_out, input_out, narrow_out, outer_out, small_out = results
    width = outer_out.shape[1]
    shape = jax.ShapeDtypeStruct
    f32 = jnp.float32
    inside = pl.BlockSpec(memory_space=pltpu.VMEM)
    return pl.pallas_call(
        hand_out_kernel,
        out_shape=[shape(layer_out.shape, layer_out.dtype), shape(input_out.shape, input_out.dtype)]
        + [shape((narrow, width), f32)] * 4
        + [shape((narrow, narrow_out.shape[1] - 4 * width), f32), shape(outer_out.shape, f32)]
        + [shape((1, narrow), f32)] * 8
        + [shape((1, inner_width), f32)]
        + [shape((MEM, narrow), f32)] * 2,
        in_specs=[inside] * 5,
        out_specs=[inside] * 19,
        compiler_params=pltpu.CompilerParams(vmem_limit_bytes=32 * 2**20),
    )(layer_out, input_out, narrow_out, outer_out, small_out)


def small_block(vectors, inner_bias, read_init, write_init):
    width = vectors[0].shape[0]
    inner_width = inner_bias.shape[0]
    rows = jnp.concatenate([read_init, write_init] + [v[None] for v in vectors], axis=0)
    rows = jnp.pad(rows, ((0, 4), (0, 128 - width)))
    return rows + jnp.pad(inner_bias[None], ((28, 3), (0, 128 - inner_width)))


def apart(tokens, cotangent, start, length, weights, small, blocks):
    half, model_width = tokens.shape[1:]
    width, inner_width = weights[0].shape[0], weights[5].shape[0]
    axes = AXES
    pair = [(0, 1), (1, 0)]
    others = lax.ppermute(tokens, AXES[0], pair)
    whole = [lax.all_gather(w, axes, axis=0, tiled=True) for w in weights]
    small_all = lax.all_gather(small, axes, axis=0)
    vectors = small_all[:, :, :width].transpose(1, 0, 2).reshape(32, model_width).astype(jnp.float32)
    bias_inner = small_all[:, 28, :inner_width].reshape(1, -1).astype(jnp.float32)
    mine = lax.axis_index(AXES[0])
    place_in = jnp.arange(half)
    position = jnp.concatenate(
        [
            (1 - mine) * half + place_in,
            mine * half + place_in,
            jnp.where(jnp.arange(MEMORY) < LINE, -1, 1 << 30),
        ]
    )
    mask = jnp.where(position[None, :] < length[:, None], 0.0, NEG_FILL)[:, None, :]
    results = middle(start, mask, tokens, others, cotangent, vectors, bias_inner, whole)
    received = lax.ppermute(results[2], AXES[0], pair)
    input_grad = (results[1] + received.astype(jnp.float32)).astype(jnp.bfloat16)
    small_grads = jnp.pad(
        results[3].reshape(32, blocks, width).transpose(1, 0, 2), ((0, 0), (0, 0), (0, 128 - width))
    )
    inner_rows = jnp.pad(results[4].reshape(blocks, 1, inner_width), ((0, 0), (28, 3), (0, 128 - inner_width)))
    small_grads = jnp.where(jnp.arange(32)[None, :, None] == 28, inner_rows, small_grads).astype(jnp.bfloat16)

    def summed(grad):
        paired = lax.psum_scatter(grad, AXES[0], scatter_dimension=0, tiled=True).astype(jnp.float32)
        return lax.psum_scatter(paired, AXES[1], scatter_dimension=0, tiled=True)

    small_sum = summed(small_grads.reshape(-1, 128))
    return results[0], input_grad, [summed(g) for g in results[5:]], small_sum


def shards(
    tokens,
    cotangent,
    chain_start,
    seg_len,
    query_weight,
    key_weight,
    value_weight,
    output_weight,
    query_bias,
    value_bias,
    output_bias,
    first_gain,
    first_shift,
    inner_weight,
    inner_bias,
    outer_weight,
    outer_bias,
    second_gain,
    second_shift,
    read_init,
    write_init,
):
    width = query_bias.shape[0]
    levels = lax.axis_size(AXES[1]) // 4
    blocks = 8 * levels
    weights = (query_weight, key_weight, value_weight, output_weight, inner_weight, outer_weight)
    vectors = (
        query_bias,
        value_bias,
        output_bias,
        first_gain,
        first_shift,
        outer_bias,
        second_gain,
        second_shift,
    )
    inner_width = inner_bias.shape[0]
    if width % 8 == 0:
        results = whole_layer(
            levels,
            chain_start[0],
            seg_len[0],
            tokens[0],
            cotangent[0],
            weights,
            vectors,
            inner_bias,
            read_init,
            write_init,
        )
        results = hand_out(results[:5], width, inner_width)
        layer_out, input_grad = results[:2]
        sums = results[2:8]
        vector = [v[0] for v in results[8:16]]
        inner_sum, read_sum, write_sum = results[16][0], results[17], results[18]
    else:
        small = small_block(vectors, inner_bias, read_init, write_init)
        layer_out, input_grad, sums, small_sum = apart(
            tokens[0], cotangent[0], chain_start[0], seg_len[0], weights, small, blocks
        )
        vector = [small_sum[LINE + i, :width] for i in range(8)]
        inner_sum = small_sum[28, :inner_width]
        read_sum, write_sum = small_sum[:MEM, :width], small_sum[MEM:LINE, :width]
    return (
        layer_out[None],
        input_grad[None],
        *sums[:4],
        *vector[:5],
        sums[4],
        inner_sum,
        sums[5],
        *vector[5:],
        read_sum,
        write_sum,
    )


def solution(mesh):
    rows = P(AXES[1], None, AXES[0], None)
    scalars = P(AXES[1], None)
    matrix, vector, memory = P(AXES, None), P(AXES), P(None, AXES)
    weights = (
        (matrix,) * 4
        + (vector,) * 5
        + (matrix, vector, matrix)
        + (vector,) * 3
        + (memory,) * 2
    )
    return jax.shard_map(
        shards,
        mesh=mesh,
        in_specs=(rows, rows, scalars, scalars) + weights,
        out_specs=(rows, rows) + weights,
        check_vma=False,
    )
```

```python
import functools
import math
from typing import Any, NamedTuple

import jax
import jax.numpy as jnp
from jax import lax
from jax.experimental import pallas as pl
from jax.experimental.pallas import tpu as pltpu
from jax.sharding import PartitionSpec as P

HEADS = 12
MEM = 10
EPS = 1e-12
INV_ROOT_TWO = 1.0 / math.sqrt(2.0)
INV_ROOT_TWO_PI = 1.0 / math.sqrt(2.0 * math.pi)
NEG_FILL = -1000000000.0

AXES = ("seq", "chain")


MESH = pl.DeviceIdType.MESH


def place():
    seq = lax.axis_index(AXES[0])
    chain = lax.axis_index(AXES[1])
    return seq, chain // 4, lax.rem(chain // 2, 2), lax.rem(chain, 2)


def block_of(levels, seq, level, side, core):
    return seq * (4 * levels) + level * 4 + side * 2 + core


def device_of(seq, level, side, core):
    return (seq, level * 4 + side * 2 + core)


def fori(count, body):
    def step(index, carry):
        body(index)
        return carry

    lax.fori_loop(0, count, step, 0)


def span(index, size):
    return pl.ds(pl.multiple_of(index * size, size), size)


def dot_nn(former, latter):
    return jnp.dot(former, latter, preferred_element_type=jnp.float32)


def dot_nt(former, latter):
    return lax.dot_general(former, latter, (((1,), (1,)), ((), ())), preferred_element_type=jnp.float32)


def dot_tn(former, latter):
    return lax.dot_general(former, latter, (((0,), (0,)), ((), ())), preferred_element_type=jnp.float32)


def fold(rows):
    return jnp.sum(rows.reshape(rows.shape[0] // 8, 8, rows.shape[1]), axis=0)


CHUNK = 48
MEMORY = 32
LANES = 128
LINE = 2 * MEM


class Layer:
    def __init__(self, seq, refs):
        self.seq = seq
        self.__dict__.update(refs)
        self.slots = self.layer_out.shape[0]
        self.half, self.width = self.layer_out.shape[1:]
        self.rows = self.half + MEMORY
        self.keys = self.rows + self.half
        self.hidden = self.w_inner.shape[1]
        self.pairs = self.width // LANES
        self.scale = 1.0 / math.sqrt(self.width // HEADS)
        lane = lax.broadcasted_iota(jnp.int32, (1, LANES), 1)
        self.low = lane < LANES // 2
        self.low_f = jnp.where(self.low, 1.0, 0.0)
        self.low_b = self.low_f.astype(jnp.bfloat16)
        self.high_f = 1.0 - self.low_f
        self.high_b = self.high_f.astype(jnp.bfloat16)
        self.mem_row = lax.broadcasted_iota(jnp.int32, (MEMORY, 1), 0)

    def vec(self, at):
        return self.vectors[LINE + at : LINE + at + 1, :]

    def slot_rows(self, slot):
        return pl.ds(slot * self.rows, self.rows)

    def slot_keys(self, slot):
        return pl.ds(slot * self.keys, self.keys)

    def slot_queries(self, slot):
        return pl.ds(slot * self.keys + self.half, self.rows)

    def weight(self, at):
        return self.w_attention.at[:, pl.ds(at * self.width, self.width)]

    def pair_room(self, slot):
        if self.pair_out is not None:
            return self.pair_out.at[slot]
        return (self.key if slot else self.value).at[pl.ds(self.keys, self.half)]

    def set_memory(self, slot):
        initial = jnp.where(self.mem_row < LINE, self.vectors[0:MEMORY, :], 0.0)
        if slot > 0:
            second = self.work[self.half : self.rows].astype(jnp.bfloat16).astype(jnp.float32)
            carried = pltpu.roll(second, MEMORY - MEM, 0)
        else:
            carried = jnp.zeros_like(initial)
        restart = self.start[slot] == 1
        initial = jnp.where(jnp.logical_or(self.mem_row >= MEM, restart), initial, carried)
        base = slot * self.keys + 2 * self.half
        self.hid[base : base + MEMORY] = initial.astype(jnp.bfloat16)

    def project_query(self, slot):
        out = dot_nn(self.hid[self.slot_queries(slot)], self.weight(0)[...]) + self.vec(0)
        self.query[self.slot_rows(slot)] = out.astype(jnp.bfloat16)

    def project_key(self, slot):
        self.key[self.slot_keys(slot)] = dot_nn(self.hid[self.slot_keys(slot)], self.weight(1)[...]).astype(
            jnp.bfloat16
        )

    def project_value(self, slot):
        out = dot_nn(self.hid[self.slot_keys(slot)], self.weight(2)[...]) + self.vec(1)
        self.value[self.slot_keys(slot)] = out.astype(jnp.bfloat16)

    def share_at(self, slot, p):
        return p if self.shares.shape[0] == self.pairs else slot * self.pairs + p

    def attend(self, slot, pairs=None):
        valid = self.mask[slot]
        low_scaled = (self.low_f * self.scale).astype(jnp.bfloat16)
        high_scaled = (self.high_f * self.scale).astype(jnp.bfloat16)
        rows = self.rows
        for p in pairs or range(self.pairs):
            here = pl.ds(p * LANES, LANES)
            query_pair = self.query[self.slot_rows(slot), here]
            key_pair = self.key[self.slot_keys(slot), here]
            value_pair = self.value[self.slot_keys(slot), here]
            stacked = jnp.concatenate([query_pair * low_scaled, query_pair * high_scaled], axis=0)
            scores = dot_nt(stacked, key_pair) + valid
            raised = jnp.exp(scores - jnp.max(scores, axis=1, keepdims=True)).astype(jnp.bfloat16)
            self.shares[self.share_at(slot, p)] = raised
            ones = jnp.ones((self.keys, LANES), jnp.bfloat16)
            summed = dot_nn(raised, jnp.concatenate([value_pair, ones], axis=1))
            inverse = 1.0 / summed[:, LANES:]
            out = summed[:, :LANES] * inverse
            self.inverse_total[self.slot_rows(slot), here] = jnp.where(self.low, inverse[:rows], inverse[rows:])
            self.mixed[self.slot_rows(slot), here] = jnp.where(self.low, out[:rows], out[rows:]).astype(jnp.bfloat16)

    def norm(self, slot, normed, inverse, gain_at, shift_at, rounded=None):
        for r in range(self.rows // CHUNK):
            here = pl.ds(r * CHUNK, CHUNK)
            there = pl.ds(slot * self.rows + r * CHUNK, CHUNK)
            z = self.work[here, :]
            centred = z - jnp.mean(z, axis=1, keepdims=True)
            inv = lax.rsqrt(jnp.mean(centred * centred, axis=1, keepdims=True) + EPS)
            unit = centred * inv
            normed[there] = unit.astype(jnp.bfloat16)
            self.inverse[there, inverse : inverse + 1] = inv
            out = unit * self.vec(gain_at) + self.vec(shift_at)
            self.work[here, :] = out
            if rounded is not None:
                rounded[there] = out.astype(jnp.bfloat16)

    def branch(self, slot):
        out = dot_nn(self.mixed[self.slot_rows(slot)], self.weight(3)[...]) + self.vec(2)
        self.work[...] = out + self.hid[self.slot_queries(slot)].astype(jnp.float32)
        self.norm(slot, self.normed_one, 0, 3, 4, self.first_b)

    def inner(self, slot, j):
        here = span(j, self.width)
        u = dot_nn(self.first_b[self.slot_rows(slot)], self.w_inner[:, here]) + self.inner_bias[:, here]
        cumulative = 0.5 * (1.0 + lax.erf(u * INV_ROOT_TWO))
        density = jnp.exp(-0.5 * u * u) * INV_ROOT_TWO_PI
        self.active[self.slot_rows(slot), here] = (u * cumulative).astype(jnp.bfloat16)
        self.slope[self.slot_rows(slot), here] = (cumulative + u * density).astype(jnp.bfloat16)

    def outer(self, slot):
        self.work[...] += dot_nn(self.active[self.slot_rows(slot)], self.w_outer[...]) + self.vec(5)
        self.norm(slot, self.normed_two, 1, 6, 7)
        self.layer_out[slot] = self.work[0 : self.half].astype(jnp.bfloat16)

    def add_small(self, at, folded):
        self.small[LINE + at : LINE + at + 1, :] += jnp.sum(folded, axis=0, keepdims=True)

    def norm_back(self, slot, normed, inverse, gain_at, shift_at, bias_at, rounded):
        zero = jnp.zeros((8, self.width), jnp.float32)
        gain_sum, shift_sum, bias_sum = zero, zero, zero
        for r in range(self.rows // CHUNK):
            here = pl.ds(r * CHUNK, CHUNK)
            there = pl.ds(slot * self.rows + r * CHUNK, CHUNK)
            grad = self.work[here, :]
            unit = normed[there].astype(jnp.float32)
            gain_sum = gain_sum + fold(grad * unit)
            shift_sum = shift_sum + fold(grad)
            scaled = grad * self.vec(gain_at)
            dz = self.inverse[there, inverse : inverse + 1] * (
                scaled
                - jnp.mean(scaled, axis=1, keepdims=True)
                - unit * jnp.mean(scaled * unit, axis=1, keepdims=True)
            )
            self.work[here, :] = dz
            dz_b = dz.astype(jnp.bfloat16)
            rounded[there] = dz_b
            bias_sum = bias_sum + fold(dz_b.astype(jnp.float32))
        self.add_small(gain_at, gain_sum)
        self.add_small(shift_at, shift_sum)
        self.add_small(bias_at, bias_sum)

    def outer_back(self, slot):
        self.work[0 : self.half] = self.cot[slot if self.cot.shape[0] > 1 else 0].astype(jnp.float32)
        self.work[self.half : self.rows] = self.memory[...]
        self.norm_back(slot, self.normed_two, 1, 6, 7, 5, self.grad_two_b)

        def tile(j):
            here = span(j, self.width)
            rows = self.slot_rows(slot)
            grad = dot_nt(self.grad_two_b[rows], self.w_outer[here, :]) * self.slope[rows, here].astype(jnp.float32)
            grad_b = grad.astype(jnp.bfloat16)
            self.slope[rows, here] = grad_b
            self.inner_bias_grad[:, here] += jnp.sum(fold(grad_b.astype(jnp.float32)), axis=0, keepdims=True)

        fori(self.hidden // self.width, tile)

    def inner_back(self, slot):
        self.work[...] += dot_nt(self.slope[self.slot_rows(slot)], self.w_inner[...])
        self.norm_back(slot, self.normed_one, 0, 3, 4, 2, self.grad_one_b)

    def mix_back(self, slot):
        grad = dot_nt(self.grad_one_b[self.slot_rows(slot)], self.weight(3)[...])
        self.grad_mixed[...] = grad.astype(jnp.bfloat16)

    def attend_back(self, slot, pairs=None):
        rows = self.rows
        own = self.slot_rows(slot)
        every = self.slot_keys(slot)

        def pair(p):
            here = pl.ds(p * LANES, LANES)
            query_pair = self.query[own, here]
            key_pair = self.key[every, here]
            value_pair = self.value[every, here]
            grad = self.grad_mixed[:, here].astype(jnp.float32) * self.inverse_total[own, here]
            product = grad * self.mixed[own, here].astype(jnp.float32)
            delta = jnp.concatenate(
                [
                    jnp.sum(product * self.low_f, axis=1, keepdims=True),
                    jnp.sum(product * self.high_f, axis=1, keepdims=True),
                ],
                axis=0,
            )
            grad_b = grad.astype(jnp.bfloat16)
            stacked = jnp.concatenate([grad_b * self.low_b, grad_b * self.high_b], axis=0)
            raised = self.shares[self.share_at(slot, p)]
            grad_scores = (raised.astype(jnp.float32) * (dot_nt(stacked, value_pair) - delta)).astype(jnp.bfloat16)
            both = dot_nn(grad_scores, key_pair)
            query_b = (jnp.where(self.low, both[:rows], both[rows:]) * self.scale).astype(jnp.bfloat16)
            queries = jnp.concatenate([query_pair * self.low_b, query_pair * self.high_b], axis=0)
            value_b = dot_tn(stacked, raised).T.astype(jnp.bfloat16)
            self.grad_query[own, here] = query_b
            self.grad_key[every, here] = (dot_tn(queries, grad_scores) * self.scale).T.astype(jnp.bfloat16)
            self.grad_value[every, here] = value_b
            self.small[LINE : LINE + 1, here] += jnp.sum(fold(query_b.astype(jnp.float32)), axis=0, keepdims=True)
            self.small[LINE + 1 : LINE + 2, here] += jnp.sum(fold(value_b.astype(jnp.float32)), axis=0, keepdims=True)

        for p in pairs or range(self.pairs):
            pair(p)

    def input_back(self, slot):
        every = self.slot_keys(slot)
        half = self.half
        grads = dot_nt(self.grad_key[every], self.weight(1)[...]) + dot_nt(self.grad_value[every], self.weight(2)[...])
        self.pair_room(slot)[...] = grads[0:half].astype(jnp.bfloat16)
        mine = grads[half:] + dot_nt(self.grad_query[self.slot_rows(slot)], self.weight(0)[...]) + self.work[...]
        self.own_out[slot] = mine[0:half].astype(self.own_out.dtype)
        memory = mine[half:]
        restart = self.start[slot] == 1
        counted = jnp.logical_or(
            jnp.logical_and(self.mem_row < MEM, restart),
            jnp.logical_and(self.mem_row >= MEM, self.mem_row < LINE),
        )
        self.small[0:MEMORY, :] += jnp.where(counted, memory, 0.0)
        return jnp.where(jnp.logical_and(self.mem_row < MEM, jnp.logical_not(restart)), memory, 0.0)

    def outer_weight_grad(self, j):
        here = span(j, self.width)
        self.w_outer[here, :] = dot_tn(self.active[:, here], self.grad_two_b[...]).astype(jnp.bfloat16)

    def inner_weight_grad(self, j):
        here = span(j, self.width)
        self.w_inner[:, here] = dot_tn(self.first_b[...], self.slope[:, here]).astype(jnp.bfloat16)

    def output_weight_grad(self):
        self.weight(3)[...] = dot_tn(self.mixed[...], self.grad_one_b[...]).astype(jnp.bfloat16)

    def query_weight_grad(self):
        total = None
        for slot in range(self.slots):
            term = dot_tn(self.hid[self.slot_queries(slot)], self.grad_query[self.slot_rows(slot)])
            total = term if total is None else total + term
        self.weight(0)[...] = total.astype(jnp.bfloat16)

    def key_weight_grad(self):
        self.weight(1)[...] = dot_tn(self.hid[...], self.grad_key[...]).astype(jnp.bfloat16)

    def value_weight_grad(self):
        self.weight(2)[...] = dot_tn(self.hid[...], self.grad_value[...]).astype(jnp.bfloat16)


class State(NamedTuple):
    w_attention: Any
    w_inner: Any
    w_outer: Any
    hid: Any
    query: Any
    key: Any
    value: Any
    shares: Any
    inverse_total: Any
    mixed: Any
    normed_one: Any
    normed_two: Any
    inverse: Any
    first_b: Any
    slope: Any
    active: Any
    grad_two_b: Any
    grad_one_b: Any
    grad_mixed: Any
    grad_query: Any
    grad_key: Any
    grad_value: Any
    work: Any
    memory: Any
    swap_out: Any
    swap_in: Any


def state_shapes(slots, half, width, hidden):
    rows, keys = half + MEMORY, 2 * half + MEMORY
    bf16, f32 = jnp.bfloat16, jnp.float32
    pairs = width // LANES
    by_row, by_key = ((slots * rows, width), bf16), ((slots * keys, width), bf16)
    return State(
        w_attention=((width, 4 * width), bf16),
        w_inner=((width, hidden), bf16),
        w_outer=((hidden, width), bf16),
        hid=by_key,
        query=by_row,
        key=by_key,
        value=by_key,
        shares=((slots * pairs, 2 * rows, keys), bf16),
        inverse_total=((slots * rows, width), f32),
        mixed=by_row,
        normed_one=by_row,
        normed_two=by_row,
        inverse=((slots * rows, 2), f32),
        first_b=by_row,
        slope=((slots * rows, hidden), bf16),
        active=((slots * rows, hidden), bf16),
        grad_two_b=by_row,
        grad_one_b=by_row,
        grad_mixed=((rows, width), bf16),
        grad_query=by_row,
        grad_key=by_key,
        grad_value=by_key,
        work=((rows, width), f32),
        memory=((MEMORY, width), f32),
        swap_out=((MEMORY, width), f32),
        swap_in=((MEMORY, width), f32),
    )


class Inputs(NamedTuple):
    start: Any
    mask: Any
    tokens: Any
    others: Any
    cot: Any
    vectors: Any
    inner_bias: Any


class Outputs(NamedTuple):
    layer_out: Any
    own_out: Any
    pair_out: Any
    small: Any
    inner_bias_grad: Any


def take(refs, kind):
    return kind(*(refs.pop(0) for _ in kind._fields))._asdict()


def middle_kernel(*refs):
    refs = list(refs)
    given = take(refs, Inputs)
    weights = [refs.pop(0) for _ in range(6)]
    given.update(take(refs, Outputs))
    grads = [refs.pop(0) for _ in range(6)]
    given.update(take(refs, State))
    load_sems, pair_sems = refs
    seq = lax.axis_index(AXES[0])
    chain = lax.axis_index(AXES[1])
    barrier = pltpu.get_barrier_semaphore()
    pl.semaphore_signal(barrier, inc=1, device_id=(1 - seq, chain), device_id_type=MESH)
    layer = Layer(seq, given)
    places = [layer.weight(i) for i in range(4)] + [layer.w_inner, layer.w_outer]
    loads = [pltpu.make_async_copy(weights[i], places[i], load_sems.at[i]) for i in range(6)]
    stores = [pltpu.make_async_copy(places[i], grads[i], load_sems.at[i]) for i in range(6)]
    for load in loads:
        load.start()
    layer.small[...] = jnp.zeros_like(layer.small)
    layer.inner_bias_grad[...] = jnp.zeros_like(layer.inner_bias_grad)
    for slot in range(layer.slots):
        def need(i):
            if slot == 0:
                loads[i].wait()
        base = slot * layer.keys
        layer.hid[base : base + layer.half] = layer.others[slot]
        layer.hid[base + layer.half : base + 2 * layer.half] = layer.tokens[slot]
        layer.set_memory(slot)
        need(0)
        layer.project_query(slot)
        need(1)
        layer.project_key(slot)
        need(2)
        layer.project_value(slot)
        layer.attend(slot)
        need(3)
        layer.branch(slot)
        need(4)
        fori(layer.hidden // layer.width, lambda j: layer.inner(slot, j))
        need(5)
        layer.outer(slot)
    layer.memory[...] = jnp.zeros_like(layer.memory)
    for slot in reversed(range(layer.slots)):
        layer.outer_back(slot)
        layer.inner_back(slot)
        if slot == 0:
            fori(layer.hidden // layer.width, layer.outer_weight_grad)
            stores[5].start()
            fori(layer.hidden // layer.width, layer.inner_weight_grad)
            stores[4].start()
        layer.mix_back(slot)
        layer.attend_back(slot)
        passed = layer.input_back(slot)
        if slot > 0:
            layer.swap_out[...] = passed
            pl.semaphore_wait(barrier, 1)
            swap = pltpu.make_async_remote_copy(
                src_ref=layer.swap_out,
                dst_ref=layer.swap_in,
                send_sem=pair_sems.at[0],
                recv_sem=pair_sems.at[1],
                device_id=(1 - seq, chain),
                device_id_type=MESH,
            )
            swap.start()
            swap.wait()
            summed = pltpu.roll(passed + layer.swap_in[...], MEM, 0)
            layer.memory[...] = jnp.where(seq == 0, summed, 0.0)
    layer.output_weight_grad()
    stores[3].start()
    layer.query_weight_grad()
    stores[0].start()
    layer.key_weight_grad()
    stores[1].start()
    layer.value_weight_grad()
    stores[2].start()
    for store in stores:
        store.wait()


def middle(start, mask, tokens, others, cotangent, vectors, inner_bias, weights):
    slots, half, width = tokens.shape
    hidden = inner_bias.shape[1]
    bf16, f32 = jnp.bfloat16, jnp.float32
    inside = pl.BlockSpec(memory_space=pltpu.VMEM)
    anywhere = pl.BlockSpec(memory_space=pl.ANY)
    shape = jax.ShapeDtypeStruct
    state = state_shapes(slots, half, width, hidden)
    return pl.pallas_call(
        middle_kernel,
        out_shape=[
            shape((slots, half, width), bf16),
            shape((slots, half, width), f32),
            shape((slots, half, width), bf16),
            shape((MEMORY, width), f32),
            shape((1, hidden), f32),
        ]
        + [shape(w.shape, bf16) for w in weights],
        in_specs=[pl.BlockSpec(memory_space=pltpu.SMEM)] + [inside] * 6 + [anywhere] * 6,
        out_specs=[inside] * 5 + [anywhere] * 6,
        scratch_shapes=[pltpu.VMEM(*s) for s in state]
        + [pltpu.SemaphoreType.DMA((6,)), pltpu.SemaphoreType.DMA((2,))],
        compiler_params=pltpu.CompilerParams(
            collective_id=2, has_side_effects=True, vmem_limit_bytes=62 * 2**20
        ),
        cost_estimate=pl.CostEstimate(flops=31 * 10**9, bytes_accessed=40 * 10**6, transcendentals=10**7),
    )(start, mask, tokens, others, cotangent, vectors, inner_bias, *weights)


class Links:
    def __init__(self, levels, refs):
        self.levels = levels
        self.seq, self.level, self.side, self.core = place()
        self.__dict__.update(refs)
        self.width = self.w_attention.shape[0]
        self.thick = self.width // (4 * levels)
        self.tall = self.w_outer.shape[0] // (8 * levels)

    def device(self, kind):
        seq, level, side, core = self.seq, self.level, self.side, self.core
        return device_of(
            *(
                (seq, level, side, 1 - core),
                (seq, level, 1 - side, core),
                (1 - seq, level, side, core),
                (seq, level + 1, side, core),
                (seq, level - 1, side, core),
            )[kind]
        )

    def chip(self, rel, at):
        seq = self.seq if rel < 2 else 1 - self.seq
        side = self.side if rel % 2 == 0 else 1 - self.side
        return seq * (2 * self.levels) + at * 2 + side

    def view(self, part, chip, core, small):
        if part < 4:
            whole = self.w_attention if part < 2 else self.w_inner
            column = pl.multiple_of(core * (2 * self.width) + (part % 2) * self.width, LANES)
            return whole.at[
                pl.ds(pl.multiple_of(chip * self.thick, 16), self.thick), pl.ds(column, self.width)
            ]
        if part < 6:
            size = self.tall // 2
            row = pl.multiple_of(chip * (2 * self.tall) + core * self.tall + (part - 4) * size, 16)
            return self.w_outer.at[pl.ds(row, size), :]
        return small.at[chip * 2 + core]

    def remote(self, source, target, send_sem, recv_sem, kind):
        return pltpu.make_async_remote_copy(
            src_ref=source,
            dst_ref=target,
            send_sem=send_sem,
            recv_sem=recv_sem,
            device_id=self.device(kind),
            device_id_type=MESH,
        )

    def amount(self, part, count):
        if part < 6:
            return self.w_outer.at[pl.ds(0, count * self.thick), :]
        return self.small_all.at[pl.ds(0, count)]

    def all_sent(self, part, count, semaphore):
        whole = self.amount(part, count)
        self.remote(whole, whole, semaphore, semaphore, 0).wait_send()

    def all_arrived(self, part, count, semaphore):
        whole = self.amount(part, count)
        self.remote(whole, whole, semaphore, semaphore, 0).wait_recv()

    def has_up(self):
        return self.level < self.levels - 1

    def has_down(self):
        return self.level > 0

    def neighbours(self):
        return 3 + self.has_up().astype(jnp.int32) + self.has_down().astype(jnp.int32)

    def tell_all(self, semaphore):
        for kind in range(3):
            pl.semaphore_signal(semaphore, inc=1, device_id=self.device(kind), device_id_type=MESH)

        @pl.when(self.has_up())
        def _():
            pl.semaphore_signal(semaphore, inc=1, device_id=self.device(3), device_id_type=MESH)

        @pl.when(self.has_down())
        def _():
            pl.semaphore_signal(semaphore, inc=1, device_id=self.device(4), device_id_type=MESH)


class Gather(Links):
    def copy(self, part, rel, at, kind):
        chip = self.chip(rel, at)
        here = self.view(part, chip, self.core, self.small_all)
        arrives = self.gather_recv.at[part, chip]
        if kind == 0:
            sends, arrives = self.core_send.at[part], self.core_recv.at[part]
        elif kind < 3:
            sends = self.plane_send.at[part, kind - 1]
        else:
            sends = self.line_send.at[part, 0 if rel == 0 else 1, at + (kind - 3)]
        return self.remote(here, here, sends, arrives, kind)

    def arrived(self, part, rel, at):
        self.copy(part, rel, at, 1).wait_recv()

    def up(self, part, rel, at):
        pl.when(self.has_up())(lambda: self.copy(part, rel, at, 3).start())

    def down(self, part, rel, at):
        pl.when(self.has_down())(lambda: self.copy(part, rel, at, 4).start())

    def own(self, part):
        self.up(part, 0, self.level)
        self.down(part, 0, self.level)
        for kind in (1, 2, 0):
            self.copy(part, 0, self.level, kind).start()

    def from_plane(self, part, at):
        self.arrived(part, 1, at)
        if LAST[part] == 2:
            self.copy(part, 1, at, 2).start()
        self.copy(part, 1, at, 0).start()
        self.arrived(part, 2, at)
        if LAST[part] == 1:
            self.copy(part, 2, at, 1).start()
        self.copy(part, 2, at, 0).start()

    def passed_on(self, part, rel, at):
        self.arrived(part, rel, at)
        self.copy(part, rel, at, 0).start()

    def around(self, distance, body):
        if not 0 <= distance < self.levels:
            return
        for sign in (-1, 1) if distance else (0,):
            at = self.level + sign * distance
            pl.when(jnp.logical_and(at >= 0, at < self.levels))(functools.partial(body, at, sign))

    def step(self, part, step):
        last = LAST[part]
        first = 3 - last

        def column(rel, kinds, at, sign):
            self.arrived(part, rel, at)
            if sign <= 0:
                self.up(part, rel, at)
            if sign >= 0:
                self.down(part, rel, at)
            for kind in kinds:
                self.copy(part, rel, at, kind).start()

        if part in STRAIGHT:
            if step:
                self.around(step, functools.partial(column, 0, (1, 2, 0)))
            self.around(step - 1, lambda at, sign: self.from_plane(part, at))
            self.around(step - 2, lambda at, sign: self.passed_on(part, 3, at))
            return
        self.around(step, functools.partial(column, 0, (last, 0)))
        self.around(step - 1, functools.partial(column, first, (last, 0)))
        self.around(step - 1, lambda at, sign: self.passed_on(part, last, at))
        self.around(step - 2, lambda at, sign: self.passed_on(part, 3, at))

    def other_core(self, part):
        self.all_arrived(part, 4 * self.levels, self.core_recv.at[part])

    def sent(self, part):
        self.all_sent(part, 4 * self.levels, self.core_send.at[part])
        straight = part in STRAIGHT
        for kind in (1, 2):
            count = self.levels if straight else 1
            if kind == LAST[part]:
                count = 2 * self.levels
            self.all_sent(part, count, self.plane_send.at[part, kind - 1])

        def body(at):
            for rel in (0,) if straight else (0, 3 - LAST[part]):
                pl.when(jnp.logical_and(at <= self.level, self.has_up()))(
                    lambda rel=rel: self.copy(part, rel, at, 3).wait_send()
                )
                pl.when(jnp.logical_and(at >= self.level, self.has_down()))(
                    lambda rel=rel: self.copy(part, rel, at, 4).wait_send()
                )

        fori(self.levels, body)


class Scatter(Links):
    def land(self, kind, part, slot):
        if part >= 2:
            return self.lands[part - 2][kind].at[slot]
        levels = self.levels
        at = slot + (0, 4 * levels, 6 * levels, 7 * levels)[kind]
        hold = self.active if part == 0 else self.slope
        per_row = hold.shape[1] // self.width
        row = pl.multiple_of((at // per_row) * self.thick, 16)
        column = pl.multiple_of(lax.rem(at, per_row) * self.width, LANES)
        return hold.at[pl.ds(row, self.thick), pl.ds(column, self.width)]

    def mine(self, part, rel, at, core=None):
        return self.view(part, self.chip(rel, at), self.core if core is None else core, self.small_grad)

    def over_core(self, part, at, rel):
        return self.remote(
            self.mine(part, rel, at, 1 - self.core),
            self.land(0, part, at * 4 + rel),
            self.sum_core_send.at[part],
            self.sum_core_recv.at[part],
            0,
        )

    def over_first(self, part, at, second):
        first = CROSS[part]
        slot = at + second * self.levels
        return self.remote(
            self.land(0, part, at * 4 + (3 if second else first)),
            self.land(1, part, slot),
            self.sum_plane_send.at[part, 0],
            self.sum_plane_recv.at[part, slot],
            first,
        )

    def over_last(self, part, at=None):
        last = 3 - CROSS[part]
        straight = part in SUM_STRAIGHT
        slot = at if straight else 0
        return self.remote(
            self.land(0, part, (at if straight else self.level) * 4 + last),
            self.land(2, part, slot),
            self.sum_plane_send.at[part, 1],
            self.sum_plane_recv.at[part, 2 * self.levels + slot],
            last,
        )

    def plane(self, part):
        if part not in SUM_STRAIGHT:
            return
        rel = 3 - CROSS[part]

        def body(i):
            at = lax.rem(self.level + 1 + i, self.levels)
            self.over_first(part, at, 1).wait_recv()
            self.keep(part, at, rel, self.total(part, at, rel, self.land(1, part, at + self.levels)))
            self.over_last(part, at).start()

        fori(self.levels, body)

    def along(self, part, target, second, kind):
        slot = target + 1 if kind == 3 else target
        rel = 3 - CROSS[part] if second else 0
        return self.remote(
            self.land(0, part, target * 4 + rel),
            self.land(3, part, slot + second * (self.levels + 1)),
            self.sum_line_send.at[part, second, target],
            self.sum_line_recv.at[part, second, slot],
            kind,
        )

    def total(self, part, at, rel, *more):
        value = self.mine(part, rel, at)[...].astype(jnp.float32)
        value = value + self.land(0, part, at * 4 + rel)[...].astype(jnp.float32)
        for ref in more:
            value = value + ref[...].astype(jnp.float32)
        return value

    def keep(self, part, at, rel, value):
        self.land(0, part, at * 4 + rel)[...] = value.astype(jnp.bfloat16)

    def start_core(self, part):
        for rel in (3, CROSS[part], 3 - CROSS[part], 0):
            fori(self.levels, lambda at: self.over_core(part, at, rel).start())

    def cross(self, part):
        self.all_arrived(part, 4 * self.levels, self.sum_core_recv.at[part])

        def body(i):
            at = lax.rem(self.level + 1 + i, self.levels)
            for second in (1, 0):
                rel = 3 if second else CROSS[part]
                self.keep(part, at, rel, self.total(part, at, rel))
                self.over_first(part, at, second).start()

        fori(self.levels, body)

    def column(self, part, at, second, *more):
        rel = 3 - CROSS[part] if second else 0
        if part in SUM_STRAIGHT:
            more += (self.land(2, part, at),)
        return self.total(part, at, rel, self.land(1, part, at + second * self.levels), *more)

    def ready(self, part, at, second):
        self.over_first(part, at, second).wait_recv()
        if part in SUM_STRAIGHT:
            self.over_last(part, at).wait_recv()

    def columns(self, part):
        return (0,) if part in SUM_STRAIGHT else (0, 1)

    def line(self, part, step):
        last = self.levels - 1
        level = self.level

        def go(target, kind, first):
            for second in self.columns(part):
                rel = 3 - CROSS[part] if second else 0
                self.ready(part, target, second)

                @pl.when(first)
                def _():
                    self.keep(part, target, rel, self.column(part, target, second))

                @pl.when(jnp.logical_not(first))
                def _():
                    self.along(part, target, second, kind).wait_recv()
                    slot = (target + 1 if kind == 3 else target) + second * (self.levels + 1)
                    self.keep(part, target, rel, self.column(part, target, second, self.land(3, part, slot)))

                self.along(part, target, second, kind).start()

        pl.when(jnp.logical_and(step >= level, self.has_up()))(lambda: go(last - step + level, 3, level == 0))
        pl.when(jnp.logical_and(step >= last - level, self.has_down()))(
            lambda: go(level - last + step, 4, level == last)
        )

    def ends(self, part, second, out):
        level = self.level
        base = second * (self.levels + 1)
        self.ready(part, level, second)
        pl.when(self.has_down())(lambda: self.along(part, level, second, 3).wait_recv())
        pl.when(self.has_up())(lambda: self.along(part, level, second, 4).wait_recv())
        below = self.land(3, part, base + level + 1)
        above = self.land(3, part, base + level)
        inner = jnp.logical_and(self.has_down(), self.has_up())
        pl.when(inner)(lambda: out(self.column(part, level, second, below, above)))
        pl.when(jnp.logical_not(self.has_up()))(lambda: out(self.column(part, level, second, below)))
        pl.when(jnp.logical_not(self.has_down()))(lambda: out(self.column(part, level, second, above)))

    def settle(self, part):
        if part in SUM_STRAIGHT:
            return
        rel = 3 - CROSS[part]
        self.ends(part, 1, lambda value: self.keep(part, self.level, rel, value))
        self.over_last(part).start()

    def last(self, part, out):
        def put(value):
            out[...] = value

        self.ends(part, 0, put)
        if part in SUM_STRAIGHT:
            return
        self.over_last(part).wait_recv()
        out[...] += self.land(2, part, 0)[...].astype(jnp.float32)

    def sent(self, part):
        self.all_sent(part, 4 * self.levels, self.sum_core_send.at[part])
        self.all_sent(part, 2 * self.levels, self.sum_plane_send.at[part, 0])
        self.all_sent(part, self.levels if part in SUM_STRAIGHT else 1, self.sum_plane_send.at[part, 1])

        def body(at):
            for second in self.columns(part):
                pl.when(at > self.level)(lambda: self.along(part, at, second, 3).wait_send())
                pl.when(at < self.level)(lambda: self.along(part, at, second, 4).wait_send())

        fori(self.levels, body)


STRAIGHT = (4, 5)
SUM_STRAIGHT = (0, 1)
CROSS = (1, 2, 1, 2, 1, 2, 1)
PARTS = 7
LAGS = (0, 0, 0)

LAST = (1, 2, 1, 2, 1, 2, 1)


class Given(NamedTuple):
    start: Any
    length: Any
    tokens: Any
    cot_in: Any
    query_in: Any
    key_in: Any
    value_in: Any
    output_in: Any
    inner_in: Any
    outer_in: Any
    query_bias: Any
    value_bias: Any
    output_bias: Any
    first_gain: Any
    first_shift: Any
    outer_bias: Any
    second_gain: Any
    second_shift: Any
    inner_bias_in: Any
    read_in: Any
    write_in: Any


class Made(NamedTuple):
    layer_out: Any
    input_out: Any
    narrow_out: Any
    outer_out: Any
    small_out: Any
    spill: Any


class Room(NamedTuple):
    cot: Any
    mask: Any
    vectors: Any
    inner_bias: Any
    small: Any
    inner_bias_grad: Any
    pair_in: Any
    narrow: Any
    narrow_in: Any
    small_all: Any
    small_rows: Any


class Signals(NamedTuple):
    core_send: Any
    core_recv: Any
    plane_send: Any
    line_send: Any
    gather_recv: Any
    sum_core_send: Any
    sum_core_recv: Any
    sum_plane_send: Any
    sum_plane_recv: Any
    sum_line_send: Any
    sum_line_recv: Any
    trade_sems: Any
    pair_sems: Any
    result_sems: Any
    local_sems: Any
    free_sem: Any


def spread(ref_rows, per, count):
    tiles = [None] * (per * count // LANES)
    lane = lax.broadcasted_iota(jnp.int32, (1, LANES), 1)
    for w in range(count):
        block = jnp.where(lane < per, ref_rows(w), 0.0)
        tile, shift = divmod(per * w, LANES)
        moved = pltpu.roll(block, shift, 1) if shift else block
        pieces = [(tile, jnp.where(lane >= shift, moved, 0.0) if shift else moved)]
        if shift + per > LANES:
            pieces.append((tile + 1, jnp.where(lane < shift + per - LANES, moved, 0.0)))
        for tile, piece in pieces:
            tiles[tile] = piece if tiles[tile] is None else tiles[tile] + piece
    return tiles


def picked(tile_of, per, w):
    lane = lax.broadcasted_iota(jnp.int32, (1, LANES), 1)
    tile, shift = divmod(per * w, LANES)
    block = tile_of(tile)
    if shift:
        block = pltpu.roll(block, LANES - shift, 1)
        if shift + per > LANES:
            block = jnp.where(lane < LANES - shift, block, pltpu.roll(tile_of(tile + 1), LANES - shift, 1))
    return jnp.where(lane < per, block, 0.0)


def whole_kernel(levels, *refs):
    left = list(refs)
    refs = {}
    for kind in (Given, Made, State, Room, Signals):
        refs.update(take(left, kind))
    refs.update(lands=[left[4 * i : 4 * i + 4] for i in range(PARTS - 2)])
    refs.update(own_out=refs.get(Made._fields[1]), small_grad=refs.get(Room._fields[9]), pair_out=None)
    gather = Gather(levels, refs)
    scatter = Scatter(levels, refs)
    layer = Layer(gather.seq, refs)
    seq, level, side, core = gather.seq, gather.level, gather.side, gather.core
    width, half, keys, rows = layer.width, layer.half, layer.keys, layer.rows
    narrow = layer.narrow.shape[0]
    blocks = 8 * levels
    chip = gather.chip(0, level)
    tiles = layer.hidden // width
    barrier = pltpu.get_barrier_semaphore()
    gather.tell_all(barrier)

    for i, piece in enumerate((layer.query_in, layer.key_in, layer.value_in, layer.output_in)):
        layer.narrow[:, i * width : (i + 1) * width] = piece[...]
    layer.narrow[:, 4 * width :] = layer.inner_in[...]
    own_width = layer.query_bias.shape[1]
    layer.small_rows[...] = jnp.zeros_like(layer.small_rows)
    layer.small_rows[0:MEM, 0:own_width] = layer.read_in[...].astype(jnp.float32)
    layer.small_rows[MEM:LINE, 0:own_width] = layer.write_in[...].astype(jnp.float32)
    for i, piece in enumerate(
        (
            layer.query_bias,
            layer.value_bias,
            layer.output_bias,
            layer.first_gain,
            layer.first_shift,
            layer.outer_bias,
            layer.second_gain,
            layer.second_shift,
        )
    ):
        layer.small_rows[LINE + i : LINE + i + 1, 0:own_width] = piece[...].astype(jnp.float32)
    layer.small_rows[28:29, 0 : layer.inner_bias_in.shape[1]] = layer.inner_bias_in[...].astype(jnp.float32)
    layer.small_all[chip * 2 + core] = layer.small_rows[...].astype(jnp.bfloat16)
    own_outer = pltpu.make_async_copy(
        layer.outer_in,
        layer.w_outer.at[pl.ds(pl.multiple_of((chip * 2 + core) * gather.tall, 16), gather.tall), :],
        layer.local_sems.at[0],
    )
    own_outer.start()
    own_tokens = [
        pltpu.make_async_copy(
            layer.tokens.at[slot], layer.hid.at[pl.ds(slot * keys + half, half)], layer.local_sems.at[1 + slot]
        )
        for slot in range(layer.slots)
    ]
    cots = [
        pltpu.make_async_copy(layer.cot_in.at[slot], layer.cot.at[0], layer.local_sems.at[5 + slot])
        for slot in range(layer.slots)
    ]
    for copy in own_tokens:
        copy.start()
    cots[1].start()
    share_tokens = [
        gather.remote(
            layer.tokens.at[slot],
            layer.hid.at[pl.ds(slot * keys, half)],
            layer.pair_sems.at[0, slot],
            layer.pair_sems.at[1, slot],
            2,
        )
        for slot in range(layer.slots)
    ]
    pl.semaphore_wait(barrier, gather.neighbours())
    trade = [
        gather.remote(
            layer.narrow.at[:, pl.ds(pl.multiple_of((2 * i + 1 - core) * (2 * width), LANES), 2 * width)],
            layer.narrow_in.at[i],
            layer.trade_sems.at[0, i],
            layer.trade_sems.at[1, i],
            0,
        )
        for i in range(2)
    ]
    for copy in trade:
        copy.start()
    gather.own(6)
    own_outer.wait()
    first = core == 0
    for i, whole in enumerate((layer.w_attention, layer.w_inner)):
        trade[i].wait_recv()
        column = pl.multiple_of(core * (2 * width), LANES)
        mine = layer.narrow[:, pl.ds(pl.multiple_of((2 * i + core) * (2 * width), LANES), 2 * width)].astype(jnp.float32)
        other = layer.narrow_in[i].astype(jnp.float32)
        merged = jnp.concatenate([jnp.where(first, mine, other), jnp.where(first, other, mine)], axis=0)
        whole[pl.ds(pl.multiple_of(chip * gather.thick, 16), gather.thick), pl.ds(column, 2 * width)] = merged.astype(
            jnp.bfloat16
        )
        gather.own(2 * i)
        gather.own(2 * i + 1)
        if i == 0:
            share_tokens[0].start()
    gather.own(4)
    gather.own(5)
    for step in range(1, levels + 2):
        gather.step(6, step)

    def turn(number):
        for group in range(3):
            for part in (2 * group, 2 * group + 1):
                if 1 <= number - LAGS[group] <= levels + 1:
                    gather.step(part, number - LAGS[group])

    def have(*parts):
        for part in parts:
            gather.other_core(part)

    layer.small[...] = jnp.zeros_like(layer.small)
    layer.inner_bias_grad[...] = jnp.zeros_like(layer.inner_bias_grad)
    spot = lax.broadcasted_iota(jnp.int32, (1, keys), 1)
    position = jnp.where(
        spot < half,
        spot + (1 - seq) * half,
        jnp.where(spot < 2 * half, spot + (seq - 1) * half, jnp.where(spot < 2 * half + LINE, -1, 1 << 30)),
    )
    for slot in range(layer.slots):
        layer.mask[slot] = jnp.where(position < layer.length[slot], 0.0, NEG_FILL)

    have(6)
    vectors = spread(lambda w: layer.small_all[w].astype(jnp.float32), width // blocks, blocks)
    for i, tile in enumerate(vectors):
        layer.vectors[:, i * LANES : (i + 1) * LANES] = tile
    biases = spread(
        lambda w: layer.small_all[w].astype(jnp.float32)[28:29, :], layer.hidden // blocks, blocks
    )
    for i, tile in enumerate(biases):
        layer.inner_bias[:, i * LANES : (i + 1) * LANES] = tile
    layer.set_memory(0)

    spill = [
        pltpu.make_async_copy(layer.shares, layer.spill, layer.local_sems.at[3]),
        pltpu.make_async_copy(layer.spill, layer.shares, layer.local_sems.at[4]),
    ]

    def project():
        have(0, 1)
        own_tokens[0].wait()
        share_tokens[0].wait()
        layer.project_query(0)
        layer.project_key(0)
        layer.project_value(0)

    def attend(*pairs):
        return lambda: layer.attend(0, pairs)

    work = [
        project,
        attend(0, 1, 2),
        attend(3, 4, 5),
        lambda: (spill[0].start(), layer.branch(0)),
    ]
    for number in range(1, levels + 2 + max(LAGS)):
        turn(number)
        if number > levels:
            work.pop(0)()
    share_tokens[1].start()
    for item in work:
        item()
    have(2, 3)
    fori(tiles, lambda j: layer.inner(0, j))
    have(4, 5)
    layer.outer(0)

    layer.set_memory(1)
    own_tokens[1].wait()
    share_tokens[1].wait()
    layer.project_query(1)
    layer.project_key(1)
    layer.project_value(1)
    spill[0].wait()
    layer.attend(1)
    layer.branch(1)
    fori(tiles, lambda j: layer.inner(1, j))
    layer.outer(1)
    for part in range(PARTS):
        gather.sent(part)
    for copy in trade:
        copy.wait_send()
    layer.memory[...] = jnp.zeros_like(layer.memory)

    def pair_copy(slot):
        return gather.remote(
            layer.pair_room(slot),
            layer.pair_in.at[slot],
            layer.pair_sems.at[2, slot],
            layer.pair_sems.at[3, slot],
            2,
        )

    cots[1].wait()
    layer.outer_back(1)
    cots[0].start()
    layer.inner_back(1)
    layer.mix_back(1)
    layer.attend_back(1)
    spill[1].start()
    passed = layer.input_back(1)
    layer.swap_out[...] = passed
    swap = gather.remote(layer.swap_out, layer.swap_in, layer.pair_sems.at[4, 0], layer.pair_sems.at[4, 1], 2)
    swap.start()
    swap.wait()
    pair_copy(1).start()
    summed = pltpu.roll(passed + layer.swap_in[...], MEM, 0)
    layer.memory[...] = jnp.where(seq == 0, summed, 0.0)
    cots[0].wait()
    layer.outer_back(0)

    def narrow_result(part):
        scatter.last(part, layer.work.at[pl.ds(part * 2 * narrow, 2 * narrow), :])
        column = pl.ds(pl.multiple_of((part // 2) * (4 * width) + core * (2 * width) + (part % 2) * width, LANES), width)
        layer.narrow_out[:, column] = layer.work[pl.ds(pl.multiple_of((2 * part + core) * narrow, 8), narrow), :]
        share_result(part).start()

    def share_result(part):
        column = pl.ds(pl.multiple_of((part // 2) * (4 * width) + core * (2 * width) + (part % 2) * width, LANES), width)
        return gather.remote(
            layer.work.at[pl.ds(pl.multiple_of((2 * part + 1 - core) * narrow, 8), narrow), :],
            layer.narrow_out.at[:, column],
            layer.result_sems.at[0, part],
            layer.result_sems.at[1, part],
            0,
        )

    def share_result_in(part):
        column = pl.ds(
            pl.multiple_of((part // 2) * (4 * width) + (1 - core) * (2 * width) + (part % 2) * width, LANES), width
        )
        return gather.remote(
            layer.work.at[pl.ds(pl.multiple_of((2 * part + 1 - core) * narrow, 8), narrow), :],
            layer.narrow_out.at[:, column],
            layer.result_sems.at[0, part],
            layer.result_sems.at[1, part],
            0,
        )

    def outer_result(part):
        size = gather.tall // 2
        scatter.last(part, layer.outer_out.at[pl.ds((part - 4) * size, size), :])

    def both(function, *parts, **more):
        for part in parts:
            function(part, **more)

    def give_input(slot):
        pair_copy(slot).wait()
        total = layer.input_out[slot].astype(jnp.float32) + layer.pair_in[slot].astype(jnp.float32)
        layer.input_out[slot] = total.astype(jnp.bfloat16)

    fori(tiles, layer.outer_weight_grad)
    both(scatter.start_core, 4, 5)
    layer.inner_back(0)
    both(scatter.cross, 4, 5)
    fori(tiles, layer.inner_weight_grad)
    scatter.tell_all(layer.free_sem)
    both(scatter.start_core, 2, 3)
    both(scatter.plane, 4, 5)
    both(scatter.line, 4, 5, step=0)
    layer.mix_back(0)
    spill[1].wait()
    layer.attend_back(0, (0, 1))
    both(scatter.cross, 2, 3)
    both(scatter.line, 4, 5, step=1)
    layer.attend_back(0, (2, 3))
    both(scatter.plane, 2, 3)
    both(scatter.line, 2, 3, step=0)
    both(scatter.line, 4, 5, step=2)
    layer.attend_back(0, (4, 5))
    both(scatter.line, 2, 3, step=1)
    both(scatter.settle, 4, 5)
    layer.input_back(0)
    pair_copy(0).start()
    both(scatter.line, 2, 3, step=2)
    layer.output_weight_grad()
    layer.value_weight_grad()
    layer.query_weight_grad()
    layer.key_weight_grad()
    pl.semaphore_wait(layer.free_sem, scatter.neighbours())
    both(scatter.start_core, 0, 1)
    small_tile = lambda i: layer.small[:, i * LANES : (i + 1) * LANES]
    inner_tile = lambda i: layer.inner_bias_grad[:, i * LANES : (i + 1) * LANES]
    small_row = lax.broadcasted_iota(jnp.int32, (32, 1), 0)
    for w in range(blocks):
        vectors_part = picked(small_tile, width // blocks, w)
        bias_part = picked(inner_tile, layer.hidden // blocks, w)
        layer.small_grad[w] = jnp.where(small_row == 28, bias_part, vectors_part).astype(jnp.bfloat16)
    scatter.start_core(6)
    both(scatter.cross, 0, 1, 6)
    both(outer_result, 4, 5)
    both(scatter.settle, 2, 3)
    both(scatter.plane, 0, 1, 6)
    both(scatter.line, 0, 1, 6, step=0)
    both(narrow_result, 2, 3)
    give_input(1)
    for step in range(1, levels - 1):
        both(scatter.line, 0, 1, 6, step=step)
    give_input(0)
    both(scatter.settle, 0, 1, 6)
    both(narrow_result, 0, 1)
    scatter.last(6, layer.small_out)
    for part in range(4):
        share_result_in(part).wait_recv()
        share_result(part).wait_send()
    for part in range(PARTS):
        scatter.sent(part)


def whole_layer(levels, start, length, tokens, cotangent, weights, vectors, inner_bias, read_init, write_init):
    slots, half, width = tokens.shape
    query_in, outer_in, inner_in = weights[0], weights[5], weights[4]
    hidden = inner_in.shape[1]
    narrow, tall = query_in.shape[0], outer_in.shape[0]
    blocks = 8 * levels
    bf16, f32 = jnp.bfloat16, jnp.float32
    inside = pl.BlockSpec(memory_space=pltpu.VMEM)
    scalars = pl.BlockSpec(memory_space=pltpu.SMEM)
    anywhere = pl.BlockSpec(memory_space=pl.ANY)
    shape = jax.ShapeDtypeStruct
    dma = pltpu.SemaphoreType.DMA
    state = state_shapes(slots, half, width, hidden)
    shares = (width // LANES,) + state.shares[0][1:]
    state = state._replace(shares=(shares, bf16))
    room = Room(
        cot=((1, half, width), bf16),
        mask=((slots, 1, 2 * half + MEMORY), f32),
        vectors=((32, width), f32),
        inner_bias=((1, hidden), f32),
        small=((32, width), f32),
        inner_bias_grad=((1, hidden), f32),
        pair_in=((slots, half, width), bf16),
        narrow=((narrow, 8 * width), bf16),
        narrow_in=((2, narrow, 2 * width), bf16),
        small_all=((blocks, 32, LANES), bf16),
        small_rows=((32, LANES), f32),
    )
    signals = Signals(
        core_send=dma((PARTS,)),
        core_recv=dma((PARTS,)),
        plane_send=dma((PARTS, 2)),
        line_send=dma((PARTS, 2, levels + 1)),
        gather_recv=dma((PARTS, 4 * levels)),
        sum_core_send=dma((PARTS,)),
        sum_core_recv=dma((PARTS,)),
        sum_plane_send=dma((PARTS, 2)),
        sum_plane_recv=dma((PARTS, 3 * levels)),
        sum_line_send=dma((PARTS, 2, levels)),
        sum_line_recv=dma((PARTS, 2, levels + 1)),
        trade_sems=dma((2, 2)),
        pair_sems=dma((5, 2)),
        result_sems=dma((2, 4)),
        local_sems=dma((7,)),
        free_sem=pltpu.SemaphoreType.REGULAR,
    )
    lands = []
    for part in range(2, PARTS):
        size = (2 * narrow, width) if part < 4 else (tall // 2, width) if part < 6 else (32, LANES)
        late = (levels, levels + 1) if part in SUM_STRAIGHT else (1, 2 * levels + 2)
        lands += [pltpu.VMEM((count,) + size, bf16) for count in (4 * levels, 2 * levels) + late]
    return pl.pallas_call(
        functools.partial(whole_kernel, levels),
        out_shape=[
            shape((slots, half, width), bf16),
            shape((slots, half, width), bf16),
            shape((narrow, 8 * width), f32),
            shape((tall, width), f32),
            shape((32, LANES), f32),
            shape(shares, bf16),
        ],
        in_specs=[scalars] * 2 + [anywhere] * 2 + [inside] * 5 + [anywhere] + [inside] * 11,
        out_specs=[inside] * 5 + [anywhere],
        scratch_shapes=[pltpu.VMEM(*s) for s in state + room] + list(signals) + lands,
        compiler_params=pltpu.CompilerParams(
            collective_id=0, has_side_effects=True, vmem_limit_bytes=63 * 2**20
        ),
        cost_estimate=pl.CostEstimate(flops=31 * 10**9, bytes_accessed=10 * 10**6, transcendentals=10**7),
        name="whole_layer",
    )(start, length, tokens, cotangent, *weights, *(v[None] for v in vectors), inner_bias[None], read_init, write_init)


def hand_out_kernel(layer_ref, input_ref, narrow_ref, outer_ref, small_ref, *out_refs):
    width = outer_ref.shape[1]
    out_refs[0][...] = layer_ref[...]
    out_refs[1][...] = input_ref[...]
    for i in range(4):
        out_refs[2 + i][...] = narrow_ref[:, i * width : (i + 1) * width]
    out_refs[6][...] = narrow_ref[:, 4 * width :]
    out_refs[7][...] = outer_ref[...]
    for i in range(8):
        out_refs[8 + i][...] = small_ref[LINE + i : LINE + i + 1, 0 : out_refs[8 + i].shape[1]]
    out_refs[16][...] = small_ref[28:29, 0 : out_refs[16].shape[1]]
    out_refs[17][...] = small_ref[0:MEM, 0 : out_refs[17].shape[1]]
    out_refs[18][...] = small_ref[MEM:LINE, 0 : out_refs[18].shape[1]]


def hand_out(results, narrow, inner_width):
    layer_out, input_out, narrow_out, outer_out, small_out = results
    width = outer_out.shape[1]
    shape = jax.ShapeDtypeStruct
    f32 = jnp.float32
    inside = pl.BlockSpec(memory_space=pltpu.VMEM)
    return pl.pallas_call(
        hand_out_kernel,
        out_shape=[shape(layer_out.shape, layer_out.dtype), shape(input_out.shape, input_out.dtype)]
        + [shape((narrow, width), f32)] * 4
        + [shape((narrow, narrow_out.shape[1] - 4 * width), f32), shape(outer_out.shape, f32)]
        + [shape((1, narrow), f32)] * 8
        + [shape((1, inner_width), f32)]
        + [shape((MEM, narrow), f32)] * 2,
        in_specs=[inside] * 5,
        out_specs=[inside] * 19,
        compiler_params=pltpu.CompilerParams(vmem_limit_bytes=62 * 2**20),
    )(layer_out, input_out, narrow_out, outer_out, small_out)


def small_block(vectors, inner_bias, read_init, write_init):
    width = vectors[0].shape[0]
    inner_width = inner_bias.shape[0]
    rows = jnp.concatenate([read_init, write_init] + [v[None] for v in vectors], axis=0)
    rows = jnp.pad(rows, ((0, 4), (0, 128 - width)))
    return rows + jnp.pad(inner_bias[None], ((28, 3), (0, 128 - inner_width)))


def apart(tokens, cotangent, start, length, weights, small, blocks):
    half, model_width = tokens.shape[1:]
    width, inner_width = weights[0].shape[0], weights[5].shape[0]
    axes = AXES
    pair = [(0, 1), (1, 0)]
    others = lax.ppermute(tokens, AXES[0], pair)
    whole = [lax.all_gather(w, axes, axis=0, tiled=True) for w in weights]
    small_all = lax.all_gather(small, axes, axis=0)
    vectors = small_all[:, :, :width].transpose(1, 0, 2).reshape(32, model_width).astype(jnp.float32)
    bias_inner = small_all[:, 28, :inner_width].reshape(1, -1).astype(jnp.float32)
    mine = lax.axis_index(AXES[0])
    place_in = jnp.arange(half)
    position = jnp.concatenate(
        [
            (1 - mine) * half + place_in,
            mine * half + place_in,
            jnp.where(jnp.arange(MEMORY) < LINE, -1, 1 << 30),
        ]
    )
    mask = jnp.where(position[None, :] < length[:, None], 0.0, NEG_FILL)[:, None, :]
    results = middle(start, mask, tokens, others, cotangent, vectors, bias_inner, whole)
    received = lax.ppermute(results[2], AXES[0], pair)
    input_grad = (results[1] + received.astype(jnp.float32)).astype(jnp.bfloat16)
    small_grads = jnp.pad(
        results[3].reshape(32, blocks, width).transpose(1, 0, 2), ((0, 0), (0, 0), (0, 128 - width))
    )
    inner_rows = jnp.pad(results[4].reshape(blocks, 1, inner_width), ((0, 0), (28, 3), (0, 128 - inner_width)))
    small_grads = jnp.where(jnp.arange(32)[None, :, None] == 28, inner_rows, small_grads).astype(jnp.bfloat16)

    def summed(grad):
        paired = lax.psum_scatter(grad, AXES[0], scatter_dimension=0, tiled=True).astype(jnp.float32)
        return lax.psum_scatter(paired, AXES[1], scatter_dimension=0, tiled=True)

    small_sum = summed(small_grads.reshape(-1, 128))
    return results[0], input_grad, [summed(g) for g in results[5:]], small_sum


def shards(
    tokens,
    cotangent,
    chain_start,
    seg_len,
    query_weight,
    key_weight,
    value_weight,
    output_weight,
    query_bias,
    value_bias,
    output_bias,
    first_gain,
    first_shift,
    inner_weight,
    inner_bias,
    outer_weight,
    outer_bias,
    second_gain,
    second_shift,
    read_init,
    write_init,
):
    width = query_bias.shape[0]
    levels = lax.axis_size(AXES[1]) // 4
    blocks = 8 * levels
    weights = (query_weight, key_weight, value_weight, output_weight, inner_weight, outer_weight)
    vectors = (
        query_bias,
        value_bias,
        output_bias,
        first_gain,
        first_shift,
        outer_bias,
        second_gain,
        second_shift,
    )
    inner_width = inner_bias.shape[0]
    if width % 8 == 0:
        results = whole_layer(
            levels,
            chain_start[0],
            seg_len[0],
            tokens[0],
            cotangent[0],
            weights,
            vectors,
            inner_bias,
            read_init,
            write_init,
        )
        results = hand_out(results[:5], width, inner_width)
        layer_out, input_grad = results[:2]
        sums = results[2:8]
        vector = [v[0] for v in results[8:16]]
        inner_sum, read_sum, write_sum = results[16][0], results[17], results[18]
    else:
        small = small_block(vectors, inner_bias, read_init, write_init)
        layer_out, input_grad, sums, small_sum = apart(
            tokens[0], cotangent[0], chain_start[0], seg_len[0], weights, small, blocks
        )
        vector = [small_sum[LINE + i, :width] for i in range(8)]
        inner_sum = small_sum[28, :inner_width]
        read_sum, write_sum = small_sum[:MEM, :width], small_sum[MEM:LINE, :width]
    return (
        layer_out[None],
        input_grad[None],
        *sums[:4],
        *vector[:5],
        sums[4],
        inner_sum,
        sums[5],
        *vector[5:],
        read_sum,
        write_sum,
    )


def solution(mesh):
    rows = P(AXES[1], None, AXES[0], None)
    scalars = P(AXES[1], None)
    matrix, vector, memory = P(AXES, None), P(AXES), P(None, AXES)
    weights = (
        (matrix,) * 4
        + (vector,) * 5
        + (matrix, vector, matrix)
        + (vector,) * 3
        + (memory,) * 2
    )
    return jax.shard_map(
        shards,
        mesh=mesh,
        in_specs=(rows, rows, scalars, scalars) + weights,
        out_specs=(rows, rows) + weights,
        check_vma=False,
    )
```

```python
import functools
import math
from typing import Any, NamedTuple

import jax
import jax.numpy as jnp
from jax import lax
from jax.experimental import pallas as pl
from jax.experimental.pallas import tpu as pltpu
from jax.sharding import PartitionSpec as P

HEADS = 12
MEM = 10
EPS = 1e-12
INV_ROOT_TWO = 1.0 / math.sqrt(2.0)
INV_ROOT_TWO_PI = 1.0 / math.sqrt(2.0 * math.pi)
NEG_FILL = -1000000000.0

AXES = ("seq", "chain")


MESH = pl.DeviceIdType.MESH


def place():
    seq = lax.axis_index(AXES[0])
    chain = lax.axis_index(AXES[1])
    return seq, chain // 4, lax.rem(chain // 2, 2), lax.rem(chain, 2)


def block_of(levels, seq, level, side, core):
    return seq * (4 * levels) + level * 4 + side * 2 + core


def device_of(seq, level, side, core):
    return (seq, level * 4 + side * 2 + core)


def fori(count, body):
    def step(index, carry):
        body(index)
        return carry

    lax.fori_loop(0, count, step, 0)


def span(index, size):
    return pl.ds(pl.multiple_of(index * size, size), size)


def dot_nn(former, latter):
    return jnp.dot(former, latter, preferred_element_type=jnp.float32)


def dot_nt(former, latter):
    return lax.dot_general(former, latter, (((1,), (1,)), ((), ())), preferred_element_type=jnp.float32)


def dot_tn(former, latter):
    return lax.dot_general(former, latter, (((0,), (0,)), ((), ())), preferred_element_type=jnp.float32)


def fold(rows):
    return jnp.sum(rows.reshape(rows.shape[0] // 8, 8, rows.shape[1]), axis=0)


CHUNK = 48
MEMORY = 32
LANES = 128
LINE = 2 * MEM


class Layer:
    def __init__(self, seq, refs):
        self.seq = seq
        self.__dict__.update(refs)
        self.slots = self.layer_out.shape[0]
        self.half, self.width = self.layer_out.shape[1:]
        self.rows = self.half + MEMORY
        self.keys = self.rows + self.half
        self.hidden = self.w_inner.shape[1]
        self.pairs = self.width // LANES
        self.scale = 1.0 / math.sqrt(self.width // HEADS)
        lane = lax.broadcasted_iota(jnp.int32, (1, LANES), 1)
        self.low = lane < LANES // 2
        self.low_f = jnp.where(self.low, 1.0, 0.0)
        self.low_b = self.low_f.astype(jnp.bfloat16)
        self.high_f = 1.0 - self.low_f
        self.high_b = self.high_f.astype(jnp.bfloat16)
        self.mem_row = lax.broadcasted_iota(jnp.int32, (MEMORY, 1), 0)

    def vec(self, at):
        return self.vectors[LINE + at : LINE + at + 1, :]

    def slot_rows(self, slot):
        return pl.ds(slot * self.rows, self.rows)

    def slot_keys(self, slot):
        return pl.ds(slot * self.keys, self.keys)

    def slot_queries(self, slot):
        return pl.ds(slot * self.keys + self.half, self.rows)

    def weight(self, at):
        return self.w_attention.at[:, pl.ds(at * self.width, self.width)]

    def pair_room(self, slot):
        if self.pair_out is not None:
            return self.pair_out.at[slot]
        return (self.key if slot else self.value).at[pl.ds(self.keys, self.half)]

    def set_memory(self, slot):
        initial = jnp.where(self.mem_row < LINE, self.vectors[0:MEMORY, :], 0.0)
        if slot > 0:
            second = self.work[self.half : self.rows].astype(jnp.bfloat16).astype(jnp.float32)
            carried = pltpu.roll(second, MEMORY - MEM, 0)
        else:
            carried = jnp.zeros_like(initial)
        restart = self.start[slot] == 1
        initial = jnp.where(jnp.logical_or(self.mem_row >= MEM, restart), initial, carried)
        base = slot * self.keys + 2 * self.half
        self.hid[base : base + MEMORY] = initial.astype(jnp.bfloat16)

    def project_query(self, slot):
        out = dot_nn(self.hid[self.slot_queries(slot)], self.weight(0)[...]) + self.vec(0)
        self.query[self.slot_rows(slot)] = out.astype(jnp.bfloat16)

    def project_key(self, slot):
        self.key[self.slot_keys(slot)] = dot_nn(self.hid[self.slot_keys(slot)], self.weight(1)[...]).astype(
            jnp.bfloat16
        )

    def project_value(self, slot):
        out = dot_nn(self.hid[self.slot_keys(slot)], self.weight(2)[...]) + self.vec(1)
        self.value[self.slot_keys(slot)] = out.astype(jnp.bfloat16)

    def share_at(self, slot, p):
        return p if self.shares.shape[0] == self.pairs else slot * self.pairs + p

    def attend(self, slot, pairs=None):
        valid = self.mask[slot]
        low_scaled = (self.low_f * self.scale).astype(jnp.bfloat16)
        high_scaled = (self.high_f * self.scale).astype(jnp.bfloat16)
        rows = self.rows
        for p in pairs or range(self.pairs):
            here = pl.ds(p * LANES, LANES)
            query_pair = self.query[self.slot_rows(slot), here]
            key_pair = self.key[self.slot_keys(slot), here]
            value_pair = self.value[self.slot_keys(slot), here]
            stacked = jnp.concatenate([query_pair * low_scaled, query_pair * high_scaled], axis=0)
            scores = dot_nt(stacked, key_pair) + valid
            raised = jnp.exp(scores - jnp.max(scores, axis=1, keepdims=True)).astype(jnp.bfloat16)
            self.shares[self.share_at(slot, p)] = raised
            ones = jnp.ones((self.keys, LANES), jnp.bfloat16)
            summed = dot_nn(raised, jnp.concatenate([value_pair, ones], axis=1))
            inverse = 1.0 / summed[:, LANES:]
            out = summed[:, :LANES] * inverse
            self.inverse_total[self.slot_rows(slot), here] = jnp.where(self.low, inverse[:rows], inverse[rows:])
            self.mixed[self.slot_rows(slot), here] = jnp.where(self.low, out[:rows], out[rows:]).astype(jnp.bfloat16)

    def norm(self, slot, normed, inverse, gain_at, shift_at, rounded=None):
        for r in range(self.rows // CHUNK):
            here = pl.ds(r * CHUNK, CHUNK)
            there = pl.ds(slot * self.rows + r * CHUNK, CHUNK)
            z = self.work[here, :]
            centred = z - jnp.mean(z, axis=1, keepdims=True)
            inv = lax.rsqrt(jnp.mean(centred * centred, axis=1, keepdims=True) + EPS)
            unit = centred * inv
            normed[there] = unit.astype(jnp.bfloat16)
            self.inverse[there, inverse : inverse + 1] = inv
            out = unit * self.vec(gain_at) + self.vec(shift_at)
            self.work[here, :] = out
            if rounded is not None:
                rounded[there] = out.astype(jnp.bfloat16)

    def branch(self, slot):
        out = dot_nn(self.mixed[self.slot_rows(slot)], self.weight(3)[...]) + self.vec(2)
        self.work[...] = out + self.hid[self.slot_queries(slot)].astype(jnp.float32)
        self.norm(slot, self.normed_one, 0, 3, 4, self.first_b)

    def inner(self, slot, j):
        here = span(j, self.width)
        u = dot_nn(self.first_b[self.slot_rows(slot)], self.w_inner[:, here]) + self.inner_bias[:, here]
        cumulative = 0.5 * (1.0 + lax.erf(u * INV_ROOT_TWO))
        density = jnp.exp(-0.5 * u * u) * INV_ROOT_TWO_PI
        self.active[self.slot_rows(slot), here] = (u * cumulative).astype(jnp.bfloat16)
        self.slope[self.slot_rows(slot), here] = (cumulative + u * density).astype(jnp.bfloat16)

    def outer(self, slot):
        self.work[...] += dot_nn(self.active[self.slot_rows(slot)], self.w_outer[...]) + self.vec(5)
        self.norm(slot, self.normed_two, 1, 6, 7)
        self.layer_out[slot] = self.work[0 : self.half].astype(jnp.bfloat16)

    def add_small(self, at, folded):
        self.small[LINE + at : LINE + at + 1, :] += jnp.sum(folded, axis=0, keepdims=True)

    def norm_back(self, slot, normed, inverse, gain_at, shift_at, bias_at, rounded):
        zero = jnp.zeros((8, self.width), jnp.float32)
        gain_sum, shift_sum, bias_sum = zero, zero, zero
        for r in range(self.rows // CHUNK):
            here = pl.ds(r * CHUNK, CHUNK)
            there = pl.ds(slot * self.rows + r * CHUNK, CHUNK)
            grad = self.work[here, :]
            unit = normed[there].astype(jnp.float32)
            gain_sum = gain_sum + fold(grad * unit)
            shift_sum = shift_sum + fold(grad)
            scaled = grad * self.vec(gain_at)
            dz = self.inverse[there, inverse : inverse + 1] * (
                scaled
                - jnp.mean(scaled, axis=1, keepdims=True)
                - unit * jnp.mean(scaled * unit, axis=1, keepdims=True)
            )
            self.work[here, :] = dz
            dz_b = dz.astype(jnp.bfloat16)
            rounded[there] = dz_b
            bias_sum = bias_sum + fold(dz_b.astype(jnp.float32))
        self.add_small(gain_at, gain_sum)
        self.add_small(shift_at, shift_sum)
        self.add_small(bias_at, bias_sum)

    def outer_back(self, slot):
        self.work[0 : self.half] = self.cot[slot if self.cot.shape[0] > 1 else 0].astype(jnp.float32)
        self.work[self.half : self.rows] = self.memory[...]
        self.norm_back(slot, self.normed_two, 1, 6, 7, 5, self.grad_two_b)

        def tile(j):
            here = span(j, self.width)
            rows = self.slot_rows(slot)
            grad = dot_nt(self.grad_two_b[rows], self.w_outer[here, :]) * self.slope[rows, here].astype(jnp.float32)
            grad_b = grad.astype(jnp.bfloat16)
            self.slope[rows, here] = grad_b
            self.inner_bias_grad[:, here] += jnp.sum(fold(grad_b.astype(jnp.float32)), axis=0, keepdims=True)

        fori(self.hidden // self.width, tile)

    def inner_back(self, slot):
        self.work[...] += dot_nt(self.slope[self.slot_rows(slot)], self.w_inner[...])
        self.norm_back(slot, self.normed_one, 0, 3, 4, 2, self.grad_one_b)

    def mix_back(self, slot):
        grad = dot_nt(self.grad_one_b[self.slot_rows(slot)], self.weight(3)[...])
        self.grad_mixed[...] = grad.astype(jnp.bfloat16)

    def attend_back(self, slot, pairs=None):
        rows = self.rows
        own = self.slot_rows(slot)
        every = self.slot_keys(slot)

        def pair(p):
            here = pl.ds(p * LANES, LANES)
            query_pair = self.query[own, here]
            key_pair = self.key[every, here]
            value_pair = self.value[every, here]
            grad = self.grad_mixed[:, here].astype(jnp.float32) * self.inverse_total[own, here]
            product = grad * self.mixed[own, here].astype(jnp.float32)
            delta = jnp.concatenate(
                [
                    jnp.sum(product * self.low_f, axis=1, keepdims=True),
                    jnp.sum(product * self.high_f, axis=1, keepdims=True),
                ],
                axis=0,
            )
            grad_b = grad.astype(jnp.bfloat16)
            stacked = jnp.concatenate([grad_b * self.low_b, grad_b * self.high_b], axis=0)
            raised = self.shares[self.share_at(slot, p)]
            grad_scores = (raised.astype(jnp.float32) * (dot_nt(stacked, value_pair) - delta)).astype(jnp.bfloat16)
            both = dot_nn(grad_scores, key_pair)
            query_b = (jnp.where(self.low, both[:rows], both[rows:]) * self.scale).astype(jnp.bfloat16)
            queries = jnp.concatenate([query_pair * self.low_b, query_pair * self.high_b], axis=0)
            value_b = dot_tn(stacked, raised).T.astype(jnp.bfloat16)
            self.grad_query[own, here] = query_b
            self.grad_key[every, here] = (dot_tn(queries, grad_scores) * self.scale).T.astype(jnp.bfloat16)
            self.grad_value[every, here] = value_b
            self.small[LINE : LINE + 1, here] += jnp.sum(fold(query_b.astype(jnp.float32)), axis=0, keepdims=True)
            self.small[LINE + 1 : LINE + 2, here] += jnp.sum(fold(value_b.astype(jnp.float32)), axis=0, keepdims=True)

        for p in pairs or range(self.pairs):
            pair(p)

    def input_back(self, slot):
        every = self.slot_keys(slot)
        half = self.half
        grads = dot_nt(self.grad_key[every], self.weight(1)[...]) + dot_nt(self.grad_value[every], self.weight(2)[...])
        self.pair_room(slot)[...] = grads[0:half].astype(jnp.bfloat16)
        mine = grads[half:] + dot_nt(self.grad_query[self.slot_rows(slot)], self.weight(0)[...]) + self.work[...]
        self.own_out[slot] = mine[0:half].astype(self.own_out.dtype)
        memory = mine[half:]
        restart = self.start[slot] == 1
        counted = jnp.logical_or(
            jnp.logical_and(self.mem_row < MEM, restart),
            jnp.logical_and(self.mem_row >= MEM, self.mem_row < LINE),
        )
        self.small[0:MEMORY, :] += jnp.where(counted, memory, 0.0)
        return jnp.where(jnp.logical_and(self.mem_row < MEM, jnp.logical_not(restart)), memory, 0.0)

    def outer_weight_grad(self, j):
        here = span(j, self.width)
        self.w_outer[here, :] = dot_tn(self.active[:, here], self.grad_two_b[...]).astype(jnp.bfloat16)

    def inner_weight_grad(self, j):
        here = span(j, self.width)
        self.w_inner[:, here] = dot_tn(self.first_b[...], self.slope[:, here]).astype(jnp.bfloat16)

    def output_weight_grad(self):
        self.weight(3)[...] = dot_tn(self.mixed[...], self.grad_one_b[...]).astype(jnp.bfloat16)

    def query_weight_grad(self):
        total = None
        for slot in range(self.slots):
            term = dot_tn(self.hid[self.slot_queries(slot)], self.grad_query[self.slot_rows(slot)])
            total = term if total is None else total + term
        self.weight(0)[...] = total.astype(jnp.bfloat16)

    def key_weight_grad(self):
        self.weight(1)[...] = dot_tn(self.hid[...], self.grad_key[...]).astype(jnp.bfloat16)

    def value_weight_grad(self):
        self.weight(2)[...] = dot_tn(self.hid[...], self.grad_value[...]).astype(jnp.bfloat16)


class State(NamedTuple):
    w_attention: Any
    w_inner: Any
    w_outer: Any
    hid: Any
    query: Any
    key: Any
    value: Any
    shares: Any
    inverse_total: Any
    mixed: Any
    normed_one: Any
    normed_two: Any
    inverse: Any
    first_b: Any
    slope: Any
    active: Any
    grad_two_b: Any
    grad_one_b: Any
    grad_mixed: Any
    grad_query: Any
    grad_key: Any
    grad_value: Any
    work: Any
    memory: Any
    swap_out: Any
    swap_in: Any


def state_shapes(slots, half, width, hidden):
    rows, keys = half + MEMORY, 2 * half + MEMORY
    bf16, f32 = jnp.bfloat16, jnp.float32
    pairs = width // LANES
    by_row, by_key = ((slots * rows, width), bf16), ((slots * keys, width), bf16)
    return State(
        w_attention=((width, 4 * width), bf16),
        w_inner=((width, hidden), bf16),
        w_outer=((hidden, width), bf16),
        hid=by_key,
        query=by_row,
        key=by_key,
        value=by_key,
        shares=((slots * pairs, 2 * rows, keys), bf16),
        inverse_total=((slots * rows, width), f32),
        mixed=by_row,
        normed_one=by_row,
        normed_two=by_row,
        inverse=((slots * rows, 2), f32),
        first_b=by_row,
        slope=((slots * rows, hidden), bf16),
        active=((slots * rows, hidden), bf16),
        grad_two_b=by_row,
        grad_one_b=by_row,
        grad_mixed=((rows, width), bf16),
        grad_query=by_row,
        grad_key=by_key,
        grad_value=by_key,
        work=((rows, width), f32),
        memory=((MEMORY, width), f32),
        swap_out=((MEMORY, width), f32),
        swap_in=((MEMORY, width), f32),
    )


class Inputs(NamedTuple):
    start: Any
    mask: Any
    tokens: Any
    others: Any
    cot: Any
    vectors: Any
    inner_bias: Any


class Outputs(NamedTuple):
    layer_out: Any
    own_out: Any
    pair_out: Any
    small: Any
    inner_bias_grad: Any


def take(refs, kind):
    return kind(*(refs.pop(0) for _ in kind._fields))._asdict()


def middle_kernel(*refs):
    refs = list(refs)
    given = take(refs, Inputs)
    weights = [refs.pop(0) for _ in range(6)]
    given.update(take(refs, Outputs))
    grads = [refs.pop(0) for _ in range(6)]
    given.update(take(refs, State))
    load_sems, pair_sems = refs
    seq = lax.axis_index(AXES[0])
    chain = lax.axis_index(AXES[1])
    barrier = pltpu.get_barrier_semaphore()
    pl.semaphore_signal(barrier, inc=1, device_id=(1 - seq, chain), device_id_type=MESH)
    layer = Layer(seq, given)
    places = [layer.weight(i) for i in range(4)] + [layer.w_inner, layer.w_outer]
    loads = [pltpu.make_async_copy(weights[i], places[i], load_sems.at[i]) for i in range(6)]
    stores = [pltpu.make_async_copy(places[i], grads[i], load_sems.at[i]) for i in range(6)]
    for load in loads:
        load.start()
    layer.small[...] = jnp.zeros_like(layer.small)
    layer.inner_bias_grad[...] = jnp.zeros_like(layer.inner_bias_grad)
    for slot in range(layer.slots):
        def need(i):
            if slot == 0:
                loads[i].wait()
        base = slot * layer.keys
        layer.hid[base : base + layer.half] = layer.others[slot]
        layer.hid[base + layer.half : base + 2 * layer.half] = layer.tokens[slot]
        layer.set_memory(slot)
        need(0)
        layer.project_query(slot)
        need(1)
        layer.project_key(slot)
        need(2)
        layer.project_value(slot)
        layer.attend(slot)
        need(3)
        layer.branch(slot)
        need(4)
        fori(layer.hidden // layer.width, lambda j: layer.inner(slot, j))
        need(5)
        layer.outer(slot)
    layer.memory[...] = jnp.zeros_like(layer.memory)
    for slot in reversed(range(layer.slots)):
        layer.outer_back(slot)
        layer.inner_back(slot)
        if slot == 0:
            fori(layer.hidden // layer.width, layer.outer_weight_grad)
            stores[5].start()
            fori(layer.hidden // layer.width, layer.inner_weight_grad)
            stores[4].start()
        layer.mix_back(slot)
        layer.attend_back(slot)
        passed = layer.input_back(slot)
        if slot > 0:
            layer.swap_out[...] = passed
            pl.semaphore_wait(barrier, 1)
            swap = pltpu.make_async_remote_copy(
                src_ref=layer.swap_out,
                dst_ref=layer.swap_in,
                send_sem=pair_sems.at[0],
                recv_sem=pair_sems.at[1],
                device_id=(1 - seq, chain),
                device_id_type=MESH,
            )
            swap.start()
            swap.wait()
            summed = pltpu.roll(passed + layer.swap_in[...], MEM, 0)
            layer.memory[...] = jnp.where(seq == 0, summed, 0.0)
    layer.output_weight_grad()
    stores[3].start()
    layer.query_weight_grad()
    stores[0].start()
    layer.key_weight_grad()
    stores[1].start()
    layer.value_weight_grad()
    stores[2].start()
    for store in stores:
        store.wait()


def middle(start, mask, tokens, others, cotangent, vectors, inner_bias, weights):
    slots, half, width = tokens.shape
    hidden = inner_bias.shape[1]
    bf16, f32 = jnp.bfloat16, jnp.float32
    inside = pl.BlockSpec(memory_space=pltpu.VMEM)
    anywhere = pl.BlockSpec(memory_space=pl.ANY)
    shape = jax.ShapeDtypeStruct
    state = state_shapes(slots, half, width, hidden)
    return pl.pallas_call(
        middle_kernel,
        out_shape=[
            shape((slots, half, width), bf16),
            shape((slots, half, width), f32),
            shape((slots, half, width), bf16),
            shape((MEMORY, width), f32),
            shape((1, hidden), f32),
        ]
        + [shape(w.shape, bf16) for w in weights],
        in_specs=[pl.BlockSpec(memory_space=pltpu.SMEM)] + [inside] * 6 + [anywhere] * 6,
        out_specs=[inside] * 5 + [anywhere] * 6,
        scratch_shapes=[pltpu.VMEM(*s) for s in state]
        + [pltpu.SemaphoreType.DMA((6,)), pltpu.SemaphoreType.DMA((2,))],
        compiler_params=pltpu.CompilerParams(
            collective_id=2, has_side_effects=True, vmem_limit_bytes=62 * 2**20
        ),
        cost_estimate=pl.CostEstimate(flops=31 * 10**9, bytes_accessed=40 * 10**6, transcendentals=10**7),
    )(start, mask, tokens, others, cotangent, vectors, inner_bias, *weights)


class Links:
    def __init__(self, levels, refs):
        self.levels = levels
        self.seq, self.level, self.side, self.core = place()
        self.__dict__.update(refs)
        self.width = self.w_attention.shape[0]
        self.thick = self.width // (4 * levels)
        self.tall = self.w_outer.shape[0] // (8 * levels)

    def device(self, kind):
        seq, level, side, core = self.seq, self.level, self.side, self.core
        return device_of(
            *(
                (seq, level, side, 1 - core),
                (seq, level, 1 - side, core),
                (1 - seq, level, side, core),
                (seq, level + 1, side, core),
                (seq, level - 1, side, core),
            )[kind]
        )

    def chip(self, rel, at):
        seq = self.seq if rel < 2 else 1 - self.seq
        side = self.side if rel % 2 == 0 else 1 - self.side
        return seq * (2 * self.levels) + at * 2 + side

    def view(self, part, chip, core, small):
        if part < 4:
            whole = self.w_attention if part < 2 else self.w_inner
            column = pl.multiple_of(core * (2 * self.width) + (part % 2) * self.width, LANES)
            return whole.at[
                pl.ds(pl.multiple_of(chip * self.thick, 16), self.thick), pl.ds(column, self.width)
            ]
        if part < 6:
            size = self.tall // 2
            row = pl.multiple_of(chip * (2 * self.tall) + core * self.tall + (part - 4) * size, 16)
            return self.w_outer.at[pl.ds(row, size), :]
        return small.at[chip * 2 + core]

    def remote(self, source, target, send_sem, recv_sem, kind):
        return pltpu.make_async_remote_copy(
            src_ref=source,
            dst_ref=target,
            send_sem=send_sem,
            recv_sem=recv_sem,
            device_id=self.device(kind),
            device_id_type=MESH,
        )

    def amount(self, part, count):
        if part < 6:
            return self.w_outer.at[pl.ds(0, count * self.thick), :]
        return self.small_all.at[pl.ds(0, count)]

    def all_sent(self, part, count, semaphore):
        whole = self.amount(part, count)
        self.remote(whole, whole, semaphore, semaphore, 0).wait_send()

    def all_arrived(self, part, count, semaphore):
        whole = self.amount(part, count)
        self.remote(whole, whole, semaphore, semaphore, 0).wait_recv()

    def has_up(self):
        return self.level < self.levels - 1

    def has_down(self):
        return self.level > 0

    def neighbours(self):
        return 3 + self.has_up().astype(jnp.int32) + self.has_down().astype(jnp.int32)

    def tell_all(self, semaphore):
        for kind in range(3):
            pl.semaphore_signal(semaphore, inc=1, device_id=self.device(kind), device_id_type=MESH)

        @pl.when(self.has_up())
        def _():
            pl.semaphore_signal(semaphore, inc=1, device_id=self.device(3), device_id_type=MESH)

        @pl.when(self.has_down())
        def _():
            pl.semaphore_signal(semaphore, inc=1, device_id=self.device(4), device_id_type=MESH)


class Gather(Links):
    def copy(self, part, rel, at, kind):
        chip = self.chip(rel, at)
        here = self.view(part, chip, self.core, self.small_all)
        arrives = self.gather_recv.at[part, chip]
        if kind == 0:
            sends, arrives = self.core_send.at[part], self.core_recv.at[part]
        elif kind < 3:
            sends = self.plane_send.at[part, kind - 1]
        else:
            sends = self.line_send.at[part, 0 if rel == 0 else 1, at + (kind - 3)]
        return self.remote(here, here, sends, arrives, kind)

    def arrived(self, part, rel, at):
        self.copy(part, rel, at, 1).wait_recv()

    def up(self, part, rel, at):
        pl.when(self.has_up())(lambda: self.copy(part, rel, at, 3).start())

    def down(self, part, rel, at):
        pl.when(self.has_down())(lambda: self.copy(part, rel, at, 4).start())

    def own(self, part):
        self.up(part, 0, self.level)
        self.down(part, 0, self.level)
        for kind in (1, 2, 0):
            self.copy(part, 0, self.level, kind).start()

    def from_plane(self, part, at):
        self.arrived(part, 1, at)
        if LAST[part] == 2:
            self.copy(part, 1, at, 2).start()
        self.copy(part, 1, at, 0).start()
        self.arrived(part, 2, at)
        if LAST[part] == 1:
            self.copy(part, 2, at, 1).start()
        self.copy(part, 2, at, 0).start()

    def passed_on(self, part, rel, at):
        self.arrived(part, rel, at)
        self.copy(part, rel, at, 0).start()

    def around(self, distance, body):
        if not 0 <= distance < self.levels:
            return
        for sign in (-1, 1) if distance else (0,):
            at = self.level + sign * distance
            pl.when(jnp.logical_and(at >= 0, at < self.levels))(functools.partial(body, at, sign))

    def step(self, part, step):
        last = LAST[part]
        first = 3 - last

        def column(rel, kinds, at, sign):
            self.arrived(part, rel, at)
            if sign <= 0:
                self.up(part, rel, at)
            if sign >= 0:
                self.down(part, rel, at)
            for kind in kinds:
                self.copy(part, rel, at, kind).start()

        if part in STRAIGHT:
            if step:
                self.around(step, functools.partial(column, 0, (1, 2, 0)))
            self.around(step - 1, lambda at, sign: self.from_plane(part, at))
            self.around(step - 2, lambda at, sign: self.passed_on(part, 3, at))
            return
        self.around(step, functools.partial(column, 0, (last, 0)))
        self.around(step - 1, functools.partial(column, first, (last, 0)))
        self.around(step - 1, lambda at, sign: self.passed_on(part, last, at))
        self.around(step - 2, lambda at, sign: self.passed_on(part, 3, at))

    def other_core(self, part):
        self.all_arrived(part, 4 * self.levels, self.core_recv.at[part])

    def sent(self, part):
        self.all_sent(part, 4 * self.levels, self.core_send.at[part])
        straight = part in STRAIGHT
        for kind in (1, 2):
            count = self.levels if straight else 1
            if kind == LAST[part]:
                count = 2 * self.levels
            self.all_sent(part, count, self.plane_send.at[part, kind - 1])

        def body(at):
            for rel in (0,) if straight else (0, 3 - LAST[part]):
                pl.when(jnp.logical_and(at <= self.level, self.has_up()))(
                    lambda rel=rel: self.copy(part, rel, at, 3).wait_send()
                )
                pl.when(jnp.logical_and(at >= self.level, self.has_down()))(
                    lambda rel=rel: self.copy(part, rel, at, 4).wait_send()
                )

        fori(self.levels, body)


class Scatter(Links):
    def land(self, kind, part, slot):
        if part >= 2:
            return self.lands[part - 2][kind].at[slot]
        levels = self.levels
        at = slot + (0, 4 * levels, 6 * levels, 7 * levels)[kind]
        hold = self.active if part == 0 else self.slope
        per_row = hold.shape[1] // self.width
        row = pl.multiple_of((at // per_row) * self.thick, 16)
        column = pl.multiple_of(lax.rem(at, per_row) * self.width, LANES)
        return hold.at[pl.ds(row, self.thick), pl.ds(column, self.width)]

    def mine(self, part, rel, at, core=None):
        return self.view(part, self.chip(rel, at), self.core if core is None else core, self.small_grad)

    def over_core(self, part, at, rel):
        return self.remote(
            self.mine(part, rel, at, 1 - self.core),
            self.land(0, part, at * 4 + rel),
            self.sum_core_send.at[part],
            self.sum_core_recv.at[part],
            0,
        )

    def over_first(self, part, at, second):
        first = CROSS[part]
        slot = at + second * self.levels
        return self.remote(
            self.land(0, part, at * 4 + (3 if second else first)),
            self.land(1, part, slot),
            self.sum_plane_send.at[part, 0],
            self.sum_plane_recv.at[part, slot],
            first,
        )

    def over_last(self, part, at=None):
        last = 3 - CROSS[part]
        straight = part in SUM_STRAIGHT
        slot = at if straight else 0
        return self.remote(
            self.land(0, part, (at if straight else self.level) * 4 + last),
            self.land(2, part, slot),
            self.sum_plane_send.at[part, 1],
            self.sum_plane_recv.at[part, 2 * self.levels + slot],
            last,
        )

    def plane(self, part):
        if part not in SUM_STRAIGHT:
            return
        rel = 3 - CROSS[part]

        def body(i):
            at = lax.rem(self.level + 1 + i, self.levels)
            self.over_first(part, at, 1).wait_recv()
            self.keep(part, at, rel, self.total(part, at, rel, self.land(1, part, at + self.levels)))
            self.over_last(part, at).start()

        fori(self.levels, body)

    def along(self, part, target, second, kind):
        slot = target + 1 if kind == 3 else target
        rel = 3 - CROSS[part] if second else 0
        return self.remote(
            self.land(0, part, target * 4 + rel),
            self.land(3, part, slot + second * (self.levels + 1)),
            self.sum_line_send.at[part, second, target],
            self.sum_line_recv.at[part, second, slot],
            kind,
        )

    def total(self, part, at, rel, *more):
        value = self.mine(part, rel, at)[...].astype(jnp.float32)
        value = value + self.land(0, part, at * 4 + rel)[...].astype(jnp.float32)
        for ref in more:
            value = value + ref[...].astype(jnp.float32)
        return value

    def keep(self, part, at, rel, value):
        self.land(0, part, at * 4 + rel)[...] = value.astype(jnp.bfloat16)

    def start_core(self, part):
        for rel in (3, CROSS[part], 3 - CROSS[part], 0):
            fori(self.levels, lambda at: self.over_core(part, at, rel).start())

    def cross(self, part):
        self.all_arrived(part, 4 * self.levels, self.sum_core_recv.at[part])

        def body(i):
            at = lax.rem(self.level + 1 + i, self.levels)
            for second in (1, 0):
                rel = 3 if second else CROSS[part]
                self.keep(part, at, rel, self.total(part, at, rel))
                self.over_first(part, at, second).start()

        fori(self.levels, body)

    def column(self, part, at, second, *more):
        rel = 3 - CROSS[part] if second else 0
        if part in SUM_STRAIGHT:
            more += (self.land(2, part, at),)
        return self.total(part, at, rel, self.land(1, part, at + second * self.levels), *more)

    def ready(self, part, at, second):
        self.over_first(part, at, second).wait_recv()
        if part in SUM_STRAIGHT:
            self.over_last(part, at).wait_recv()

    def columns(self, part):
        return (0,) if part in SUM_STRAIGHT else (0, 1)

    def line(self, part, step):
        last = self.levels - 1
        level = self.level

        def go(target, kind, first):
            for second in self.columns(part):
                rel = 3 - CROSS[part] if second else 0
                self.ready(part, target, second)

                @pl.when(first)
                def _():
                    self.keep(part, target, rel, self.column(part, target, second))

                @pl.when(jnp.logical_not(first))
                def _():
                    self.along(part, target, second, kind).wait_recv()
                    slot = (target + 1 if kind == 3 else target) + second * (self.levels + 1)
                    self.keep(part, target, rel, self.column(part, target, second, self.land(3, part, slot)))

                self.along(part, target, second, kind).start()

        pl.when(jnp.logical_and(step >= level, self.has_up()))(lambda: go(last - step + level, 3, level == 0))
        pl.when(jnp.logical_and(step >= last - level, self.has_down()))(
            lambda: go(level - last + step, 4, level == last)
        )

    def ends(self, part, second, out):
        level = self.level
        base = second * (self.levels + 1)
        self.ready(part, level, second)
        pl.when(self.has_down())(lambda: self.along(part, level, second, 3).wait_recv())
        pl.when(self.has_up())(lambda: self.along(part, level, second, 4).wait_recv())
        below = self.land(3, part, base + level + 1)
        above = self.land(3, part, base + level)
        inner = jnp.logical_and(self.has_down(), self.has_up())
        pl.when(inner)(lambda: out(self.column(part, level, second, below, above)))
        pl.when(jnp.logical_not(self.has_up()))(lambda: out(self.column(part, level, second, below)))
        pl.when(jnp.logical_not(self.has_down()))(lambda: out(self.column(part, level, second, above)))

    def settle(self, part):
        if part in SUM_STRAIGHT:
            return
        rel = 3 - CROSS[part]
        self.ends(part, 1, lambda value: self.keep(part, self.level, rel, value))
        self.over_last(part).start()

    def last(self, part, out):
        def put(value):
            out[...] = value

        self.ends(part, 0, put)
        if part in SUM_STRAIGHT:
            return
        self.over_last(part).wait_recv()
        out[...] += self.land(2, part, 0)[...].astype(jnp.float32)

    def sent(self, part):
        self.all_sent(part, 4 * self.levels, self.sum_core_send.at[part])
        self.all_sent(part, 2 * self.levels, self.sum_plane_send.at[part, 0])
        self.all_sent(part, self.levels if part in SUM_STRAIGHT else 1, self.sum_plane_send.at[part, 1])

        def body(at):
            for second in self.columns(part):
                pl.when(at > self.level)(lambda: self.along(part, at, second, 3).wait_send())
                pl.when(at < self.level)(lambda: self.along(part, at, second, 4).wait_send())

        fori(self.levels, body)


STRAIGHT = (4, 5)
SUM_STRAIGHT = (0, 1)
CROSS = (1, 2, 1, 2, 1, 2, 1)
PARTS = 7
LEVELS = 4
LAGS = (0, 0, 0)

LAST = (1, 2, 1, 2, 1, 2, 1)


class Given(NamedTuple):
    start: Any
    length: Any
    tokens: Any
    cot_in: Any
    query_in: Any
    key_in: Any
    value_in: Any
    output_in: Any
    inner_in: Any
    outer_in: Any
    query_bias: Any
    value_bias: Any
    output_bias: Any
    first_gain: Any
    first_shift: Any
    outer_bias: Any
    second_gain: Any
    second_shift: Any
    inner_bias_in: Any
    read_in: Any
    write_in: Any


class Made(NamedTuple):
    layer_out: Any
    input_out: Any
    narrow_out: Any
    outer_out: Any
    small_out: Any
    spill: Any


class Room(NamedTuple):
    cot: Any
    mask: Any
    vectors: Any
    inner_bias: Any
    small: Any
    inner_bias_grad: Any
    pair_in: Any
    narrow: Any
    narrow_in: Any
    small_all: Any
    small_rows: Any


class Signals(NamedTuple):
    core_send: Any
    core_recv: Any
    plane_send: Any
    line_send: Any
    gather_recv: Any
    sum_core_send: Any
    sum_core_recv: Any
    sum_plane_send: Any
    sum_plane_recv: Any
    sum_line_send: Any
    sum_line_recv: Any
    trade_sems: Any
    pair_sems: Any
    result_sems: Any
    local_sems: Any
    free_sem: Any


def spread(ref_rows, per, count):
    tiles = [None] * (per * count // LANES)
    lane = lax.broadcasted_iota(jnp.int32, (1, LANES), 1)
    for w in range(count):
        block = jnp.where(lane < per, ref_rows(w), 0.0)
        tile, shift = divmod(per * w, LANES)
        moved = pltpu.roll(block, shift, 1) if shift else block
        pieces = [(tile, jnp.where(lane >= shift, moved, 0.0) if shift else moved)]
        if shift + per > LANES:
            pieces.append((tile + 1, jnp.where(lane < shift + per - LANES, moved, 0.0)))
        for tile, piece in pieces:
            tiles[tile] = piece if tiles[tile] is None else tiles[tile] + piece
    return tiles


def picked(tile_of, per, w):
    lane = lax.broadcasted_iota(jnp.int32, (1, LANES), 1)
    tile, shift = divmod(per * w, LANES)
    block = tile_of(tile)
    if shift:
        block = pltpu.roll(block, LANES - shift, 1)
        if shift + per > LANES:
            block = jnp.where(lane < LANES - shift, block, pltpu.roll(tile_of(tile + 1), LANES - shift, 1))
    return jnp.where(lane < per, block, 0.0)


def whole_kernel(levels, *refs):
    left = list(refs)
    refs = {}
    for kind in (Given, Made, State, Room, Signals):
        refs.update(take(left, kind))
    refs.update(lands=[left[4 * i : 4 * i + 4] for i in range(PARTS - 2)])
    refs.update(own_out=refs.get(Made._fields[1]), small_grad=refs.get(Room._fields[9]), pair_out=None)
    gather = Gather(levels, refs)
    scatter = Scatter(levels, refs)
    layer = Layer(gather.seq, refs)
    seq, level, side, core = gather.seq, gather.level, gather.side, gather.core
    width, half, keys, rows = layer.width, layer.half, layer.keys, layer.rows
    narrow = layer.narrow.shape[0]
    blocks = 8 * levels
    chip = gather.chip(0, level)
    tiles = layer.hidden // width
    barrier = pltpu.get_barrier_semaphore()
    gather.tell_all(barrier)

    for i, piece in enumerate((layer.query_in, layer.key_in, layer.value_in, layer.output_in)):
        layer.narrow[:, i * width : (i + 1) * width] = piece[...]
    layer.narrow[:, 4 * width :] = layer.inner_in[...]
    own_width = layer.query_bias.shape[1]
    layer.small_rows[...] = jnp.zeros_like(layer.small_rows)
    layer.small_rows[0:MEM, 0:own_width] = layer.read_in[...].astype(jnp.float32)
    layer.small_rows[MEM:LINE, 0:own_width] = layer.write_in[...].astype(jnp.float32)
    for i, piece in enumerate(
        (
            layer.query_bias,
            layer.value_bias,
            layer.output_bias,
            layer.first_gain,
            layer.first_shift,
            layer.outer_bias,
            layer.second_gain,
            layer.second_shift,
        )
    ):
        layer.small_rows[LINE + i : LINE + i + 1, 0:own_width] = piece[...].astype(jnp.float32)
    layer.small_rows[28:29, 0 : layer.inner_bias_in.shape[1]] = layer.inner_bias_in[...].astype(jnp.float32)
    layer.small_all[chip * 2 + core] = layer.small_rows[...].astype(jnp.bfloat16)
    own_outer = pltpu.make_async_copy(
        layer.outer_in,
        layer.w_outer.at[pl.ds(pl.multiple_of((chip * 2 + core) * gather.tall, 16), gather.tall), :],
        layer.local_sems.at[0],
    )
    own_outer.start()
    own_tokens = [
        pltpu.make_async_copy(
            layer.tokens.at[slot], layer.hid.at[pl.ds(slot * keys + half, half)], layer.local_sems.at[1 + slot]
        )
        for slot in range(layer.slots)
    ]
    cots = [
        pltpu.make_async_copy(layer.cot_in.at[slot], layer.cot.at[0], layer.local_sems.at[5 + slot])
        for slot in range(layer.slots)
    ]
    for copy in own_tokens:
        copy.start()
    cots[1].start()
    share_tokens = [
        gather.remote(
            layer.tokens.at[slot],
            layer.hid.at[pl.ds(slot * keys, half)],
            layer.pair_sems.at[0, slot],
            layer.pair_sems.at[1, slot],
            2,
        )
        for slot in range(layer.slots)
    ]
    pl.semaphore_wait(barrier, gather.neighbours())
    trade = [
        gather.remote(
            layer.narrow.at[:, pl.ds(pl.multiple_of((2 * i + 1 - core) * (2 * width), LANES), 2 * width)],
            layer.narrow_in.at[i],
            layer.trade_sems.at[0, i],
            layer.trade_sems.at[1, i],
            0,
        )
        for i in range(2)
    ]
    for copy in trade:
        copy.start()
    gather.own(6)
    own_outer.wait()
    first = core == 0
    for i, whole in enumerate((layer.w_attention, layer.w_inner)):
        trade[i].wait_recv()
        column = pl.multiple_of(core * (2 * width), LANES)
        mine = layer.narrow[:, pl.ds(pl.multiple_of((2 * i + core) * (2 * width), LANES), 2 * width)].astype(jnp.float32)
        other = layer.narrow_in[i].astype(jnp.float32)
        merged = jnp.concatenate([jnp.where(first, mine, other), jnp.where(first, other, mine)], axis=0)
        whole[pl.ds(pl.multiple_of(chip * gather.thick, 16), gather.thick), pl.ds(column, 2 * width)] = merged.astype(
            jnp.bfloat16
        )
        gather.own(2 * i)
        gather.own(2 * i + 1)
        if i == 0:
            share_tokens[0].start()
    gather.own(4)
    gather.own(5)
    for step in range(1, levels + 2):
        gather.step(6, step)

    def turn(number):
        for group in range(3):
            for part in (2 * group, 2 * group + 1):
                if 1 <= number - LAGS[group] <= levels + 1:
                    gather.step(part, number - LAGS[group])

    def have(*parts):
        for part in parts:
            gather.other_core(part)

    layer.small[...] = jnp.zeros_like(layer.small)
    layer.inner_bias_grad[...] = jnp.zeros_like(layer.inner_bias_grad)
    spot = lax.broadcasted_iota(jnp.int32, (1, keys), 1)
    position = jnp.where(
        spot < half,
        spot + (1 - seq) * half,
        jnp.where(spot < 2 * half, spot + (seq - 1) * half, jnp.where(spot < 2 * half + LINE, -1, 1 << 30)),
    )
    for slot in range(layer.slots):
        layer.mask[slot] = jnp.where(position < layer.length[slot], 0.0, NEG_FILL)

    have(6)
    vectors = spread(lambda w: layer.small_all[w].astype(jnp.float32), width // blocks, blocks)
    for i, tile in enumerate(vectors):
        layer.vectors[:, i * LANES : (i + 1) * LANES] = tile
    biases = spread(
        lambda w: layer.small_all[w].astype(jnp.float32)[28:29, :], layer.hidden // blocks, blocks
    )
    for i, tile in enumerate(biases):
        layer.inner_bias[:, i * LANES : (i + 1) * LANES] = tile
    layer.set_memory(0)

    spill = [
        pltpu.make_async_copy(layer.shares, layer.spill, layer.local_sems.at[3]),
        pltpu.make_async_copy(layer.spill, layer.shares, layer.local_sems.at[4]),
    ]

    def project():
        have(0, 1)
        own_tokens[0].wait()
        share_tokens[0].wait()
        layer.project_query(0)
        layer.project_key(0)
        layer.project_value(0)

    def attend(*pairs):
        return lambda: layer.attend(0, pairs)

    work = [
        project,
        attend(0, 1, 2),
        attend(3, 4, 5),
        lambda: (spill[0].start(), layer.branch(0)),
    ]
    for number in range(1, levels + 2 + max(LAGS)):
        turn(number)
        if number > levels:
            work.pop(0)()
    share_tokens[1].start()
    for item in work:
        item()
    have(2, 3)
    fori(tiles, lambda j: layer.inner(0, j))
    have(4, 5)
    layer.outer(0)

    layer.set_memory(1)
    own_tokens[1].wait()
    share_tokens[1].wait()
    layer.project_query(1)
    layer.project_key(1)
    layer.project_value(1)
    spill[0].wait()
    layer.attend(1)
    layer.branch(1)
    fori(tiles, lambda j: layer.inner(1, j))
    layer.outer(1)
    for part in range(PARTS):
        gather.sent(part)
    for copy in trade:
        copy.wait_send()
    layer.memory[...] = jnp.zeros_like(layer.memory)

    def pair_copy(slot):
        return gather.remote(
            layer.pair_room(slot),
            layer.pair_in.at[slot],
            layer.pair_sems.at[2, slot],
            layer.pair_sems.at[3, slot],
            2,
        )

    cots[1].wait()
    layer.outer_back(1)
    cots[0].start()
    layer.inner_back(1)
    layer.mix_back(1)
    layer.attend_back(1)
    spill[1].start()
    passed = layer.input_back(1)
    layer.swap_out[...] = passed
    swap = gather.remote(layer.swap_out, layer.swap_in, layer.pair_sems.at[4, 0], layer.pair_sems.at[4, 1], 2)
    swap.start()
    swap.wait()
    pair_copy(1).start()
    summed = pltpu.roll(passed + layer.swap_in[...], MEM, 0)
    layer.memory[...] = jnp.where(seq == 0, summed, 0.0)
    cots[0].wait()
    layer.outer_back(0)

    def narrow_result(part):
        scatter.last(part, layer.work.at[pl.ds(part * 2 * narrow, 2 * narrow), :])
        column = pl.ds(pl.multiple_of((part // 2) * (4 * width) + core * (2 * width) + (part % 2) * width, LANES), width)
        layer.narrow_out[:, column] = layer.work[pl.ds(pl.multiple_of((2 * part + core) * narrow, 8), narrow), :]
        share_result(part).start()

    def share_result(part):
        column = pl.ds(pl.multiple_of((part // 2) * (4 * width) + core * (2 * width) + (part % 2) * width, LANES), width)
        return gather.remote(
            layer.work.at[pl.ds(pl.multiple_of((2 * part + 1 - core) * narrow, 8), narrow), :],
            layer.narrow_out.at[:, column],
            layer.result_sems.at[0, part],
            layer.result_sems.at[1, part],
            0,
        )

    def share_result_in(part):
        column = pl.ds(
            pl.multiple_of((part // 2) * (4 * width) + (1 - core) * (2 * width) + (part % 2) * width, LANES), width
        )
        return gather.remote(
            layer.work.at[pl.ds(pl.multiple_of((2 * part + 1 - core) * narrow, 8), narrow), :],
            layer.narrow_out.at[:, column],
            layer.result_sems.at[0, part],
            layer.result_sems.at[1, part],
            0,
        )

    def outer_result(part):
        size = gather.tall // 2
        scatter.last(part, layer.outer_out.at[pl.ds((part - 4) * size, size), :])

    def both(function, *parts, **more):
        for part in parts:
            function(part, **more)

    def give_input(slot):
        pair_copy(slot).wait()
        total = layer.input_out[slot].astype(jnp.float32) + layer.pair_in[slot].astype(jnp.float32)
        layer.input_out[slot] = total.astype(jnp.bfloat16)

    fori(tiles, layer.outer_weight_grad)
    both(scatter.start_core, 4, 5)
    layer.inner_back(0)
    both(scatter.cross, 4, 5)
    fori(tiles, layer.inner_weight_grad)
    scatter.tell_all(layer.free_sem)
    both(scatter.start_core, 2, 3)
    scatter.line(4, 0)
    layer.mix_back(0)
    spill[1].wait()
    layer.attend_back(0, (0, 1))
    scatter.cross(2)
    scatter.line(5, 0)
    scatter.line(4, 1)
    layer.attend_back(0, (2, 3))
    scatter.cross(3)
    scatter.line(5, 1)
    layer.attend_back(0, (4, 5))
    scatter.line(2, 0)
    scatter.line(4, 2)
    layer.input_back(0)
    pair_copy(0).start()
    layer.value_weight_grad()
    layer.query_weight_grad()
    pl.semaphore_wait(layer.free_sem, scatter.neighbours())
    scatter.start_core(0)
    scatter.line(3, 0)
    scatter.line(5, 2)
    layer.output_weight_grad()
    scatter.cross(0)
    layer.key_weight_grad()
    scatter.start_core(1)
    scatter.line(2, 1)
    scatter.line(3, 1)
    small_tile = lambda i: layer.small[:, i * LANES : (i + 1) * LANES]
    inner_tile = lambda i: layer.inner_bias_grad[:, i * LANES : (i + 1) * LANES]
    small_row = lax.broadcasted_iota(jnp.int32, (32, 1), 0)
    for w in range(blocks):
        vectors_part = picked(small_tile, width // blocks, w)
        bias_part = picked(inner_tile, layer.hidden // blocks, w)
        layer.small_grad[w] = jnp.where(small_row == 28, bias_part, vectors_part).astype(jnp.bfloat16)
    scatter.start_core(6)
    scatter.cross(1)
    scatter.cross(6)
    scatter.settle(4)
    scatter.line(2, 2)
    scatter.plane(0)
    scatter.line(3, 2)
    scatter.line(0, 0)
    outer_result(4)
    scatter.settle(5)
    scatter.plane(1)
    scatter.line(0, 1)
    scatter.line(1, 0)
    scatter.line(6, 0)
    outer_result(5)
    scatter.settle(2)
    for step in range(2, levels - 1):
        scatter.line(0, step)
        scatter.line(1, step - 1)
        scatter.line(6, step - 1)
    scatter.settle(3)
    narrow_result(2)
    scatter.line(1, levels - 2)
    scatter.line(6, levels - 2)
    narrow_result(3)
    give_input(1)
    give_input(0)
    narrow_result(0)
    scatter.settle(6)
    narrow_result(1)
    scatter.last(6, layer.small_out)
    for part in range(4):
        share_result_in(part).wait_recv()
        share_result(part).wait_send()
    for part in range(PARTS):
        scatter.sent(part)


def whole_layer(levels, start, length, tokens, cotangent, weights, vectors, inner_bias, read_init, write_init):
    slots, half, width = tokens.shape
    query_in, outer_in, inner_in = weights[0], weights[5], weights[4]
    hidden = inner_in.shape[1]
    narrow, tall = query_in.shape[0], outer_in.shape[0]
    blocks = 8 * levels
    bf16, f32 = jnp.bfloat16, jnp.float32
    inside = pl.BlockSpec(memory_space=pltpu.VMEM)
    scalars = pl.BlockSpec(memory_space=pltpu.SMEM)
    anywhere = pl.BlockSpec(memory_space=pl.ANY)
    shape = jax.ShapeDtypeStruct
    dma = pltpu.SemaphoreType.DMA
    state = state_shapes(slots, half, width, hidden)
    shares = (width // LANES,) + state.shares[0][1:]
    state = state._replace(shares=(shares, bf16))
    room = Room(
        cot=((1, half, width), bf16),
        mask=((slots, 1, 2 * half + MEMORY), f32),
        vectors=((32, width), f32),
        inner_bias=((1, hidden), f32),
        small=((32, width), f32),
        inner_bias_grad=((1, hidden), f32),
        pair_in=((slots, half, width), bf16),
        narrow=((narrow, 8 * width), bf16),
        narrow_in=((2, narrow, 2 * width), bf16),
        small_all=((blocks, 32, LANES), bf16),
        small_rows=((32, LANES), f32),
    )
    signals = Signals(
        core_send=dma((PARTS,)),
        core_recv=dma((PARTS,)),
        plane_send=dma((PARTS, 2)),
        line_send=dma((PARTS, 2, levels + 1)),
        gather_recv=dma((PARTS, 4 * levels)),
        sum_core_send=dma((PARTS,)),
        sum_core_recv=dma((PARTS,)),
        sum_plane_send=dma((PARTS, 2)),
        sum_plane_recv=dma((PARTS, 3 * levels)),
        sum_line_send=dma((PARTS, 2, levels)),
        sum_line_recv=dma((PARTS, 2, levels + 1)),
        trade_sems=dma((2, 2)),
        pair_sems=dma((5, 2)),
        result_sems=dma((2, 4)),
        local_sems=dma((7,)),
        free_sem=pltpu.SemaphoreType.REGULAR,
    )
    lands = []
    for part in range(2, PARTS):
        size = (2 * narrow, width) if part < 4 else (tall // 2, width) if part < 6 else (32, LANES)
        late = (levels, levels + 1) if part in SUM_STRAIGHT else (1, 2 * levels + 2)
        lands += [pltpu.VMEM((count,) + size, bf16) for count in (4 * levels, 2 * levels) + late]
    return pl.pallas_call(
        functools.partial(whole_kernel, levels),
        out_shape=[
            shape((slots, half, width), bf16),
            shape((slots, half, width), bf16),
            shape((narrow, 8 * width), f32),
            shape((tall, width), f32),
            shape((32, LANES), f32),
            shape(shares, bf16),
        ],
        in_specs=[scalars] * 2 + [anywhere] * 2 + [inside] * 5 + [anywhere] + [inside] * 11,
        out_specs=[inside] * 5 + [anywhere],
        scratch_shapes=[pltpu.VMEM(*s) for s in state + room] + list(signals) + lands,
        compiler_params=pltpu.CompilerParams(
            collective_id=0, has_side_effects=True, vmem_limit_bytes=63 * 2**20
        ),
        cost_estimate=pl.CostEstimate(flops=31 * 10**9, bytes_accessed=10 * 10**6, transcendentals=10**7),
        name="whole_layer",
    )(start, length, tokens, cotangent, *weights, *(v[None] for v in vectors), inner_bias[None], read_init, write_init)


def hand_out_kernel(layer_ref, input_ref, narrow_ref, outer_ref, small_ref, *out_refs):
    width = outer_ref.shape[1]
    out_refs[0][...] = layer_ref[...]
    out_refs[1][...] = input_ref[...]
    for i in range(4):
        out_refs[2 + i][...] = narrow_ref[:, i * width : (i + 1) * width]
    out_refs[6][...] = narrow_ref[:, 4 * width :]
    out_refs[7][...] = outer_ref[...]
    for i in range(8):
        out_refs[8 + i][...] = small_ref[LINE + i : LINE + i + 1, 0 : out_refs[8 + i].shape[1]]
    out_refs[16][...] = small_ref[28:29, 0 : out_refs[16].shape[1]]
    out_refs[17][...] = small_ref[0:MEM, 0 : out_refs[17].shape[1]]
    out_refs[18][...] = small_ref[MEM:LINE, 0 : out_refs[18].shape[1]]


def hand_out(results, narrow, inner_width):
    layer_out, input_out, narrow_out, outer_out, small_out = results
    width = outer_out.shape[1]
    shape = jax.ShapeDtypeStruct
    f32 = jnp.float32
    inside = pl.BlockSpec(memory_space=pltpu.VMEM)
    return pl.pallas_call(
        hand_out_kernel,
        out_shape=[shape(layer_out.shape, layer_out.dtype), shape(input_out.shape, input_out.dtype)]
        + [shape((narrow, width), f32)] * 4
        + [shape((narrow, narrow_out.shape[1] - 4 * width), f32), shape(outer_out.shape, f32)]
        + [shape((1, narrow), f32)] * 8
        + [shape((1, inner_width), f32)]
        + [shape((MEM, narrow), f32)] * 2,
        in_specs=[inside] * 5,
        out_specs=[inside] * 19,
        compiler_params=pltpu.CompilerParams(vmem_limit_bytes=62 * 2**20),
    )(layer_out, input_out, narrow_out, outer_out, small_out)


def small_block(vectors, inner_bias, read_init, write_init):
    width = vectors[0].shape[0]
    inner_width = inner_bias.shape[0]
    rows = jnp.concatenate([read_init, write_init] + [v[None] for v in vectors], axis=0)
    rows = jnp.pad(rows, ((0, 4), (0, 128 - width)))
    return rows + jnp.pad(inner_bias[None], ((28, 3), (0, 128 - inner_width)))


def apart(tokens, cotangent, start, length, weights, small, blocks):
    half, model_width = tokens.shape[1:]
    width, inner_width = weights[0].shape[0], weights[5].shape[0]
    axes = AXES
    pair = [(0, 1), (1, 0)]
    others = lax.ppermute(tokens, AXES[0], pair)
    whole = [lax.all_gather(w, axes, axis=0, tiled=True) for w in weights]
    small_all = lax.all_gather(small, axes, axis=0)
    vectors = small_all[:, :, :width].transpose(1, 0, 2).reshape(32, model_width).astype(jnp.float32)
    bias_inner = small_all[:, 28, :inner_width].reshape(1, -1).astype(jnp.float32)
    mine = lax.axis_index(AXES[0])
    place_in = jnp.arange(half)
    position = jnp.concatenate(
        [
            (1 - mine) * half + place_in,
            mine * half + place_in,
            jnp.where(jnp.arange(MEMORY) < LINE, -1, 1 << 30),
        ]
    )
    mask = jnp.where(position[None, :] < length[:, None], 0.0, NEG_FILL)[:, None, :]
    results = middle(start, mask, tokens, others, cotangent, vectors, bias_inner, whole)
    received = lax.ppermute(results[2], AXES[0], pair)
    input_grad = (results[1] + received.astype(jnp.float32)).astype(jnp.bfloat16)
    small_grads = jnp.pad(
        results[3].reshape(32, blocks, width).transpose(1, 0, 2), ((0, 0), (0, 0), (0, 128 - width))
    )
    inner_rows = jnp.pad(results[4].reshape(blocks, 1, inner_width), ((0, 0), (28, 3), (0, 128 - inner_width)))
    small_grads = jnp.where(jnp.arange(32)[None, :, None] == 28, inner_rows, small_grads).astype(jnp.bfloat16)

    def summed(grad):
        paired = lax.psum_scatter(grad, AXES[0], scatter_dimension=0, tiled=True).astype(jnp.float32)
        return lax.psum_scatter(paired, AXES[1], scatter_dimension=0, tiled=True)

    small_sum = summed(small_grads.reshape(-1, 128))
    return results[0], input_grad, [summed(g) for g in results[5:]], small_sum


def shards(
    tokens,
    cotangent,
    chain_start,
    seg_len,
    query_weight,
    key_weight,
    value_weight,
    output_weight,
    query_bias,
    value_bias,
    output_bias,
    first_gain,
    first_shift,
    inner_weight,
    inner_bias,
    outer_weight,
    outer_bias,
    second_gain,
    second_shift,
    read_init,
    write_init,
):
    width = query_bias.shape[0]
    levels = lax.axis_size(AXES[1]) // 4
    blocks = 8 * levels
    weights = (query_weight, key_weight, value_weight, output_weight, inner_weight, outer_weight)
    vectors = (
        query_bias,
        value_bias,
        output_bias,
        first_gain,
        first_shift,
        outer_bias,
        second_gain,
        second_shift,
    )
    inner_width = inner_bias.shape[0]
    if width % 8 == 0 and levels == LEVELS:
        results = whole_layer(
            levels,
            chain_start[0],
            seg_len[0],
            tokens[0],
            cotangent[0],
            weights,
            vectors,
            inner_bias,
            read_init,
            write_init,
        )
        results = hand_out(results[:5], width, inner_width)
        layer_out, input_grad = results[:2]
        sums = results[2:8]
        vector = [v[0] for v in results[8:16]]
        inner_sum, read_sum, write_sum = results[16][0], results[17], results[18]
    else:
        small = small_block(vectors, inner_bias, read_init, write_init)
        layer_out, input_grad, sums, small_sum = apart(
            tokens[0], cotangent[0], chain_start[0], seg_len[0], weights, small, blocks
        )
        vector = [small_sum[LINE + i, :width] for i in range(8)]
        inner_sum = small_sum[28, :inner_width]
        read_sum, write_sum = small_sum[:MEM, :width], small_sum[MEM:LINE, :width]
    return (
        layer_out[None],
        input_grad[None],
        *sums[:4],
        *vector[:5],
        sums[4],
        inner_sum,
        sums[5],
        *vector[5:],
        read_sum,
        write_sum,
    )


def solution(mesh):
    rows = P(AXES[1], None, AXES[0], None)
    scalars = P(AXES[1], None)
    matrix, vector, memory = P(AXES, None), P(AXES), P(None, AXES)
    weights = (
        (matrix,) * 4
        + (vector,) * 5
        + (matrix, vector, matrix)
        + (vector,) * 3
        + (memory,) * 2
    )
    return jax.shard_map(
        shards,
        mesh=mesh,
        in_specs=(rows, rows, scalars, scalars) + weights,
        out_specs=(rows, rows) + weights,
        check_vma=False,
    )
```
